32 devices in a mesh: dp: 4 (over x, core), fsdp: 8 (over z, y).
Axes of the slice: x: 2, y: 2, z: 4, core: 2. Of those that a mesh axis runs over, the one named last changes fastest.
Arguments:
- queries: bfloat16 [8, 256, 4096], P('fsdp', 'dp'), may hold values from -0.21875 to 0.21875
- candidates: bfloat16 [8, 4, 80, 4096], P('fsdp', 'dp'), may hold values from -0.21875 to 0.21875
- positives: int32 [8, 256], P('fsdp', 'dp'), may hold values from 0 to 255, as said below
- hard_blocks: int32 [8, 256], P('fsdp', 'dp'), may hold values from 0 to 3, as said below
- query_hidden: bfloat16 [8, 256, 4096], P('fsdp', 'dp'), may hold values from -6 to 6
- candidate_hidden: bfloat16 [8, 4, 80, 4096], P('fsdp', 'dp'), may hold values from -6 to 6
- adapter_down: bfloat16 [16, 4096], P(None, 'fsdp'), may hold values from -0.09375 to 0.09375
- adapter_up: bfloat16 [16, 4096], P(None, 'fsdp'), may hold values from -0.0234375 to 0.0234375
Outputs:
- question_derivative_vectors: bfloat16 [8, 256, 4096], P('fsdp', 'dp')
- candidate_grad_rows: bfloat16 [8, 4, 80, 4096], P('fsdp', 'dp')
- down_gradient: float32 [16, 4096], P(None, 'fsdp')
- up_gradient: float32 [16, 4096], P(None, 'fsdp')
The draws below stay inside these ranges and needn't reach their ends.
Inputs may be any that keep to these rules, and one draw needn't show every extreme that they name: Within each group the positives are a permutation of the 256 passages. `hard_blocks`: within each group every block is named by some query.
All inputs are finite; a program needn't handle non-finite values.
Results may differ from the reference program's by a relative error of at most 0.012.
Values may be sent and summed in bfloat16 or wider, within the bound.
No kernel may reach another device: no remote copies, remote signals or barrier semaphores. Data moves between devices by JAX's collectives and lax.ppermute only.
A program may use at most 64 MiB of HBM per device.

```python
import math
import jax
import jax.numpy as jnp
from jax import lax

D = 4096
R = 16
ROWS = 64
HARD = 16
BLK = 80
PAIRS = 256
GROUPS = 8
N_DP = 4


def shuffled(key):
    return jax.random.permutation(key, PAIRS).astype(jnp.int32)


def placed(owned, index):
    return jnp.zeros_like(owned).at[index].set(owned)


def picked(values, index):
    return values[index]


def common_layout(key):
    subkeys = jax.random.split(key, 8)
    positives = jax.vmap(shuffled)(jax.random.split(subkeys[0], GROUPS))
    hard_ids = jax.random.randint(subkeys[1], (GROUPS, PAIRS), 0, N_DP, dtype=jnp.int32)
    chosen = jax.vmap(shuffled)(jax.random.split(subkeys[2], GROUPS))[:, :N_DP]
    every_block = jnp.broadcast_to(jnp.arange(N_DP, dtype=jnp.int32)[None, :], (GROUPS, N_DP))
    hard_ids = hard_ids.at[jnp.arange(GROUPS, dtype=jnp.int32)[:, None], chosen].set(every_block)
    block_uniform = jax.random.uniform(subkeys[3], (GROUPS, N_DP, D), jnp.float32, 0.0, 1.0)
    row_uniform = jax.random.uniform(subkeys[4], (GROUPS, PAIRS, D), jnp.float32, 0.0, 1.0)
    alignment = jax.random.uniform(subkeys[5], (GROUPS, PAIRS, 1), jnp.float32, 0.55, 0.8)
    offset = jax.random.uniform(subkeys[6], (GROUPS, PAIRS, 1), jnp.float32, 0.5, 2.5)
    levels = jax.random.uniform(subkeys[7], (GROUPS, PAIRS, 1), jnp.float32, 0.0, 1.0)
    return (positives, hard_ids, block_uniform, row_uniform, alignment, offset, levels)


def bell_values(uniform_values):
    inner = jnp.clip(uniform_values, 1e-06, 1.0 - 1e-06)
    logistic = jnp.log(inner) - jnp.log(1.0 - inner)
    return jnp.clip(logistic * 0.5513289, -4.0, 4.0) * D ** (-0.5)


def directions(block_values, row_values, hard_ids):
    owner_rows = jax.vmap(picked)(block_values, hard_ids)
    return 0.7 * owner_rows + 0.7141428 * row_values


def query_scales(levels, lowest, highest):
    return jnp.exp(math.log(lowest) + levels * (math.log(highest) - math.log(lowest)))


def candidate_rows(block_values, row_values, spread, negative_noise, scales, positives, hard_ids, alignment, offset, negative_levels):
    unit_rows = directions(block_values, row_values, hard_ids)
    ceiling = math.log(PAIRS) + 1.0
    target = ceiling + offset
    owned = target / (50.0 * scales * alignment) * (alignment * unit_rows + jnp.sqrt(1.0 - alignment * alignment) * spread)
    document_vectors = jax.vmap(placed)(owned, positives)
    distractor_affinity = ceiling - 1.0 + negative_levels
    owner_blocks = jnp.repeat(block_values, HARD, axis=1)
    distractor_vectors = distractor_affinity / 28.0 * (0.8 * owner_blocks + 0.6 * negative_noise)
    return (document_vectors, distractor_vectors)


def draw_positives(key, part):
    return common_layout(key)[0]


def draw_hard_blocks(key, part):
    return common_layout(key)[1]


def draw_queries(key, part):
    positives, hard_ids, block_uniform, row_uniform, alignment, offset, levels = common_layout(key)
    block_values = bell_values(block_uniform)
    row_values = bell_values(row_uniform)
    scales = query_scales(levels, 0.5, 2.0)
    values = scales * directions(block_values, row_values, hard_ids)
    return values.astype(jnp.bfloat16)


def draw_candidates(key, part):
    positives, hard_ids, block_uniform, row_uniform, alignment, offset, levels = common_layout(key)
    key = jax.random.fold_in(key, 23)
    subkeys = jax.random.split(key, 3)
    negative_levels = jax.random.uniform(subkeys[2], (GROUPS, N_DP * HARD, 1), jnp.float32, -1.0, 1.0)
    block_values = bell_values(block_uniform)
    row_values = bell_values(row_uniform)
    spread = jnp.clip(jax.random.normal(subkeys[0], (GROUPS, PAIRS, D), jnp.float32), -4.0, 4.0) * D ** (-0.5)
    negative_noise = jnp.clip(jax.random.normal(subkeys[1], (GROUPS, N_DP * HARD, D), jnp.float32), -4.0, 4.0) * D ** (-0.5)
    scales = query_scales(levels, 0.5, 2.0)
    document_vectors, distractor_vectors = candidate_rows(block_values, row_values, spread, negative_noise, scales, positives, hard_ids, alignment, offset, negative_levels)
    combined = jnp.concatenate([document_vectors.reshape(GROUPS, N_DP, ROWS, D), distractor_vectors.reshape(GROUPS, N_DP, HARD, D)], axis=2)
    return combined.astype(jnp.bfloat16)


def raised(array, own_key, source, target, shards_of, factor):
    owner, partner = [(jnp.arange(array.shape[axis_at]) // (array.shape[axis_at] // shards_of)).reshape([-1 if axis == axis_at else 1 for axis in range(array.ndim)]) for axis_at in (source, target)]
    chosen = jax.random.permutation(own_key, shards_of)[partner]
    strong = (owner == chosen) | (owner == (partner + shards_of // 2) % shards_of)
    return jnp.where(strong, factor * array, array)


def shard_levels(rng, extent, cuts, least, high):
    gain = 1.0
    for position, blocks in cuts:
        steps = jax.random.uniform(jax.random.fold_in(jax.random.fold_in(rng, 6), position), (blocks,), jnp.float32, least / len(cuts), high / len(cuts))
        gain = gain * jnp.repeat(jnp.exp(steps), extent[position] // blocks).reshape((-1,) + (1,) * (len(extent) - 1 - position))
    return gain


def bell_draw(key, extent, scale, bound, cuts=(), kind=jnp.bfloat16):
    factor_of = shard_levels(key, extent, cuts, -0.22, 0.18) if cuts else 1.0
    array = jax.random.normal(key, extent, jnp.float32) * scale * factor_of
    return jnp.minimum(jnp.maximum(array, -bound), bound).astype(kind)


def gaussian_with(key, shape, scale, reach, pieces, heavy, held_as=jnp.bfloat16):
    entries = scale * jax.random.normal(key, shape, jnp.float32)
    if pieces:
        entries = entries * shard_levels(key, shape, pieces, -0.22, 0.18)
    return jnp.clip(raised(entries, jax.random.fold_in(key, 3), *heavy), -reach, reach).astype(held_as)


def setup_inputs(seed: int = 0) -> dict:
    keys = jax.random.split(jax.random.key(seed), 9)
    queries = draw_queries(jax.random.fold_in(keys[8], 71), 0)
    candidates = draw_candidates(jax.random.fold_in(keys[8], 71), 0)
    positives = draw_positives(jax.random.fold_in(keys[8], 71), 0)
    hard_blocks = draw_hard_blocks(jax.random.fold_in(keys[8], 71), 0)
    query_hidden = gaussian_with(keys[4], (GROUPS, PAIRS, D), 1.0, 6.0, ((0, 8), (1, 4)), (1, 2, 4, 2.0))
    candidate_hidden = gaussian_with(keys[5], (GROUPS, N_DP, BLK, D), 1.0, 6.0, ((0, 8), (1, 4)), (0, 3, 8, 2.0))
    adapter_down = bell_draw(keys[6], (R, D), D ** -0.5, 0.09375, ((1, 8),))
    adapter_up = bell_draw(keys[7], (R, D), (16 * D) ** -0.5, 0.0234375, ((1, 8),))
    return {"queries": queries, "candidates": candidates, "positives": positives, "hard_blocks": hard_blocks, "query_hidden": query_hidden, "candidate_hidden": candidate_hidden, "adapter_down": adapter_down, "adapter_up": adapter_up}


sharpness_factor = 50.0
adapter_scale = 2.0


def pairing_matrix(left, right):
    return lax.dot_general(left, right, (((1,), (1,)), ((), ())), preferred_element_type=jnp.float32)


def flipped_pairing_matrix(left, right):
    return lax.dot_general(left, right, (((0,), (0,)), ((), ())), preferred_element_type=jnp.float32)


def one_group(group_args):
    bunched_question_vectors, group_candidates, group_positives, group_hard = group_args
    document_vectors = group_candidates[:, :ROWS].reshape(PAIRS, D)
    distractor_vectors = group_candidates[:, ROWS:].reshape(N_DP * HARD, D)
    document_affinity = pairing_matrix(bunched_question_vectors, document_vectors) * sharpness_factor
    distractor_affinity = pairing_matrix(bunched_question_vectors, distractor_vectors) * sharpness_factor
    owners = (jnp.arange(N_DP * HARD) // HARD).astype(jnp.int32)
    keep_mask = group_hard[:, None] == owners[None, :]
    distractor_affinity = jnp.where(keep_mask, distractor_affinity, -jnp.inf)
    larger = jnp.maximum(jnp.max(document_affinity, axis=1), jnp.max(distractor_affinity, axis=1))
    totals = jnp.sum(jnp.exp(document_affinity - larger[:, None]), axis=1) + jnp.sum(jnp.exp(distractor_affinity - larger[:, None]), axis=1)
    log_total = larger + jnp.log(totals)
    target = (group_positives[:, None] == jnp.arange(PAIRS, dtype=jnp.int32)[None, :]).astype(jnp.float32)
    document_likelihood = (jnp.exp(document_affinity - log_total[:, None]) - target).astype(jnp.bfloat16)
    distractor_likelihood = jnp.exp(distractor_affinity - log_total[:, None]).astype(jnp.bfloat16)
    question_share = jnp.dot(document_likelihood, document_vectors, preferred_element_type=jnp.float32) + jnp.dot(distractor_likelihood, distractor_vectors, preferred_element_type=jnp.float32)
    question_derivative_vectors = (question_share * sharpness_factor).astype(jnp.bfloat16)
    document_derivative = (flipped_pairing_matrix(document_likelihood, bunched_question_vectors) * sharpness_factor).astype(jnp.bfloat16)
    distractor_derivative = (flipped_pairing_matrix(distractor_likelihood, bunched_question_vectors) * sharpness_factor).astype(jnp.bfloat16)
    candidate_grad_rows = jnp.concatenate([document_derivative.reshape(N_DP, ROWS, D), distractor_derivative.reshape(N_DP, HARD, D)], axis=1)
    return question_derivative_vectors, candidate_grad_rows


def reference(queries, candidates, positives, hard_blocks, query_hidden, candidate_hidden, adapter_down, adapter_up):
    question_derivative_vectors, candidate_grad_rows = lax.map(one_group, (queries, candidates, positives, hard_blocks))
    hidden_rows = [query_hidden.reshape(-1, D), candidate_hidden.reshape(-1, D)]
    gradient_rows = [question_derivative_vectors.reshape(-1, D), candidate_grad_rows.reshape(-1, D)]
    up_terms = jnp.zeros((R, D), jnp.float32)
    down_terms = jnp.zeros((R, D), jnp.float32)
    for hidden, gradient in zip(hidden_rows, gradient_rows):
        low = pairing_matrix(hidden, adapter_down).astype(jnp.bfloat16)
        back = pairing_matrix(gradient, adapter_up).astype(jnp.bfloat16)
        up_terms = up_terms + flipped_pairing_matrix(low, gradient)
        down_terms = down_terms + flipped_pairing_matrix(back, hidden)
    return question_derivative_vectors, candidate_grad_rows, down_terms * adapter_scale, up_terms * adapter_scale
```

```python
import functools

import jax
import jax.numpy as jnp
from jax import lax
from jax.experimental import pallas as pl
from jax.experimental.pallas import tpu as pltpu
from jax.sharding import PartitionSpec as P

sharpness_factor = 50.0
adapter_scale = 2.0
STEP = 512
MAX, SUM, POSITIVE, HARD, BODY = 0, 1, 2, 3, 8

f32 = jnp.float32
bf16 = jnp.bfloat16


def dot(left, right, left_dim, right_dim):
    return lax.dot_general(
        left, right, (((left_dim,), (right_dim,)), ((), ())), preferred_element_type=f32
    )


def dot_wide(left, right, left_dim, right_dim):
    high = left.astype(bf16)
    low = (left - high.astype(f32)).astype(bf16)
    return dot(high, right, left_dim, right_dim) + dot(low, right, left_dim, right_dim)


def layout(position, block, shape):
    row = lax.broadcasted_iota(jnp.int32, shape, 0)
    own = row < block
    return jnp.where(own, position, position ^ 1), jnp.where(own, row, row - block)


def allowed(owner, slot, hard, rows):
    return (slot < rows) | (hard.astype(jnp.int32) == owner)


def hits(owner, slot, positive, rows):
    return (slot < rows) & (positive.astype(jnp.int32) == owner * rows + slot)


def merge(stats):
    top = functools.reduce(jnp.maximum, [m for m, _ in stats])
    return top + jnp.log(sum(s * jnp.exp(m - top) for m, s in stats))


def columns(ref, at, width):
    return ref[:, pl.ds(pl.multiple_of(at * width, width), width)]


def scores_kernel(place, c_own, c_sib, q_own, q_sib, positives, hard, scores, stats):
    block, rows = c_own.shape[0], q_own.shape[0]

    def step(i, total):
        c = jnp.concatenate([columns(c_own, i, STEP), columns(c_sib, i, STEP)], 0)
        q = jnp.concatenate([columns(q_own, i, STEP), columns(q_sib, i, STEP)], 0)
        return total + dot(c, q, 1, 1)

    total = lax.fori_loop(
        0, c_own.shape[1] // STEP, step, jnp.zeros((2 * block, 2 * rows), f32), unroll=True
    )
    total = total * sharpness_factor
    scores[...] = total
    mine = total[:, :rows]
    owner, slot = layout(place[0], block, mine.shape)
    mine = jnp.where(allowed(owner, slot, hard[...], rows), mine, -jnp.inf)
    top = jnp.max(mine, axis=0, keepdims=True)
    stats[...] = jnp.zeros_like(stats)
    stats[MAX : MAX + 1] = top
    stats[SUM : SUM + 1] = jnp.sum(jnp.exp(mine - top), axis=0, keepdims=True)
    stats[POSITIVE : POSITIVE + 1] = positives[...].astype(f32)
    stats[HARD : HARD + 1] = hard[...].astype(f32)


def adapter_slice(place, mine, got, at):
    here = place[1] ^ at
    a, b = mine[here], got[here]
    even = (place[0] & 1) == 0
    return jnp.where(even, a, b), jnp.where(even, b, a)


def low_kernel(place, maps, other, hq, hc, c_own, c_sib, stats, message, low_c, c_up):
    shards, rank, width = maps.shape
    rows, block = hq.shape[0], hc.shape[0]

    def step(i, so_far):
        down, up = adapter_slice(place, maps, other, i)
        c = jnp.concatenate([columns(c_own, i, width), columns(c_sib, i, width)], 0)
        return (
            so_far[0] + dot(down, columns(hq, i, width), 1, 1),
            so_far[1] + dot(down, columns(hc, i, width), 1, 1),
            so_far[2] + dot(up, c, 1, 1),
        )

    sums = lax.fori_loop(
        0, shards, step, tuple(jnp.zeros((rank, n), f32) for n in (rows, block, 2 * block))
    )
    message[:BODY] = stats[...]
    message[BODY:] = sums[0].astype(bf16).astype(f32)
    low_c[...] = sums[1].astype(bf16)
    c_up[...] = sums[2]


def partner_kernel(place, c_own, c_sib, q, message, c_up, answer, w_own, w_sib, low_w):
    block, rows = c_own.shape[0], q.shape[0]

    def step(i, total):
        c = jnp.concatenate([columns(c_own, i, STEP), columns(c_sib, i, STEP)], 0)
        return total + dot(c, columns(q, i, STEP), 1, 1)

    total = lax.fori_loop(
        0, c_own.shape[1] // STEP, step, jnp.zeros((2 * block, rows), f32), unroll=True
    )
    owner, slot = layout(place[0], block, total.shape)
    keep = allowed(owner, slot, message[HARD : HARD + 1], rows)
    total = jnp.where(keep, total * sharpness_factor, -jnp.inf)
    top = jnp.max(total, axis=0, keepdims=True)
    share = jnp.sum(jnp.exp(total - top), axis=0, keepdims=True)
    answer[...] = jnp.zeros_like(answer)
    answer[MAX : MAX + 1] = top
    answer[SUM : SUM + 1] = share
    log_total = merge([(message[MAX : MAX + 1], message[SUM : SUM + 1]), (top, share)])
    hit = hits(owner, slot, message[POSITIVE : POSITIVE + 1], rows)
    weights = (jnp.exp(total - log_total) - hit.astype(f32)).astype(bf16)
    answer[BODY:] = dot_wide(c_up[...], weights, 1, 0) * sharpness_factor
    w_own[...] = weights[:block]
    w_sib[...] = weights[block:]
    low_w[...] = dot(message[BODY:].astype(bf16), weights, 1, 1) * sharpness_factor


def share_kernel(w_own, w_sib, c_own, c_sib, share):
    weights = jnp.concatenate([w_own[...], w_sib[...]], 0)
    for i in range(c_own.shape[1] // STEP):
        c = jnp.concatenate([columns(c_own, i, STEP), columns(c_sib, i, STEP)], 0)
        share[:, i * STEP : (i + 1) * STEP] = (dot(weights, c, 0, 0) * sharpness_factor).astype(bf16)


def final_kernel(w_own, w_sib, c_own, c_sib, *rest):
    shares, out = rest[:-1], rest[-1]
    weights = jnp.concatenate([w_own[...], w_sib[...]], 0)
    for i in range(c_own.shape[1] // STEP):
        c = jnp.concatenate([columns(c_own, i, STEP), columns(c_sib, i, STEP)], 0)
        total = dot(weights, c, 0, 0) * sharpness_factor
        for share in shares:
            total = total + share[:, i * STEP : (i + 1) * STEP].astype(f32)
        out[:, i * STEP : (i + 1) * STEP] = total.astype(bf16)


def sums_kernel(partners, place, *refs):
    (c_own, c_sib, q_own, q_sib, hq, hc, maps, other, scores, own, sib, low_c, c_up), refs = refs[:13], refs[13:]
    answers, refs = refs[:partners], refs[partners:]
    sib_answers, refs = refs[:partners], refs[partners:]
    far_q, refs = refs[:partners], refs[partners:]
    far_q_sib, refs = refs[:partners], refs[partners:]
    far_w, refs = refs[:partners], refs[partners:]
    far_w_sib, refs = refs[:partners], refs[partners:]
    far_low, refs = refs[:partners], refs[partners:]
    grad, w_own, w_sib, keep, send, up_terms = refs
    block, rows = c_own.shape[0], q_own.shape[0]
    shards, rank, width = maps.shape

    def stats_of(ref):
        return ref[MAX : MAX + 1], ref[SUM : SUM + 1]

    def both(at):
        return jnp.concatenate([own[at : at + 1], sib[at : at + 1]], 1)

    log_total = jnp.concatenate(
        [
            merge([stats_of(own)] + [stats_of(a) for a in answers]),
            merge([stats_of(sib)] + [stats_of(a) for a in sib_answers]),
        ],
        1,
    )
    owner, slot = layout(place[0], block, scores.shape)
    kept = allowed(owner, slot, both(HARD), rows)
    hit = hits(owner, slot, both(POSITIVE), rows)
    weights = jnp.exp(jnp.where(kept, scores[...] - log_total, -jnp.inf)) - hit.astype(f32)
    weights = weights.astype(bf16)
    mine = weights[:, :rows]
    w_own[...] = mine[:block]
    w_sib[...] = mine[block:]
    low_w = dot(own[BODY:].astype(bf16), mine, 1, 1) * sharpness_factor
    for ref in far_low:
        low_w = low_w + ref[...]
    back_q = dot_wide(c_up[...], mine, 1, 0) * sharpness_factor
    for ref in answers:
        back_q = back_q + ref[BODY:]
    back_q = back_q.astype(bf16)
    all_weights = jnp.concatenate(
        [weights[:block]] + [w[...] for w in far_w] + [w[...] for w in far_w_sib], 1
    )
    all_queries = [q_own, q_sib] + list(far_q) + list(far_q_sib)

    def first(i, back_c):
        _, up = adapter_slice(place, maps, other, i)
        c = jnp.concatenate([columns(c_own, i, width), columns(c_sib, i, width)], 0)
        q = jnp.concatenate([columns(q, i, width) for q in all_queries], 0)
        rows_here = (dot(all_weights, q, 1, 0) * sharpness_factor).astype(bf16)
        grad[:, pl.ds(pl.multiple_of(i * width, width), width)] = rows_here
        up_terms[i] = dot_wide(low_w, c, 1, 0) + dot(low_c[...], rows_here, 1, 0)
        return back_c + dot(up, rows_here, 1, 1)

    back_c = lax.fori_loop(0, shards, first, jnp.zeros((rank, block), f32)).astype(bf16)
    even = (place[0] & 1) == 0

    def second(i, carry):
        down = dot(back_q, columns(hq, i, width), 1, 0) + dot(back_c, columns(hc, i, width), 1, 0)
        up = up_terms[i]
        apart = place[1] ^ i
        slot = (apart & 1) * (shards // 2) + (apart >> 1)
        keep[slot] = jnp.where(even, down, up).astype(bf16)
        send[slot] = jnp.where(even, up, down).astype(bf16)
        return carry

    lax.fori_loop(0, shards, second, 0)


def call(kernel, outs, scratch=(), flops=10_000_000, moved=2_000_000):
    smem = pl.BlockSpec(memory_space=pltpu.SMEM)
    vmem = pl.BlockSpec(memory_space=pltpu.VMEM)

    def run(*args):
        return pl.pallas_call(
            kernel,
            out_shape=outs,
            in_specs=[smem if a.dtype == jnp.int32 and a.ndim == 1 else vmem for a in args],
            out_specs=jax.tree.map(lambda _: vmem, outs),
            scratch_shapes=list(scratch),
            compiler_params=pltpu.CompilerParams(vmem_limit_bytes=40 * 2**20),
            cost_estimate=pl.CostEstimate(flops=flops, bytes_accessed=moved, transcendentals=0),
        )(*args)

    return run


def shaped(shape, dtype=f32):
    return jax.ShapeDtypeStruct(shape, dtype)


def swap(array, axis, apart):
    size = lax.axis_size(axis)
    return lax.ppermute(array, axis, [(i, i ^ apart) for i in range(size)])


def bits_of(size):
    return [1 << b for b in range(size.bit_length() - 1)]


def on_device(
    queries, candidates, positives, hard_blocks, query_hidden, candidate_hidden, adapter_down, adapter_up
):
    q_own, c_own = queries[0], candidates[0, 0]
    hq, hc = query_hidden[0], candidate_hidden[0, 0]
    rows, width = q_own.shape
    block = c_own.shape[0]
    rank, shard_width = adapter_down.shape
    devices, shards = lax.axis_size("dp"), lax.axis_size("fsdp")
    position, shard = lax.axis_index("dp"), lax.axis_index("fsdp")
    place = jnp.stack([position, shard]).astype(jnp.int32)
    partners = list(range(2, devices, 2))
    even = (position & 1) == 0

    far_q = [swap(q_own, "dp", k) for k in partners]
    c_sib, q_sib = swap(c_own, "dp", 1), swap(q_own, "dp", 1)

    maps = jnp.where(even, adapter_down, adapter_up)[None]
    for bit in bits_of(shards):
        maps = jnp.concatenate([maps, swap(maps, "fsdp", bit)], 0)
    other_maps = swap(maps, "dp", 1)

    scores, stats = call(
        scores_kernel, (shaped((2 * block, 2 * rows)), shaped((BODY, rows)))
    )(place, c_own, c_sib, q_own, q_sib, positives, hard_blocks)
    message, low_c, c_up = call(
        low_kernel,
        (shaped((BODY + rank, rows)), shaped((rank, block), bf16), shaped((rank, 2 * block))),
    )(place, maps, other_maps, hq, hc, c_own, c_sib, stats)
    sib_message = swap(message, "dp", 1)
    far_messages = [swap(message, "dp", k) for k in partners]

    answers, sib_answers, far_w, far_w_sib, far_low, shares = [], [], [], [], [], []
    for k, q, far_message in zip(partners, far_q, far_messages):
        answer, w_own, w_sib, low_w = call(
            partner_kernel,
            (
                shaped((BODY + rank, rows)),
                shaped((block, rows), bf16),
                shaped((block, rows), bf16),
                shaped((rank, 2 * block)),
            ),
        )(place, c_own, c_sib, q, far_message, c_up)
        answers.append(swap(answer, "dp", k))
        sib_answers.append(swap(answer, "dp", k ^ 1))
        far_w.append(w_own)
        far_w_sib.append(swap(w_sib, "dp", 1))
        far_low.append(low_w)
        share = call(share_kernel, shaped((rows, width), bf16))(w_own, w_sib, c_own, c_sib)
        shares.append(swap(share, "dp", k))
    far_q_sib = [swap(q, "dp", 1) for q in far_q]

    grad, w_own, w_sib, keep, send = call(
        functools.partial(sums_kernel, len(partners)),
        (
            shaped((block, width), bf16),
            shaped((block, rows), bf16),
            shaped((block, rows), bf16),
            shaped((shards, rank, shard_width), bf16),
            shaped((shards, rank, shard_width), bf16),
        ),
        [pltpu.VMEM((shards, rank, shard_width), f32)],
    )(
        place, c_own, c_sib, q_own, q_sib, hq, hc, maps, other_maps, scores, message, sib_message,
        low_c, c_up, *answers, *sib_answers, *far_q, *far_q_sib, *far_w, *far_w_sib, *far_low,
    )
    question = call(final_kernel, shaped((rows, width), bf16))(w_own, w_sib, c_own, c_sib, *shares)

    terms = keep.astype(f32) + swap(send, "dp", 1).astype(f32)
    for bit in bits_of(shards)[:1] + bits_of(shards)[:0:-1]:
        half = terms.shape[0] // 2
        terms = terms[:half] + swap(terms[half:].astype(bf16), "fsdp", bit).astype(f32)
    terms = terms[0]
    for bit in bits_of(devices)[1:]:
        terms = terms + swap(terms, "dp", bit)
    terms = terms * adapter_scale
    others = swap(terms, "dp", 1)
    return (
        question[None],
        grad[None, None],
        jnp.where(even, terms, others),
        jnp.where(even, others, terms),
    )


def solution(mesh):
    placed = (
        P("fsdp", "dp", None),
        P("fsdp", "dp", None, None),
        P("fsdp", "dp"),
        P("fsdp", "dp"),
        P("fsdp", "dp", None),
        P("fsdp", "dp", None, None),
        P(None, "fsdp"),
        P(None, "fsdp"),
    )
    return jax.shard_map(
        on_device,
        mesh=mesh,
        in_specs=placed,
        out_specs=(
            P("fsdp", "dp", None),
            P("fsdp", "dp", None, None),
            P(None, "fsdp"),
            P(None, "fsdp"),
        ),
        check_vma=False,
    )
```

```python
import functools

import jax
import jax.numpy as jnp
from jax import lax
from jax.experimental import pallas as pl
from jax.experimental.pallas import tpu as pltpu
from jax.sharding import PartitionSpec as P

sharpness_factor = 50.0
adapter_scale = 2.0
STEP = 512
MAX, SUM, POSITIVE, HARD, BODY = 0, 1, 2, 3, 8

f32 = jnp.float32
bf16 = jnp.bfloat16


def bits_of(size):
    return [1 << b for b in range(size.bit_length() - 1)]


def reversed_bits(size):
    bits = bits_of(size)
    return [sum(low for low, high in zip(bits, bits[::-1]) if i & high) for i in range(size)]


def dot(left, right, left_dim, right_dim):
    return lax.dot_general(
        left, right, (((left_dim,), (right_dim,)), ((), ())), preferred_element_type=f32
    )


def dot_wide(left, right, left_dim, right_dim):
    high = left.astype(bf16)
    low = (left - high.astype(f32)).astype(bf16)
    return dot(high, right, left_dim, right_dim) + dot(low, right, left_dim, right_dim)


def layout(position, block, shape):
    row = lax.broadcasted_iota(jnp.int32, shape, 0)
    own = row < block
    return jnp.where(own, position, position ^ 1), jnp.where(own, row, row - block)


def allowed(owner, slot, hard, rows):
    return (slot < rows) | (hard.astype(jnp.int32) == owner)


def hits(owner, slot, positive, rows):
    return (slot < rows) & (positive.astype(jnp.int32) == owner * rows + slot)


def merge(stats):
    top = functools.reduce(jnp.maximum, [m for m, _ in stats])
    return top + jnp.log(sum(s * jnp.exp(m - top) for m, s in stats))


def columns(ref, at, width):
    return ref[:, pl.ds(pl.multiple_of(at * width, width), width)]


def scores_kernel(place, c_own, c_sib, q_own, q_sib, positives, hard, scores, stats):
    block, rows = c_own.shape[0], q_own.shape[0]
    c = jnp.concatenate([c_own[...], c_sib[...]], 0)
    q = jnp.concatenate([q_own[...], q_sib[...]], 0)
    total = dot(c, q, 1, 1) * sharpness_factor
    scores[...] = total
    mine = total[:, :rows]
    owner, slot = layout(place[0], block, mine.shape)
    mine = jnp.where(allowed(owner, slot, hard[...], rows), mine, -jnp.inf)
    top = jnp.max(mine, axis=0, keepdims=True)
    stats[...] = jnp.zeros_like(stats)
    stats[MAX : MAX + 1] = top
    stats[SUM : SUM + 1] = jnp.sum(jnp.exp(mine - top), axis=0, keepdims=True)
    stats[POSITIVE : POSITIVE + 1] = positives[...].astype(f32)
    stats[HARD : HARD + 1] = hard[...].astype(f32)


def adapter_kernel(place, maps, other, hq, hq_sib, hc, hc_sib, c_own, c_sib, q_own, q_sib, message, low_c, c_up):
    shards, rank, width = maps.shape
    places = reversed_bits(shards)
    core = place[0] & 1

    def product(gathered, parts):
        total = 0.0
        for at in range(shards):
            rows = jnp.concatenate([columns(r, at ^ place[1], width) for r in parts], 0)
            total = total + dot(gathered[places[at]], rows, 1, 1)
        return total

    @pl.when(core == 0)
    def _():
        message[...] = product(maps, [hq, hq_sib]).astype(bf16).astype(f32)
        low_c[...] = product(maps, [hc, hc_sib]).astype(bf16)
        c_up[...] = product(other, [c_own, c_sib])

    @pl.when(core == 1)
    def _():
        message[...] = product(maps, [q_own, q_sib])
        low_c[...] = jnp.zeros_like(low_c)
        c_up[...] = product(maps, [c_own, c_sib])


def partner_kernel(place, c_own, c_sib, q, stats, c_up, answer, weights, q_again):
    block, rows = c_own.shape[0], q.shape[0]
    c = jnp.concatenate([c_own[...], c_sib[...]], 0)
    q_again[...] = q[...]
    total = dot(c, q[...], 1, 1)
    owner, slot = layout(place[0], block, total.shape)
    keep = allowed(owner, slot, stats[HARD : HARD + 1], rows)
    total = jnp.where(keep, total * sharpness_factor, -jnp.inf)
    top = jnp.max(total, axis=0, keepdims=True)
    share = jnp.sum(jnp.exp(total - top), axis=0, keepdims=True)
    answer[...] = jnp.zeros_like(answer)
    answer[MAX : MAX + 1] = top
    answer[SUM : SUM + 1] = share
    log_total = merge([(stats[MAX : MAX + 1], stats[SUM : SUM + 1]), (top, share)])
    hit = hits(owner, slot, stats[POSITIVE : POSITIVE + 1], rows)
    here = (jnp.exp(total - log_total) - hit.astype(f32)).astype(bf16)
    answer[BODY:] = dot_wide(c_up[...], here, 1, 0) * sharpness_factor
    weights[...] = here


def share_kernel(weights, c_own, c_sib, share):
    for i in range(c_own.shape[1] // STEP):
        at = slice(i * STEP, (i + 1) * STEP)
        c = jnp.concatenate([c_own[:, at], c_sib[:, at]], 0)
        share[:, at] = (dot(weights[...], c, 0, 0) * sharpness_factor).astype(bf16)


def question_kernel(weights, c_own, c_sib, *rest):
    shares, out = rest[:-1], rest[-1]
    for i in range(c_own.shape[1] // STEP):
        at = slice(i * STEP, (i + 1) * STEP)
        c = jnp.concatenate([c_own[:, at], c_sib[:, at]], 0)
        total = dot(weights[...], c, 0, 0) * sharpness_factor
        for share in shares:
            total = total + share[:, at].astype(f32)
        out[:, at] = total.astype(bf16)


def candidate_kernel(weights, *rest):
    queries, out = rest[:-1], rest[-1]
    for i in range(out.shape[1] // STEP):
        at = slice(i * STEP, (i + 1) * STEP)
        q = jnp.concatenate([r[:, at] for r in queries], 0)
        out[:, at] = (dot(weights[...], q, 1, 0) * sharpness_factor).astype(bf16)


def taken(refs, *counts):
    out, at = [], 0
    for count in counts:
        out.append(list(refs[at : at + count]))
        at += count
    return out


def sums_kernel(partners, place, *refs):
    n = partners
    (c, q, far_q, far_q_sib, hq, hc, stats, answers, sib_answers, far_w, far_w_sib, message, far_messages,
     (scores, low_c, c_up), (share,), (w_grad, w_own, keep, send)) = taken(
        refs, 2, 2, n, n, 2, 2, 2, n, n, n, n, 1, n, 3, n and 1, 4)
    block, rows = c[0].shape[0], q[0].shape[0]
    half, rank, width = keep.shape

    def stats_of(ref):
        return ref[MAX : MAX + 1], ref[SUM : SUM + 1]

    def both(at):
        return jnp.concatenate([ref[at : at + 1] for ref in stats], 1)

    log_total = jnp.concatenate(
        [merge([stats_of(r) for r in group]) for group in ([stats[0]] + answers, [stats[1]] + sib_answers)], 1
    )
    owner, slot = layout(place[0], block, scores.shape)
    kept = allowed(owner, slot, both(HARD), rows)
    hit = hits(owner, slot, both(POSITIVE), rows)
    near = jnp.exp(jnp.where(kept, scores[...] - log_total, -jnp.inf)) - hit.astype(f32)
    near = near.astype(bf16)
    w_own[...] = near[:, :rows]
    pieces = [near]
    for mine, other in zip(far_w, far_w_sib):
        pieces += [mine[...], jnp.concatenate([other[block:], other[:block]], 0)]
    weights = jnp.concatenate(pieces, 1)
    w_grad[...] = weights[:block]
    messages = jnp.concatenate([message[0][...]] + [r[...] for r in far_messages], 1)
    queries = list(q)
    for pair in zip(far_q, far_q_sib):
        queries += pair

    def store(at, total):
        if at & 1:
            send[at >> 1] = total.astype(bf16)
        else:
            keep[at >> 1] = total

    def split(terms):
        high = terms.astype(bf16)
        return jnp.concatenate([high, (terms - high.astype(f32)).astype(bf16)], 0)

    core = place[0] & 1

    @pl.when(core == 0)
    def _():
        by_candidate = split(dot(messages.astype(bf16), weights, 1, 1) * sharpness_factor)
        by_query = split(dot(low_c[...], weights, 1, 0) * sharpness_factor)
        for at in range(2 * half):
            from_c = jnp.concatenate([columns(r, at ^ place[1], width) for r in c], 0)
            from_q = jnp.concatenate([columns(r, at ^ place[1], width) for r in queries], 0)
            total = dot(by_candidate, from_c, 1, 0) + dot(by_query, from_q, 1, 0)
            store(at, total[:rank] + total[rank:])

    @pl.when(core == 1)
    def _():
        back_q = dot_wide(c_up[...], near, 1, 0) * sharpness_factor
        for mine, other in zip(answers, sib_answers):
            back_q = back_q + jnp.concatenate([mine[BODY:], other[BODY:]], 1)
        back_q = back_q.astype(bf16)
        back_c = (dot_wide(messages, weights, 1, 1) * sharpness_factor).astype(bf16)
        for at in range(2 * half):
            from_q = jnp.concatenate([columns(r, at ^ place[1], width) for r in hq], 0)
            from_c = jnp.concatenate([columns(r, at ^ place[1], width) for r in hc], 0)
            store(at, dot(back_q, from_q, 1, 0) + dot(back_c, from_c, 1, 0))


def call(kernel, outs):
    smem = pl.BlockSpec(memory_space=pltpu.SMEM)
    vmem = pl.BlockSpec(memory_space=pltpu.VMEM)

    def run(*args):
        return pl.pallas_call(
            kernel,
            out_shape=outs,
            in_specs=[smem if a.dtype == jnp.int32 and a.ndim == 1 else vmem for a in args],
            out_specs=jax.tree.map(lambda _: vmem, outs),
            compiler_params=pltpu.CompilerParams(vmem_limit_bytes=40 * 2**20),
            cost_estimate=pl.CostEstimate(flops=1000, bytes_accessed=1000, transcendentals=0),
        )(*args)

    return run


def shaped(shape, dtype=f32):
    return jax.ShapeDtypeStruct(shape, dtype)


def swap(array, axis, apart):
    size = lax.axis_size(axis)
    return lax.ppermute(array, axis, [(i, i ^ apart) for i in range(size)])


def on_device(
    queries, candidates, positives, hard_blocks, query_hidden, candidate_hidden, adapter_down, adapter_up
):
    q_own, c_own = queries[0], candidates[0, 0]
    hq, hc = query_hidden[0], candidate_hidden[0, 0]
    rows, width = q_own.shape
    block = c_own.shape[0]
    rank, shard_width = adapter_down.shape
    devices, shards = lax.axis_size("dp"), lax.axis_size("fsdp")
    position, shard = lax.axis_index("dp"), lax.axis_index("fsdp")
    place = jnp.stack([position, shard]).astype(jnp.int32)
    partners = list(range(2, devices, 2))
    even = (position & 1) == 0

    far_q = [swap(q_own, "dp", k) for k in partners]
    c_sib, q_sib, hq_sib, hc_sib = (swap(a, "dp", 1) for a in (c_own, q_own, hq, hc))

    maps = jnp.where(even, adapter_down, adapter_up)[None]
    for bit in bits_of(shards)[::-1]:
        maps = jnp.concatenate([maps, swap(maps, "fsdp", bit)], 0)
    other_maps = swap(maps, "dp", 1)

    scores, stats = call(scores_kernel, (shaped((2 * block, 2 * rows)), shaped((BODY, rows))))(
        place, c_own, c_sib, q_own, q_sib, positives, hard_blocks
    )
    sib_stats = swap(stats, "dp", 1)
    far_stats = [swap(stats, "dp", k) for k in partners]
    message, low_c, c_up = call(
        adapter_kernel, (shaped((rank, 2 * rows)), shaped((rank, 2 * block), bf16), shaped((rank, 2 * block)))
    )(place, maps, other_maps, hq, hq_sib, hc, hc_sib, c_own, c_sib, q_own, q_sib)
    far_messages = [swap(message, "dp", k) for k in partners]

    answers, sib_answers, far_w, far_w_sib, far_q_sib, shares, own_shares = [], [], [], [], [], [], []
    for k, q, far in zip(partners, far_q, far_stats):
        answer, weights, q_again = call(
            partner_kernel,
            (shaped((BODY + rank, rows)), shaped((2 * block, rows), bf16), shaped((rows, width), bf16)),
        )(place, c_own, c_sib, q, far, c_up)
        answers.append(swap(answer, "dp", k))
        sib_answers.append(swap(answer, "dp", k ^ 1))
        far_w.append(weights)
        far_w_sib.append(swap(weights, "dp", 1))
        far_q_sib.append(swap(q_again, "dp", 1))
        own_shares.append(call(share_kernel, shaped((rows, width), bf16))(weights, c_own, c_sib))
        shares.append(swap(own_shares[-1], "dp", k))

    w_grad, w_own, keep, send = call(
        functools.partial(sums_kernel, len(partners)),
        (
            shaped((block, rows * devices), bf16),
            shaped((2 * block, rows), bf16),
            shaped((shards // 2, rank, shard_width)),
            shaped((shards // 2, rank, shard_width), bf16),
        ),
    )(
        place, c_own, c_sib, q_own, q_sib, *far_q, *far_q_sib, hq, hq_sib, hc, hc_sib, stats, sib_stats,
        *answers, *sib_answers, *far_w, *far_w_sib, message, *far_messages, scores, low_c, c_up,
        *own_shares[:1],
    )
    queries = [q_own, q_sib]
    for pair in zip(far_q, far_q_sib):
        queries += pair
    grad = call(candidate_kernel, shaped((block, width), bf16))(w_grad, *queries)
    question = call(question_kernel, shaped((rows, width), bf16))(w_own, c_own, c_sib, *shares)

    bits = bits_of(shards)[:1] + bits_of(shards)[:0:-1]
    terms = keep + swap(send, "fsdp", bits[0]).astype(f32)
    for bit in bits[1:]:
        half = terms.shape[0] // 2
        terms = terms[:half] + swap(terms[half:].astype(bf16), "fsdp", bit).astype(f32)
    terms = terms[0]
    for bit in bits_of(devices)[1:]:
        terms = terms + swap(terms, "dp", bit)
    terms = terms * adapter_scale
    others = swap(terms, "dp", 1)
    return (
        question[None],
        grad[None, None],
        jnp.where(even, others, terms),
        jnp.where(even, terms, others),
    )


def solution(mesh):
    placed = (
        P("fsdp", "dp", None),
        P("fsdp", "dp", None, None),
        P("fsdp", "dp"),
        P("fsdp", "dp"),
        P("fsdp", "dp", None),
        P("fsdp", "dp", None, None),
        P(None, "fsdp"),
        P(None, "fsdp"),
    )
    return jax.shard_map(
        on_device,
        mesh=mesh,
        in_specs=placed,
        out_specs=(
            P("fsdp", "dp", None),
            P("fsdp", "dp", None, None),
            P(None, "fsdp"),
            P(None, "fsdp"),
        ),
        check_vma=False,
    )
```

```python
import functools

import jax
import jax.numpy as jnp
from jax import lax
from jax.experimental import pallas as pl
from jax.experimental.pallas import tpu as pltpu
from jax.sharding import PartitionSpec as P

sharpness_factor = 50.0
adapter_scale = 2.0
STEP = 512
MAX, SUM, POSITIVE, HARD, BODY = 0, 1, 2, 3, 8

f32 = jnp.float32
bf16 = jnp.bfloat16


def bits_of(size):
    return [1 << b for b in range(size.bit_length() - 1)]


def reversed_bits(size):
    bits = bits_of(size)
    return [sum(low for low, high in zip(bits, bits[::-1]) if i & high) for i in range(size)]


def dot(left, right, left_dim, right_dim):
    return lax.dot_general(
        left, right, (((left_dim,), (right_dim,)), ((), ())), preferred_element_type=f32
    )


def dot_wide(left, right, left_dim, right_dim):
    high = left.astype(bf16)
    low = (left - high.astype(f32)).astype(bf16)
    return dot(high, right, left_dim, right_dim) + dot(low, right, left_dim, right_dim)


def layout(position, block, shape):
    row = lax.broadcasted_iota(jnp.int32, shape, 0)
    own = row < block
    return jnp.where(own, position, position ^ 1), jnp.where(own, row, row - block)


def allowed(owner, slot, hard, rows):
    return (slot < rows) | (hard.astype(jnp.int32) == owner)


def hits(owner, slot, positive, rows):
    return (slot < rows) & (positive.astype(jnp.int32) == owner * rows + slot)


def merge(stats):
    top = functools.reduce(jnp.maximum, [m for m, _ in stats])
    return top + jnp.log(sum(s * jnp.exp(m - top) for m, s in stats))


def columns(ref, at, width):
    return ref[:, pl.ds(pl.multiple_of(at * width, width), width)]


def scores_kernel(place, c_own, c_sib, q_own, q_sib, positives, hard, scores, stats):
    block, rows = c_own.shape[0], q_own.shape[0]
    c = jnp.concatenate([c_own[...], c_sib[...]], 0)
    q = jnp.concatenate([q_own[...], q_sib[...]], 0)
    total = dot(c, q, 1, 1) * sharpness_factor
    scores[...] = total
    mine = total[:, :rows]
    owner, slot = layout(place[0], block, mine.shape)
    mine = jnp.where(allowed(owner, slot, hard[...], rows), mine, -jnp.inf)
    top = jnp.max(mine, axis=0, keepdims=True)
    stats[...] = jnp.zeros_like(stats)
    stats[MAX : MAX + 1] = top
    stats[SUM : SUM + 1] = jnp.sum(jnp.exp(mine - top), axis=0, keepdims=True)
    stats[POSITIVE : POSITIVE + 1] = positives[...].astype(f32)
    stats[HARD : HARD + 1] = hard[...].astype(f32)


def adapter_kernel(place, maps, hq, hq_sib, hc, hc_sib, c_own, c_sib, q_own, q_sib, message, low_c, c_up):
    shards, _, rank, width = maps.shape
    places = reversed_bits(shards)
    core = place[0] & 1

    def product(which, parts):
        total = 0.0
        for at in range(shards):
            rows = jnp.concatenate([columns(r, at ^ place[1], width) for r in parts], 0)
            total = total + dot(maps[places[at], which], rows, 1, 1)
        return total

    c_up[...] = product(1, [c_own, c_sib])

    @pl.when(core == 0)
    def _():
        message[...] = product(0, [hq, hq_sib]).astype(bf16).astype(f32)
        low_c[...] = product(0, [hc, hc_sib]).astype(bf16)

    @pl.when(core == 1)
    def _():
        message[...] = product(1, [q_own, q_sib])
        low_c[...] = jnp.zeros_like(low_c)


def partner_kernel(place, c_own, c_sib, *refs):
    *parts, stats, c_up, answer, weights, q_again = refs
    block = c_own.shape[0]
    q = jnp.concatenate([part[...] for part in parts], 1)
    rows = q.shape[0]
    c = jnp.concatenate([c_own[...], c_sib[...]], 0)
    q_again[...] = q
    total = dot(c, q, 1, 1)
    owner, slot = layout(place[0], block, total.shape)
    keep = allowed(owner, slot, stats[HARD : HARD + 1], rows)
    total = jnp.where(keep, total * sharpness_factor, -jnp.inf)
    top = jnp.max(total, axis=0, keepdims=True)
    share = jnp.sum(jnp.exp(total - top), axis=0, keepdims=True)
    answer[...] = jnp.zeros_like(answer)
    answer[MAX : MAX + 1] = top
    answer[SUM : SUM + 1] = share
    log_total = merge([(stats[MAX : MAX + 1], stats[SUM : SUM + 1]), (top, share)])
    hit = hits(owner, slot, stats[POSITIVE : POSITIVE + 1], rows)
    here = (jnp.exp(total - log_total) - hit.astype(f32)).astype(bf16)
    answer[BODY:] = dot_wide(c_up[...], here, 1, 0) * sharpness_factor
    weights[...] = here


def share_kernel(weights, c_own, c_sib, *shares):
    start = 0
    for share in shares:
        for i in range(0, share.shape[1], STEP):
            at = slice(start + i, start + i + STEP)
            c = jnp.concatenate([c_own[:, at], c_sib[:, at]], 0)
            share[:, i : i + STEP] = (dot(weights[...], c, 0, 0) * sharpness_factor).astype(bf16)
        start += share.shape[1]


def question_kernel(pieces, weights, c_own, c_sib, *rest):
    shares, out = rest[:-1], rest[-1]
    start = 0
    for at_piece in range(pieces):
        here = shares[at_piece::pieces]
        for i in range(0, here[0].shape[1], STEP):
            at = slice(start + i, start + i + STEP)
            c = jnp.concatenate([c_own[:, at], c_sib[:, at]], 0)
            total = dot(weights[...], c, 0, 0) * sharpness_factor
            for share in here:
                total = total + share[:, i : i + STEP].astype(f32)
            out[:, at] = total.astype(bf16)
        start += here[0].shape[1]


def candidate_kernel(weights, *rest):
    queries, out = rest[:-1], rest[-1]
    for i in range(out.shape[1] // STEP):
        at = slice(i * STEP, (i + 1) * STEP)
        q = jnp.concatenate([r[:, at] for r in queries], 0)
        out[:, at] = (dot(weights[...], q, 1, 0) * sharpness_factor).astype(bf16)


def taken(refs, *counts):
    out, at = [], 0
    for count in counts:
        out.append(list(refs[at : at + count]))
        at += count
    return out


def sums_kernel(partners, place, *refs):
    n = partners
    (c, q, far_q, far_q_sib, hq, hc, stats, answers, sib_answers, far_w, far_w_sib, message, far_messages,
     (scores, low_c, c_up), (w_grad, w_own, keep, send)) = taken(
        refs, 2, 2, n, n, 2, 2, 2, n, n, n, n, 1, n, 3, 4)
    block, rows = c[0].shape[0], q[0].shape[0]
    half, rank, width = keep.shape

    def stats_of(ref):
        return ref[MAX : MAX + 1], ref[SUM : SUM + 1]

    def both(at):
        return jnp.concatenate([ref[at : at + 1] for ref in stats], 1)

    log_total = jnp.concatenate(
        [merge([stats_of(r) for r in group]) for group in ([stats[0]] + answers, [stats[1]] + sib_answers)], 1
    )
    owner, slot = layout(place[0], block, scores.shape)
    kept = allowed(owner, slot, both(HARD), rows)
    hit = hits(owner, slot, both(POSITIVE), rows)
    near = jnp.exp(jnp.where(kept, scores[...] - log_total, -jnp.inf)) - hit.astype(f32)
    near = near.astype(bf16)
    w_own[...] = near[:, :rows]
    pieces = [near]
    for mine, other in zip(far_w, far_w_sib):
        pieces += [mine[...], jnp.concatenate([other[block:], other[:block]], 0)]
    weights = jnp.concatenate(pieces, 1)
    w_grad[...] = weights[:block]
    messages = jnp.concatenate([message[0][...]] + [r[...] for r in far_messages], 1)
    queries = list(q)
    for pair in zip(far_q, far_q_sib):
        queries += pair

    def store(at, total):
        if at & 1:
            send[at >> 1] = total.astype(bf16)
        else:
            keep[at >> 1] = total

    def split(terms):
        high = terms.astype(bf16)
        return jnp.concatenate([high, (terms - high.astype(f32)).astype(bf16)], 0)

    core = place[0] & 1

    @pl.when(core == 0)
    def _():
        by_candidate = split(dot(messages.astype(bf16), weights, 1, 1) * sharpness_factor)
        by_query = split(dot(low_c[...], weights, 1, 0) * sharpness_factor)
        for at in range(2 * half):
            from_c = jnp.concatenate([columns(r, at ^ place[1], width) for r in c], 0)
            from_q = jnp.concatenate([columns(r, at ^ place[1], width) for r in queries], 0)
            total = dot(by_candidate, from_c, 1, 0) + dot(by_query, from_q, 1, 0)
            store(at, total[:rank] + total[rank:])

    @pl.when(core == 1)
    def _():
        back_q = dot_wide(c_up[...], near, 1, 0) * sharpness_factor
        for mine, other in zip(answers, sib_answers):
            back_q = back_q + jnp.concatenate([mine[BODY:], other[BODY:]], 1)
        back_q = back_q.astype(bf16)
        back_c = (dot_wide(messages, weights, 1, 1) * sharpness_factor).astype(bf16)
        for at in range(2 * half):
            from_q = jnp.concatenate([columns(r, at ^ place[1], width) for r in hq], 0)
            from_c = jnp.concatenate([columns(r, at ^ place[1], width) for r in hc], 0)
            store(at, dot(back_q, from_q, 1, 0) + dot(back_c, from_c, 1, 0))


def call(kernel, outs):
    smem = pl.BlockSpec(memory_space=pltpu.SMEM)
    vmem = pl.BlockSpec(memory_space=pltpu.VMEM)

    def run(*args):
        return pl.pallas_call(
            kernel,
            out_shape=outs,
            in_specs=[smem if a.dtype == jnp.int32 and a.ndim == 1 else vmem for a in args],
            out_specs=jax.tree.map(lambda _: vmem, outs),
            compiler_params=pltpu.CompilerParams(vmem_limit_bytes=40 * 2**20),
            cost_estimate=pl.CostEstimate(flops=1000, bytes_accessed=1000, transcendentals=0),
        )(*args)

    return run


def cut(width, weights):
    steps, total = width // STEP, sum(weights)
    edges = [steps * sum(weights[:i]) // total * STEP for i in range(len(weights) + 1)]
    return [slice(a, b) for a, b in zip(edges, edges[1:])]


def shaped(shape, dtype=f32):
    return jax.ShapeDtypeStruct(shape, dtype)


def swap(array, axis, apart):
    size = lax.axis_size(axis)
    return lax.ppermute(array, axis, [(i, i ^ apart) for i in range(size)])


def on_device(
    queries, candidates, positives, hard_blocks, query_hidden, candidate_hidden, adapter_down, adapter_up
):
    q_own, c_own = queries[0], candidates[0, 0]
    hq, hc = query_hidden[0], candidate_hidden[0, 0]
    rows, width = q_own.shape
    block = c_own.shape[0]
    rank, shard_width = adapter_down.shape
    devices, shards = lax.axis_size("dp"), lax.axis_size("fsdp")
    position, shard = lax.axis_index("dp"), lax.axis_index("fsdp")
    place = jnp.stack([position, shard]).astype(jnp.int32)
    partners = list(range(2, devices, 2))
    even = (position & 1) == 0

    def after(array, *others):
        return lax.optimization_barrier((array, *others))[0]

    far_q = [[swap(q_own[:, at], "dp", k) for at in cut(width, (4, 2, 2))] for k in partners]
    c_sib, q_sib = swap(c_own, "dp", 1), swap(q_own, "dp", 1)
    hq_sib, hc_sib = (swap(after(a, c_sib, q_sib), "dp", 1) for a in (hq, hc))

    scores, stats = call(scores_kernel, (shaped((2 * block, 2 * rows)), shaped((BODY, rows))))(
        place, c_own, c_sib, q_own, q_sib, positives, hard_blocks
    )
    far_stats = [swap(stats, "dp", k) for k in partners]
    sib_stats = swap(stats, "dp", 1)

    bits = bits_of(shards)[::-1]
    maps = jnp.stack([adapter_down, adapter_up])[None]
    for at, bit in enumerate(bits):
        if at == len(bits) - 2:
            maps = after(maps, c_sib, q_sib)
        if at == len(bits) - 1:
            maps = after(maps, scores, *[q[0] for q in far_q])
        maps = jnp.concatenate([maps, swap(maps, "fsdp", bit)], 0)
    maps = after(maps, *[q[1] for q in far_q])
    message, low_c, c_up = call(
        adapter_kernel, (shaped((rank, 2 * rows)), shaped((rank, 2 * block), bf16), shaped((rank, 2 * block)))
    )(place, maps, hq, hq_sib, hc, hc_sib, c_own, c_sib, q_own, q_sib)
    far_messages = [swap(message, "dp", k) for k in partners]
    c_up = after(c_up, sib_stats, *far_messages)

    cuts = [at.stop - at.start for at in cut(width, (2, 3) + (2,) * (len(bits) - 2) + (1,))]
    answers, sib_answers, far_w, far_w_sib, far_q_near, far_q_sib, sent, shares = [], [], [], [], [], [], [], []
    for k, q, far in zip(partners, far_q, far_stats):
        answer, weights, q_again = call(
            partner_kernel,
            (shaped((BODY + rank, rows)), shaped((2 * block, rows), bf16), shaped((rows, width), bf16)),
        )(place, c_own, c_sib, *q, far, c_up)
        answers.append(swap(answer, "dp", k))
        sib_answers.append(swap(answer, "dp", k ^ 1))
        far_w.append(weights)
        far_w_sib.append(swap(weights, "dp", 1))
        far_q_near.append(q_again)
        far_q_sib.append(swap(q_again, "dp", 1))
        parts = call(share_kernel, [shaped((rows, n), bf16) for n in cuts])(weights, c_own, c_sib)
        sent.append(parts)
        shares.append([swap(part, "dp", k) for part in parts])

    scores = after(scores, *[part for parts in sent for part in parts])
    w_grad, w_own, keep, send = call(
        functools.partial(sums_kernel, len(partners)),
        (
            shaped((block, rows * devices), bf16),
            shaped((2 * block, rows), bf16),
            shaped((shards // 2, rank, shard_width)),
            shaped((shards // 2, rank, shard_width), bf16),
        ),
    )(
        place, c_own, c_sib, q_own, q_sib, *far_q_near, *far_q_sib, hq, hq_sib, hc, hc_sib, stats, sib_stats,
        *answers, *sib_answers, *far_w, *far_w_sib, message, *far_messages, scores, low_c, c_up,
    )
    queries = [q_own, q_sib]
    for pair in zip(far_q_near, far_q_sib):
        queries += pair
    grad = call(candidate_kernel, shaped((block, width), bf16))(w_grad, *queries)
    all_shares = [part for parts in shares for part in parts]
    question = call(functools.partial(question_kernel, len(cuts)), shaped((rows, width), bf16))(w_own, c_own, c_sib, *all_shares)

    bits = bits_of(shards)[:1] + bits_of(shards)[:0:-1]
    terms = keep + swap(send, "fsdp", bits[0]).astype(f32)
    for at, bit in enumerate(bits[1:]):
        terms = after(terms, *[parts[at] for parts in shares])
        half = terms.shape[0] // 2
        terms = terms[:half] + swap(terms[half:].astype(bf16), "fsdp", bit).astype(f32)
    terms = after(terms[0], *[parts[-2] for parts in shares])
    for bit in bits_of(devices)[1:]:
        terms = terms + swap(terms, "dp", bit)
    terms = after(terms, *[parts[-1] for parts in shares])
    terms = terms * adapter_scale
    others = swap(terms, "dp", 1)
    return (
        question[None],
        grad[None, None],
        jnp.where(even, others, terms),
        jnp.where(even, terms, others),
    )


def solution(mesh):
    placed = (
        P("fsdp", "dp", None),
        P("fsdp", "dp", None, None),
        P("fsdp", "dp"),
        P("fsdp", "dp"),
        P("fsdp", "dp", None),
        P("fsdp", "dp", None, None),
        P(None, "fsdp"),
        P(None, "fsdp"),
    )
    return jax.shard_map(
        on_device,
        mesh=mesh,
        in_specs=placed,
        out_specs=(
            P("fsdp", "dp", None),
            P("fsdp", "dp", None, None),
            P(None, "fsdp"),
            P(None, "fsdp"),
        ),
        check_vma=False,
    )
```

```python
import functools

import jax
import jax.numpy as jnp
from jax import lax
from jax.experimental import pallas as pl
from jax.experimental.pallas import tpu as pltpu
from jax.sharding import PartitionSpec as P

sharpness_factor = 50.0
adapter_scale = 2.0
STEP = 512
PICKS = {1: [(1,)], 2: [(1,), (0, 1), (1, 1)]}
MAX, SUM, POSITIVE, HARD, BODY = 0, 1, 2, 3, 8

f32 = jnp.float32
bf16 = jnp.bfloat16


def bits_of(size):
    return [1 << b for b in range(size.bit_length() - 1)]


def stages_of(size):
    stages, bits = [], bits_of(size)
    while bits:
        take = 1 if not stages else 2
        stages.append(sorted({sum(b for b, on in zip(bits[:take], pick) if on) for pick in PICKS[take]}))
        bits = bits[take:]
    return stages


def places_of(size):
    order = [0]
    for stage in stages_of(size)[::-1]:
        order = [apart ^ i for apart in [0] + stage for i in order]
    return [order.index(i) for i in range(size)]


def dot(left, right, left_dim, right_dim):
    return lax.dot_general(
        left, right, (((left_dim,), (right_dim,)), ((), ())), preferred_element_type=f32
    )


def dot_wide(left, right, left_dim, right_dim):
    high = left.astype(bf16)
    low = (left - high.astype(f32)).astype(bf16)
    return dot(high, right, left_dim, right_dim) + dot(low, right, left_dim, right_dim)


def layout(position, block, shape):
    row = lax.broadcasted_iota(jnp.int32, shape, 0)
    own = row < block
    return jnp.where(own, position, position ^ 1), jnp.where(own, row, row - block)


def allowed(owner, slot, hard, rows):
    return (slot < rows) | (hard.astype(jnp.int32) == owner)


def hits(owner, slot, positive, rows):
    return (slot < rows) & (positive.astype(jnp.int32) == owner * rows + slot)


def merge(stats):
    top = functools.reduce(jnp.maximum, [m for m, _ in stats])
    return top + jnp.log(sum(s * jnp.exp(m - top) for m, s in stats))


def columns(ref, at, width):
    return ref[:, pl.ds(pl.multiple_of(at * width, width), width)]


def scores_kernel(place, c_own, c_sib, q_own, q_sib, positives, hard, scores, stats):
    block, rows = c_own.shape[0], q_own.shape[0]
    c = jnp.concatenate([c_own[...], c_sib[...]], 0)
    q = jnp.concatenate([q_own[...], q_sib[...]], 0)
    total = dot(c, q, 1, 1) * sharpness_factor
    scores[...] = total
    mine = total[:, :rows]
    owner, slot = layout(place[0], block, mine.shape)
    mine = jnp.where(allowed(owner, slot, hard[...], rows), mine, -jnp.inf)
    top = jnp.max(mine, axis=0, keepdims=True)
    stats[...] = jnp.zeros_like(stats)
    stats[MAX : MAX + 1] = top
    stats[SUM : SUM + 1] = jnp.sum(jnp.exp(mine - top), axis=0, keepdims=True)
    stats[POSITIVE : POSITIVE + 1] = positives[...].astype(f32)
    stats[HARD : HARD + 1] = hard[...].astype(f32)


def adapter_kernel(place, maps, hq, hq_sib, hc, hc_sib, c_own, c_sib, q_own, q_sib, message, low_c, c_up):
    shards, _, rank, width = maps.shape
    places = places_of(shards)
    core = place[0] & 1

    def product(which, parts):
        total = 0.0
        for at in range(shards):
            rows = jnp.concatenate([columns(r, at ^ place[1], width) for r in parts], 0)
            total = total + dot(maps[places[at], which], rows, 1, 1)
        return total

    c_up[...] = product(1, [c_own, c_sib])

    @pl.when(core == 0)
    def _():
        message[...] = product(0, [hq, hq_sib]).astype(bf16).astype(f32)
        low_c[...] = product(0, [hc, hc_sib]).astype(bf16)

    @pl.when(core == 1)
    def _():
        message[...] = product(1, [q_own, q_sib])
        low_c[...] = jnp.zeros_like(low_c)


def partner_kernel(place, c_own, c_sib, *refs):
    *parts, stats, c_up, answer, weights, q_again = refs
    block = c_own.shape[0]
    q = jnp.concatenate([part[...] for part in parts], 0)
    rows = q.shape[0]
    c = jnp.concatenate([c_own[...], c_sib[...]], 0)
    q_again[...] = q
    total = dot(c, q, 1, 1)
    owner, slot = layout(place[0], block, total.shape)
    keep = allowed(owner, slot, stats[HARD : HARD + 1], rows)
    total = jnp.where(keep, total * sharpness_factor, -jnp.inf)
    top = jnp.max(total, axis=0, keepdims=True)
    share = jnp.sum(jnp.exp(total - top), axis=0, keepdims=True)
    answer[...] = jnp.zeros_like(answer)
    answer[MAX : MAX + 1] = top
    answer[SUM : SUM + 1] = share
    log_total = merge([(stats[MAX : MAX + 1], stats[SUM : SUM + 1]), (top, share)])
    hit = hits(owner, slot, stats[POSITIVE : POSITIVE + 1], rows)
    here = (jnp.exp(total - log_total) - hit.astype(f32)).astype(bf16)
    answer[BODY:] = dot_wide(c_up[...], here, 1, 0) * sharpness_factor
    weights[...] = here


def share_kernel(weights, c_own, c_sib, *shares):
    start = 0
    for share in shares:
        for i in range(0, share.shape[1], STEP):
            at = slice(start + i, start + i + STEP)
            c = jnp.concatenate([c_own[:, at], c_sib[:, at]], 0)
            share[:, i : i + STEP] = (dot(weights[...], c, 0, 0) * sharpness_factor).astype(bf16)
        start += share.shape[1]


def question_kernel(pieces, weights, c_own, c_sib, *rest):
    shares, out = rest[:-1], rest[-1]
    start = 0
    for at_piece in range(pieces):
        here = shares[at_piece::pieces]
        for i in range(0, here[0].shape[1], STEP):
            at = slice(start + i, start + i + STEP)
            c = jnp.concatenate([c_own[:, at], c_sib[:, at]], 0)
            total = dot(weights[...], c, 0, 0) * sharpness_factor
            for share in here:
                total = total + share[:, i : i + STEP].astype(f32)
            out[:, at] = total.astype(bf16)
        start += here[0].shape[1]


def candidate_kernel(weights, *rest):
    queries, out = rest[:-1], rest[-1]
    for i in range(out.shape[1] // STEP):
        at = slice(i * STEP, (i + 1) * STEP)
        q = jnp.concatenate([r[:, at] for r in queries], 0)
        out[:, at] = (dot(weights[...], q, 1, 0) * sharpness_factor).astype(bf16)


def taken(refs, *counts):
    out, at = [], 0
    for count in counts:
        out.append(list(refs[at : at + count]))
        at += count
    return out


def sums_kernel(partners, place, *refs):
    n = partners
    (c, q, far_q, far_q_sib, hq, hc, stats, answers, sib_answers, far_w, far_w_sib, message, far_messages,
     (scores, low_c, c_up), (w_grad, w_own, keep, send)) = taken(
        refs, 2, 2, n, n, 2, 2, 2, n, n, n, n, 1, n, 3, 4)
    block, rows = c[0].shape[0], q[0].shape[0]
    half, rank, width = keep.shape

    def stats_of(ref):
        return ref[MAX : MAX + 1], ref[SUM : SUM + 1]

    def both(at):
        return jnp.concatenate([ref[at : at + 1] for ref in stats], 1)

    log_total = jnp.concatenate(
        [merge([stats_of(r) for r in group]) for group in ([stats[0]] + answers, [stats[1]] + sib_answers)], 1
    )
    owner, slot = layout(place[0], block, scores.shape)
    kept = allowed(owner, slot, both(HARD), rows)
    hit = hits(owner, slot, both(POSITIVE), rows)
    near = jnp.exp(jnp.where(kept, scores[...] - log_total, -jnp.inf)) - hit.astype(f32)
    near = near.astype(bf16)
    w_own[...] = near[:, :rows]
    pieces = [near]
    for mine, other in zip(far_w, far_w_sib):
        pieces += [mine[...], jnp.concatenate([other[block:], other[:block]], 0)]
    weights = jnp.concatenate(pieces, 1)
    w_grad[...] = weights[:block]
    messages = jnp.concatenate([message[0][...]] + [r[...] for r in far_messages], 1)
    queries = list(q)
    for pair in zip(far_q, far_q_sib):
        queries += pair

    order = places_of(2 * half)

    def store(at, total):
        slot = order[at]
        if slot >= half:
            send[slot - half] = total.astype(bf16)
        else:
            keep[slot] = total

    def split(terms):
        high = terms.astype(bf16)
        return jnp.concatenate([high, (terms - high.astype(f32)).astype(bf16)], 0)

    core = place[0] & 1

    @pl.when(core == 0)
    def _():
        by_candidate = split(dot(messages.astype(bf16), weights, 1, 1) * sharpness_factor)
        by_query = split(dot(low_c[...], weights, 1, 0) * sharpness_factor)
        for at in range(2 * half):
            from_c = jnp.concatenate([columns(r, at ^ place[1], width) for r in c], 0)
            from_q = jnp.concatenate([columns(r, at ^ place[1], width) for r in queries], 0)
            total = dot(by_candidate, from_c, 1, 0) + dot(by_query, from_q, 1, 0)
            store(at, total[:rank] + total[rank:])

    @pl.when(core == 1)
    def _():
        back_q = dot_wide(c_up[...], near, 1, 0) * sharpness_factor
        for mine, other in zip(answers, sib_answers):
            back_q = back_q + jnp.concatenate([mine[BODY:], other[BODY:]], 1)
        back_q = back_q.astype(bf16)
        back_c = (dot_wide(messages, weights, 1, 1) * sharpness_factor).astype(bf16)
        for at in range(2 * half):
            from_q = jnp.concatenate([columns(r, at ^ place[1], width) for r in hq], 0)
            from_c = jnp.concatenate([columns(r, at ^ place[1], width) for r in hc], 0)
            store(at, dot(back_q, from_q, 1, 0) + dot(back_c, from_c, 1, 0))


def call(kernel, outs):
    smem = pl.BlockSpec(memory_space=pltpu.SMEM)
    vmem = pl.BlockSpec(memory_space=pltpu.VMEM)

    def run(*args):
        return pl.pallas_call(
            kernel,
            out_shape=outs,
            in_specs=[smem if a.dtype == jnp.int32 and a.ndim == 1 else vmem for a in args],
            out_specs=jax.tree.map(lambda _: vmem, outs),
            compiler_params=pltpu.CompilerParams(vmem_limit_bytes=16 * 2**20),
            cost_estimate=pl.CostEstimate(flops=1000, bytes_accessed=1000, transcendentals=0),
        )(*args)

    return run


def cut(width, weights):
    steps, total = width // STEP, sum(weights)
    edges = [steps * sum(weights[:i]) // total * STEP for i in range(len(weights) + 1)]
    return [slice(a, b) for a, b in zip(edges, edges[1:])]


def halves(size):
    return slice(0, size // 2), slice(size // 2, size)


def shaped(shape, dtype=f32):
    return jax.ShapeDtypeStruct(shape, dtype)


def swap(array, axis, apart):
    size = lax.axis_size(axis)
    return lax.ppermute(array, axis, [(i, i ^ apart) for i in range(size)])


def on_device(
    queries, candidates, positives, hard_blocks, query_hidden, candidate_hidden, adapter_down, adapter_up
):
    q_own, c_own = queries[0], candidates[0, 0]
    hq, hc = query_hidden[0], candidate_hidden[0, 0]
    rows, width = q_own.shape
    block = c_own.shape[0]
    rank, shard_width = adapter_down.shape
    devices, shards = lax.axis_size("dp"), lax.axis_size("fsdp")
    position, shard = lax.axis_index("dp"), lax.axis_index("fsdp")
    place = jnp.stack([position, shard]).astype(jnp.int32)
    partners = list(range(2, devices, 2))
    even = (position & 1) == 0

    def after(array, *others):
        return lax.optimization_barrier((array, *others))[0]

    far_q = [[swap(q_own[at], "dp", k) for at in halves(rows)] for k in partners]
    stages = stages_of(shards)
    maps = jnp.stack([adapter_down, adapter_up])[None]
    c_sib = swap(c_own, "dp", 1)
    for stage in stages[::-1]:
        if stage is stages[0]:
            maps = after(maps, c_sib, *[q[0] for q in far_q])
            q_sib, hq_sib, hc_sib = (swap(after(a, maps), "dp", 1) for a in (q_own, hq, hc))
        maps = jnp.concatenate([maps] + [swap(maps, "fsdp", apart) for apart in stage], 0)
    scores, stats = call(scores_kernel, (shaped((2 * block, 2 * rows)), shaped((BODY, rows))))(
        place, c_own, c_sib, q_own, q_sib, positives, hard_blocks
    )
    far_stats = [swap(stats, "dp", k) for k in partners]
    sib_stats = swap(stats, "dp", 1)
    message, low_c, c_up = call(
        adapter_kernel, (shaped((rank, 2 * rows)), shaped((rank, 2 * block), bf16), shaped((rank, 2 * block)))
    )(place, maps, hq, hq_sib, hc, hc_sib, c_own, c_sib, q_own, q_sib)
    far_messages = [swap(message, "dp", k) for k in partners]

    cuts = [width // 4, width // 2, width // 4]
    answers, sib_answers, far_w, far_w_sib, far_q_near, far_q_sib, sent, shares = [], [], [], [], [], [], [], []
    for k, q, far in zip(partners, far_q, far_stats):
        answer, weights, q_again = call(
            partner_kernel,
            (shaped((BODY + rank, rows)), shaped((2 * block, rows), bf16), shaped((rows, width), bf16)),
        )(place, c_own, c_sib, *q, far, c_up)
        answers.append(swap(answer, "dp", k))
        sib_answers.append(swap(answer, "dp", k ^ 1))
        far_w.append(weights)
        far_w_sib.append(swap(weights, "dp", 1))
        far_q_near.append(q_again)
        far_q_sib.append(swap(q_again, "dp", 1))
        sent.append(call(share_kernel, [shaped((rows, n), bf16) for n in cuts])(weights, c_own, c_sib))
        shares.append([swap(part, "dp", k) for part in sent[-1]])

    scores = after(scores, *[part for parts in sent for part in parts])
    w_grad, w_own, keep, send = call(
        functools.partial(sums_kernel, len(partners)),
        (
            shaped((block, rows * devices), bf16),
            shaped((2 * block, rows), bf16),
            shaped((shards // 2, rank, shard_width)),
            shaped((shards // 2, rank, shard_width), bf16),
        ),
    )(
        place, c_own, c_sib, q_own, q_sib, *far_q_near, *far_q_sib, hq, hq_sib, hc, hc_sib, stats, sib_stats,
        *answers, *sib_answers, *far_w, *far_w_sib, message, *far_messages, scores, low_c, c_up,
    )
    queries = [q_own, q_sib]
    for pair in zip(far_q_near, far_q_sib):
        queries += pair
    grad = call(candidate_kernel, shaped((block, width), bf16))(w_grad, *queries)
    question = call(functools.partial(question_kernel, len(cuts)), shaped((rows, width), bf16))(
        w_own, c_own, c_sib, *[part for parts in shares for part in parts]
    )

    terms = keep + swap(send, "fsdp", 1).astype(f32)
    for at, stage in enumerate(stages[1:]):
        terms = after(terms, *[parts[0] for parts in shares]) if at == 0 else terms
        part = terms.shape[0] // (len(stage) + 1)
        got = [swap(terms[(i + 1) * part : (i + 2) * part].astype(bf16), "fsdp", apart) for i, apart in enumerate(stage)]
        terms = sum([g.astype(f32) for g in got], terms[:part])
    terms = after(terms[0], *[parts[1] for parts in shares])
    for bit in bits_of(devices)[1:]:
        terms = terms + swap(terms, "dp", bit)
    terms = terms * adapter_scale
    others = swap(terms, "dp", 1)
    return (
        question[None],
        grad[None, None],
        jnp.where(even, others, terms),
        jnp.where(even, terms, others),
    )


def solution(mesh):
    placed = (
        P("fsdp", "dp", None),
        P("fsdp", "dp", None, None),
        P("fsdp", "dp"),
        P("fsdp", "dp"),
        P("fsdp", "dp", None),
        P("fsdp", "dp", None, None),
        P(None, "fsdp"),
        P(None, "fsdp"),
    )
    return jax.shard_map(
        on_device,
        mesh=mesh,
        in_specs=placed,
        out_specs=(
            P("fsdp", "dp", None),
            P("fsdp", "dp", None, None),
            P(None, "fsdp"),
            P(None, "fsdp"),
        ),
        check_vma=False,
    )
```

```python
import functools

import jax
import jax.numpy as jnp
from jax import lax
from jax.experimental import pallas as pl
from jax.experimental.pallas import tpu as pltpu
from jax.sharding import PartitionSpec as P

sharpness_factor = 50.0
adapter_scale = 2.0
STEP = 512
MAX, SUM, POSITIVE, HARD, STATS = 0, 1, 2, 3, 8
EXTRA = 16

f32 = jnp.float32
bf16 = jnp.bfloat16


def dot(left, right, left_dim, right_dim):
    return lax.dot_general(
        left, right, (((left_dim,), (right_dim,)), ((), ())), preferred_element_type=f32
    )


def dot_wide(left, right, left_dim, right_dim):
    high = left.astype(bf16)
    low = (left - high.astype(f32)).astype(bf16)
    return dot(high, right, left_dim, right_dim) + dot(low, right, left_dim, right_dim)


def layout(position, block, shape):
    row = lax.broadcasted_iota(jnp.int32, shape, 0)
    own = row < block
    return jnp.where(own, position, position ^ 1), jnp.where(own, row, row - block)


def allowed(owner, slot, hard, rows):
    return (slot < rows) | (hard.astype(jnp.int32) == owner)


def hits(owner, slot, positive, rows):
    return (slot < rows) & (positive.astype(jnp.int32) == owner * rows + slot)


def merge(stats):
    top = functools.reduce(jnp.maximum, [m for m, _ in stats])
    return top + jnp.log(sum(s * jnp.exp(m - top) for m, s in stats))


def terms_of(row):
    rows = []
    for _ in range(3):
        rows.append(row.astype(bf16))
        row = row - rows[-1].astype(f32)
    return rows


def whole(rows):
    rows = rows.astype(f32)
    return rows[0:1] + rows[1:2] + rows[2:3]


def packed(weights, top, share):
    block, rows = weights.shape[0] // 2, weights.shape[1]
    stats = jnp.concatenate(terms_of(top) + terms_of(share) + [jnp.zeros((EXTRA - 6, rows), bf16)], 0)
    return jnp.concatenate(
        [jnp.concatenate([weights[:block], weights[block:]], 1), jnp.concatenate([stats, stats], 1)], 0
    )


def unpacked(packet, turned=False):
    block, rows = packet.shape[0] - EXTRA, packet.shape[1] // 2
    halves = packet[:block, :rows], packet[:block, rows:]
    return jnp.concatenate(halves[::-1] if turned else halves, 0)


def packet_stats(packet):
    at, rows = packet.shape[0] - EXTRA, packet.shape[1] // 2
    return whole(packet[at : at + 3, :rows]), whole(packet[at + 3 : at + 6, :rows])


def columns(ref, at, width):
    return ref[:, pl.ds(pl.multiple_of(at * width, width), width)]


def scores_kernel(place, c_own, c_sib, q_own, q_sib, positives, hard, scores, stats):
    block, rows = c_own.shape[0], q_own.shape[0]
    c = jnp.concatenate([c_own[...], c_sib[...]], 0)
    q = jnp.concatenate([q_own[...], q_sib[...]], 0)
    total = dot(c, q, 1, 1) * sharpness_factor
    scores[...] = total
    mine = total[:, :rows]
    owner, slot = layout(place[0], block, mine.shape)
    mine = jnp.where(allowed(owner, slot, hard[...], rows), mine, -jnp.inf)
    top = jnp.max(mine, axis=0, keepdims=True)
    stats[...] = jnp.zeros_like(stats)
    stats[MAX : MAX + 1] = top
    stats[SUM : SUM + 1] = jnp.sum(jnp.exp(mine - top), axis=0, keepdims=True)
    stats[POSITIVE : POSITIVE + 1] = positives[...].astype(f32)
    stats[HARD : HARD + 1] = hard[...].astype(f32)


def adapter_kernel(place, maps, hq, hq_sib, hc, hc_sib, c_own, c_sib, q_own, q_sib, factors):
    shards, _, width = maps.shape

    def product(parts):
        total = 0.0
        for at in range(shards):
            rows = jnp.concatenate([r[:, at * width : (at + 1) * width] for r in parts], 0)
            total = total + dot(maps[at], rows, 1, 1)
        return total

    core = place[0] & 1

    @pl.when(core == 0)
    def _():
        factors[...] = product([hq, hq_sib, hc, hc_sib]).astype(bf16).astype(f32)

    @pl.when(core == 1)
    def _():
        factors[...] = product([q_own, q_sib, c_own, c_sib])


def partner_kernel(place, c_own, c_sib, q, stats, packet, q_again):
    block, rows = c_own.shape[0], q.shape[0]
    c = jnp.concatenate([c_own[...], c_sib[...]], 0)
    q_again[...] = q[...]
    total = dot(c, q[...], 1, 1)
    owner, slot = layout(place[0], block, total.shape)
    keep = allowed(owner, slot, stats[HARD : HARD + 1], rows)
    total = jnp.where(keep, total * sharpness_factor, -jnp.inf)
    top = jnp.max(total, axis=0, keepdims=True)
    share = jnp.sum(jnp.exp(total - top), axis=0, keepdims=True)
    log_total = merge([(stats[MAX : MAX + 1], stats[SUM : SUM + 1]), (top, share)])
    hit = hits(owner, slot, stats[POSITIVE : POSITIVE + 1], rows)
    packet[...] = packed((jnp.exp(total - log_total) - hit.astype(f32)).astype(bf16), top, share)


def share_kernel(packet, c_own, c_sib, share):
    weights = unpacked(packet[...])
    for i in range(share.shape[1] // STEP):
        at = slice(i * STEP, (i + 1) * STEP)
        c = jnp.concatenate([c_own[:, at], c_sib[:, at]], 0)
        share[:, at] = (dot(weights, c, 0, 0) * sharpness_factor).astype(bf16)


def question_kernel(weights, c_own, c_sib, *rest):
    shares, out = rest[:-1], rest[-1]
    for i in range(out.shape[1] // STEP):
        at = slice(i * STEP, (i + 1) * STEP)
        c = jnp.concatenate([c_own[:, at], c_sib[:, at]], 0)
        total = dot(weights[...], c, 0, 0) * sharpness_factor
        for share in shares:
            total = total + share[:, at].astype(f32)
        out[:, at] = total.astype(bf16)


def candidate_kernel(weights, *rest):
    queries, out = rest[:-1], rest[-1]
    for i in range(out.shape[1] // STEP):
        at = slice(i * STEP, (i + 1) * STEP)
        q = jnp.concatenate([r[:, at] for r in queries], 0)
        out[:, at] = (dot(weights[...], q, 1, 0) * sharpness_factor).astype(bf16)


def taken(refs, *counts):
    out, at = [], 0
    for count in counts:
        out.append(list(refs[at : at + count]))
        at += count
    return out


def sums_kernel(partners, place, *refs):
    n = partners
    (c, q, far_q, far_q_sib, hq, hc, stats, answers, sib_answers, made, made_sib, (factors,), far_factors,
     (scores,), (w_grad, w_own, terms)) = taken(refs, 2, 2, n, n, 2, 2, 2, n, n, n, n, 1, n, 1, 3)
    block, rows = c[0].shape[0], q[0].shape[0]
    shards, rank, width = terms.shape

    def both(at):
        return jnp.concatenate([ref[at : at + 1] for ref in stats], 1)

    def log_total(own, packets):
        return merge([(own[MAX : MAX + 1], own[SUM : SUM + 1])] + [packet_stats(p) for p in packets])

    owner, slot = layout(place[0], block, scores.shape)
    kept = allowed(owner, slot, both(HARD), rows)
    hit = hits(owner, slot, both(POSITIVE), rows)
    log_totals = jnp.concatenate([log_total(stats[0], answers), log_total(stats[1], sib_answers)], 1)
    near = jnp.exp(jnp.where(kept, scores[...] - log_totals, -jnp.inf)) - hit.astype(f32)
    near = near.astype(bf16)
    w_own[...] = near[:, :rows]
    pieces = [near]
    for mine, other in zip(made, made_sib):
        pieces += [unpacked(mine[...]), unpacked(other[...], turned=True)]
    weights = jnp.concatenate(pieces, 1)
    w_grad[...] = weights[:block]
    by_query = jnp.concatenate([r[:, : 2 * rows] for r in [factors] + far_factors], 1)
    by_candidate = factors[:, 2 * rows :]
    queries = list(q)
    for pair in zip(far_q, far_q_sib):
        queries += pair

    def split(terms):
        high = terms.astype(bf16)
        return jnp.concatenate([high, (terms - high.astype(f32)).astype(bf16)], 0)

    core = place[0] & 1

    @pl.when(core == 0)
    def _():
        over_c = split(dot(by_query.astype(bf16), weights, 1, 1) * sharpness_factor)
        over_q = split(dot(by_candidate.astype(bf16), weights, 1, 0) * sharpness_factor)
        for i in range(shards):
            at = slice(i * width, (i + 1) * width)
            from_c = jnp.concatenate([r[:, at] for r in c], 0)
            from_q = jnp.concatenate([r[:, at] for r in queries], 0)
            total = dot(over_c, from_c, 1, 0) + dot(over_q, from_q, 1, 0)
            terms[i] = (total[:rank] + total[rank:]).astype(bf16)

    @pl.when(core == 1)
    def _():
        back_q = dot_wide(by_candidate, near, 1, 0)
        for far, mine, other in zip(far_factors, answers, sib_answers):
            there = jnp.concatenate([unpacked(mine[...]), unpacked(other[...], turned=True)], 1)
            back_q = back_q + dot_wide(far[:, 2 * rows :], there, 1, 0)
        back_q = (back_q * sharpness_factor).astype(bf16)
        back_c = (dot_wide(by_query, weights, 1, 1) * sharpness_factor).astype(bf16)
        for i in range(shards):
            at = slice(i * width, (i + 1) * width)
            from_q = jnp.concatenate([r[:, at] for r in hq], 0)
            from_c = jnp.concatenate([r[:, at] for r in hc], 0)
            terms[i] = (dot(back_q, from_q, 1, 0) + dot(back_c, from_c, 1, 0)).astype(bf16)


def call(kernel, outs):
    smem = pl.BlockSpec(memory_space=pltpu.SMEM)
    vmem = pl.BlockSpec(memory_space=pltpu.VMEM)

    def run(*args):
        return pl.pallas_call(
            kernel,
            out_shape=outs,
            in_specs=[smem if a.dtype == jnp.int32 and a.ndim == 1 else vmem for a in args],
            out_specs=jax.tree.map(lambda _: vmem, outs),
            compiler_params=pltpu.CompilerParams(vmem_limit_bytes=16 * 2**20),
            cost_estimate=pl.CostEstimate(flops=1000, bytes_accessed=1000, transcendentals=0),
        )(*args)

    return run


def cut(width, weights):
    steps, total = width // STEP, sum(weights)
    edges = [steps * sum(weights[:i]) // total * STEP for i in range(len(weights) + 1)]
    return [slice(a, b) for a, b in zip(edges, edges[1:])]


def shaped(shape, dtype=f32):
    return jax.ShapeDtypeStruct(shape, dtype)


def swap(array, axis, apart):
    return lax.ppermute(array, axis, [(i, i ^ apart) for i in range(lax.axis_size(axis))])


def after(array, *others):
    return lax.optimization_barrier((array, *others))[0]


def on_device(
    queries, candidates, positives, hard_blocks, query_hidden, candidate_hidden, adapter_down, adapter_up
):
    q_own, c_own = queries[0], candidates[0, 0]
    hq, hc = query_hidden[0], candidate_hidden[0, 0]
    rows, width = q_own.shape
    block = c_own.shape[0]
    rank, shard_width = adapter_down.shape
    devices, shards = lax.axis_size("dp"), lax.axis_size("fsdp")
    position, shard = lax.axis_index("dp"), lax.axis_index("fsdp")
    place = jnp.stack([position, shard]).astype(jnp.int32)
    partners = list(range(2, devices, 2))
    even = (position & 1) == 0

    far_q = [swap(q_own, "dp", k) for k in partners]
    c_sib, q_sib, hq_sib, hc_sib = (swap(a, "dp", 1) for a in (c_own, q_own, hq, hc))
    scores, stats = call(scores_kernel, (shaped((2 * block, 2 * rows)), shaped((STATS, rows))))(
        place, c_own, c_sib, q_own, q_sib, positives, hard_blocks
    )
    far_stats = [swap(stats, "dp", k) for k in partners]
    sib_stats = swap(stats, "dp", 1)

    mine = jnp.broadcast_to(jnp.where(even, adapter_down, adapter_up), (shards, rank, shard_width))
    maps = lax.all_to_all(after(mine, scores, c_sib), "fsdp", 0, 0)

    factors = call(adapter_kernel, shaped((rank, 2 * rows + 2 * block)))(
        place, maps, hq, hq_sib, hc, hc_sib, c_own, c_sib, q_own, q_sib
    )
    far_factors = [swap(factors, "dp", k) for k in partners]

    far_stats[0:1] = [after(stat, factors, sib_stats) for stat in far_stats[0:1]]

    made, made_sib, answers, sib_answers, far_q_near, far_q_sib, sent, shares = [], [], [], [], [], [], [], []
    for k, q, far in zip(partners, far_q, far_stats):
        packet, q_again = call(
            partner_kernel, (shaped((block + EXTRA, 2 * rows), bf16), shaped((rows, width), bf16))
        )(place, c_own, c_sib, q, far)
        answers.append(swap(packet, "dp", k))
        sib_answers.append(swap(packet, "dp", k ^ 1))
        made.append(packet)
        made_sib.append(swap(packet, "dp", 1))
        far_q_near.append(q_again)
        far_q_sib.append(swap(q_again, "dp", 1))
        sent.append(call(share_kernel, shaped((rows, width), bf16))(after(packet, made_sib[-1], *far_factors), c_own, c_sib))
        shares.append(swap(after(sent[-1], answers[-1], sib_answers[-1]), "dp", k))
    scores = after(scores, *sent)
    w_grad, w_own, terms = call(
        functools.partial(sums_kernel, len(partners)),
        (
            shaped((block, rows * devices), bf16),
            shaped((2 * block, rows), bf16),
            shaped((shards, rank, shard_width), bf16),
        ),
    )(
        place, c_own, c_sib, q_own, q_sib, *far_q_near, *far_q_sib, hq, hq_sib, hc, hc_sib, stats, sib_stats,
        *answers, *sib_answers, *made, *made_sib, factors, *far_factors, scores,
    )
    queries = [q_own, q_sib]
    for pair in zip(far_q_near, far_q_sib):
        queries += pair
    grad = call(candidate_kernel, shaped((block, width), bf16))(w_grad, *queries)
    question = call(question_kernel, shaped((rows, width), bf16))(w_own, c_own, c_sib, *shares)

    terms = jnp.sum(lax.all_to_all(terms, "fsdp", 0, 0).astype(f32), 0)
    terms = after(terms, *shares)
    apart = 2
    while apart < devices:
        terms = terms + swap(terms, "dp", apart)
        apart *= 2
    terms = terms * adapter_scale
    others = swap(terms, "dp", 1)
    return (
        question[None],
        grad[None, None],
        jnp.where(even, others, terms),
        jnp.where(even, terms, others),
    )


def solution(mesh):
    placed = (
        P("fsdp", "dp", None),
        P("fsdp", "dp", None, None),
        P("fsdp", "dp"),
        P("fsdp", "dp"),
        P("fsdp", "dp", None),
        P("fsdp", "dp", None, None),
        P(None, "fsdp"),
        P(None, "fsdp"),
    )
    return jax.shard_map(
        on_device,
        mesh=mesh,
        in_specs=placed,
        out_specs=(
            P("fsdp", "dp", None),
            P("fsdp", "dp", None, None),
            P(None, "fsdp"),
            P(None, "fsdp"),
        ),
        check_vma=False,
    )
```

```python
import functools

import jax
import jax.numpy as jnp
from jax import lax
from jax.experimental import pallas as pl
from jax.experimental.pallas import tpu as pltpu
from jax.sharding import PartitionSpec as P

sharpness_factor = 50.0
adapter_scale = 2.0
STEP = 512
MAX, SUM, POSITIVE, HARD, STATS = 0, 1, 2, 3, 8
EXTRA = 16

f32 = jnp.float32
bf16 = jnp.bfloat16


def dot(left, right, left_dim, right_dim):
    return lax.dot_general(
        left, right, (((left_dim,), (right_dim,)), ((), ())), preferred_element_type=f32
    )


def dot_wide(left, right, left_dim, right_dim):
    high = left.astype(bf16)
    low = (left - high.astype(f32)).astype(bf16)
    return dot(high, right, left_dim, right_dim) + dot(low, right, left_dim, right_dim)


def layout(position, block, shape):
    row = lax.broadcasted_iota(jnp.int32, shape, 0)
    own = row < block
    return jnp.where(own, position, position ^ 1), jnp.where(own, row, row - block)


def allowed(owner, slot, hard, rows):
    return (slot < rows) | (hard.astype(jnp.int32) == owner)


def hits(owner, slot, positive, rows):
    return (slot < rows) & (positive.astype(jnp.int32) == owner * rows + slot)


def merge(stats):
    top = functools.reduce(jnp.maximum, [m for m, _ in stats])
    return top + jnp.log(sum(s * jnp.exp(m - top) for m, s in stats))


def terms_of(row):
    rows = []
    for _ in range(3):
        rows.append(row.astype(bf16))
        row = row - rows[-1].astype(f32)
    return rows


def whole(rows):
    rows = rows.astype(f32)
    return rows[0:1] + rows[1:2] + rows[2:3]


def packed(weights, top, share):
    block, rows = weights.shape[0] // 2, weights.shape[1]
    stats = jnp.concatenate(terms_of(top) + terms_of(share) + [jnp.zeros((EXTRA - 6, rows), bf16)], 0)
    return jnp.concatenate(
        [jnp.concatenate([weights[:block], weights[block:]], 1), jnp.concatenate([stats, stats], 1)], 0
    )


def unpacked(packet, turned=False):
    block, rows = packet.shape[0] - EXTRA, packet.shape[1] // 2
    halves = packet[:block, :rows], packet[:block, rows:]
    return jnp.concatenate(halves[::-1] if turned else halves, 0)


def packet_stats(packet):
    at, rows = packet.shape[0] - EXTRA, packet.shape[1] // 2
    return whole(packet[at : at + 3, :rows]), whole(packet[at + 3 : at + 6, :rows])


def wide_rows(array):
    high = array.astype(bf16)
    return [high, (array - high.astype(f32)).astype(bf16)]


def factor_rows(factors, rows, block):
    out = wide_rows(factors[:, : 2 * rows])
    for start in (2 * rows, 2 * rows + block):
        part = factors[:, start : start + block]
        out += [jnp.concatenate([p, jnp.zeros((p.shape[0], 2 * rows - block), bf16)], 1) for p in wide_rows(part)]
    return jnp.concatenate(out, 0)


def factors_of(packed_rows, block):
    rank = packed_rows.shape[0] // 6
    high, low = [[packed_rows[(2 * i + j) * rank : (2 * i + j + 1) * rank].astype(f32) for i in range(3)] for j in (0, 1)]
    query, own, sib = [a + b for a, b in zip(high, low)]
    return query, jnp.concatenate([own[:, :block], sib[:, :block]], 1)


def columns(ref, at, width):
    return ref[:, pl.ds(pl.multiple_of(at * width, width), width)]


def scores_kernel(c_own, c_sib, q_own, q_sib, positives, hard, scores, stats):
    block, rows = c_own.shape[0], q_own.shape[0]
    c = jnp.concatenate([c_own[...], c_sib[...]], 0)
    q = jnp.concatenate([q_own[...], q_sib[...]], 0)
    total = dot(c, q, 1, 1) * sharpness_factor
    scores[...] = total
    mine = total[:, :rows]
    owner, slot = layout(lax.axis_index("dp"), block, mine.shape)
    mine = jnp.where(allowed(owner, slot, hard[...], rows), mine, -jnp.inf)
    top = jnp.max(mine, axis=0, keepdims=True)
    stats[...] = jnp.zeros_like(stats)
    stats[MAX : MAX + 1] = top
    stats[SUM : SUM + 1] = jnp.sum(jnp.exp(mine - top), axis=0, keepdims=True)
    stats[POSITIVE : POSITIVE + 1] = positives[...].astype(f32)
    stats[HARD : HARD + 1] = hard[...].astype(f32)


def adapter_kernel(maps, hq, hq_sib, hc, hc_sib, c_own, c_sib, q_own, q_sib, factors):
    shards, _, width = maps.shape

    def product(parts):
        out = []
        for r in parts:
            total = 0.0
            for at in range(shards):
                total = total + dot(r[:, at * width : (at + 1) * width], maps[at], 1, 1)
            out.append(total)
        return jnp.concatenate(out, 0).T

    core = lax.axis_index("dp") & 1

    @pl.when(core == 0)
    def _():
        factors[...] = product([hq, hq_sib, hc, hc_sib]).astype(bf16).astype(f32)

    @pl.when(core == 1)
    def _():
        factors[...] = product([q_own, q_sib, c_own, c_sib])


def partner_kernel(c_own, c_sib, q, stats, factors, message, packet, q_again):
    block, rows = c_own.shape[0], q.shape[0]
    c = jnp.concatenate([c_own[...], c_sib[...]], 0)
    q_again[...] = q[...]
    total = dot(c, q[...], 1, 1)
    owner, slot = layout(lax.axis_index("dp"), block, total.shape)
    keep = allowed(owner, slot, stats[HARD : HARD + 1], rows)
    total = jnp.where(keep, total * sharpness_factor, -jnp.inf)
    top = jnp.max(total, axis=0, keepdims=True)
    share = jnp.sum(jnp.exp(total - top), axis=0, keepdims=True)
    log_total = merge([(stats[MAX : MAX + 1], stats[SUM : SUM + 1]), (top, share)])
    hit = hits(owner, slot, stats[POSITIVE : POSITIVE + 1], rows)
    here = packed((jnp.exp(total - log_total) - hit.astype(f32)).astype(bf16), top, share)
    packet[...] = here
    message[: here.shape[0]] = here
    message[here.shape[0] :] = factor_rows(factors[...], rows, block)


def share_kernel(packet, c_own, c_sib, share):
    weights = unpacked(packet[...])
    for i in range(share.shape[1] // STEP):
        at = slice(i * STEP, (i + 1) * STEP)
        c = jnp.concatenate([c_own[:, at], c_sib[:, at]], 0)
        share[:, at] = (dot(weights, c, 0, 0) * sharpness_factor).astype(bf16)


def question_kernel(weights, c_own, c_sib, *rest):
    shares, out = rest[:-1], rest[-1]
    for i in range(out.shape[1] // STEP):
        at = slice(i * STEP, (i + 1) * STEP)
        c = jnp.concatenate([c_own[:, at], c_sib[:, at]], 0)
        total = dot(weights[...], c, 0, 0) * sharpness_factor
        for share in shares:
            total = total + share[:, at].astype(f32)
        out[:, at] = total.astype(bf16)


def candidate_kernel(weights, *rest):
    queries, out = rest[:-1], rest[-1]
    for i in range(out.shape[1] // STEP):
        at = slice(i * STEP, (i + 1) * STEP)
        q = jnp.concatenate([r[:, at] for r in queries], 0)
        out[:, at] = (dot(weights[...], q, 1, 0) * sharpness_factor).astype(bf16)


def taken(refs, *counts):
    out, at = [], 0
    for count in counts:
        out.append(list(refs[at : at + count]))
        at += count
    return out


def sums_kernel(partners, *refs):
    n = partners
    (c, q, far_q, far_q_sib, hq, hc, stats, answers, sib_answers, made, made_sib, (factors, scores),
     (w_grad, w_own, terms)) = taken(refs, 2, 2, n, n, 2, 2, 2, n, n, n, n, 2, 3)
    block, rows = c[0].shape[0], q[0].shape[0]
    shards, rank, width = terms.shape
    end = block + EXTRA
    far_factors = [factors_of(a[end:], block) for a in answers]
    answers = [a[:end] for a in answers]

    def both(at):
        return jnp.concatenate([ref[at : at + 1] for ref in stats], 1)

    def log_total(own, packets):
        return merge([(own[MAX : MAX + 1], own[SUM : SUM + 1])] + [packet_stats(p) for p in packets])

    owner, slot = layout(lax.axis_index("dp"), block, scores.shape)
    kept = allowed(owner, slot, both(HARD), rows)
    hit = hits(owner, slot, both(POSITIVE), rows)
    log_totals = jnp.concatenate([log_total(stats[0], answers), log_total(stats[1], sib_answers)], 1)
    near = jnp.exp(jnp.where(kept, scores[...] - log_totals, -jnp.inf)) - hit.astype(f32)
    near = near.astype(bf16)
    w_own[...] = near[:, :rows]
    pieces = [near]
    for mine, other in zip(made, made_sib):
        pieces += [unpacked(mine[...]), unpacked(other[...], turned=True)]
    weights = jnp.concatenate(pieces, 1)
    w_grad[...] = weights[:block]
    by_query = jnp.concatenate([r[:, : 2 * rows] for r in [factors] + [f for f, _ in far_factors]], 1)
    by_candidate = factors[:, 2 * rows :]
    queries = list(q)
    for pair in zip(far_q, far_q_sib):
        queries += pair

    def split(terms):
        high = terms.astype(bf16)
        return jnp.concatenate([high, (terms - high.astype(f32)).astype(bf16)], 0)

    core = lax.axis_index("dp") & 1

    @pl.when(core == 0)
    def _():
        over_c = split(dot(by_query.astype(bf16), weights, 1, 1) * sharpness_factor)
        over_q = split(dot(by_candidate.astype(bf16), weights, 1, 0) * sharpness_factor)
        for i in range(shards):
            at = slice(i * width, (i + 1) * width)
            from_c = jnp.concatenate([r[:, at] for r in c], 0)
            from_q = jnp.concatenate([r[:, at] for r in queries], 0)
            total = dot(over_c, from_c, 1, 0) + dot(over_q, from_q, 1, 0)
            terms[i] = (total[:rank] + total[rank:]).astype(bf16)

    @pl.when(core == 1)
    def _():
        back_q = dot_wide(by_candidate, near, 1, 0)
        for far, mine, other in zip(far_factors, answers, sib_answers):
            there = jnp.concatenate([unpacked(mine), unpacked(other[...], turned=True)], 1)
            back_q = back_q + dot_wide(far[1], there, 1, 0)
        back_q = (back_q * sharpness_factor).astype(bf16)
        back_c = (dot_wide(by_query, weights, 1, 1) * sharpness_factor).astype(bf16)
        for i in range(shards):
            at = slice(i * width, (i + 1) * width)
            from_q = jnp.concatenate([r[:, at] for r in hq], 0)
            from_c = jnp.concatenate([r[:, at] for r in hc], 0)
            terms[i] = (dot(back_q, from_q, 1, 0) + dot(back_c, from_c, 1, 0)).astype(bf16)


def call(kernel, outs, needs=()):
    vmem = pl.BlockSpec(memory_space=pltpu.VMEM)
    anywhere = pl.BlockSpec(memory_space=pl.ANY)

    def run(*args):
        def body(*refs):
            kernel(*refs[: len(args)], *refs[len(args) + len(needs) :])

        return pl.pallas_call(
            body,
            out_shape=outs,
            in_specs=[vmem] * len(args) + [anywhere] * len(needs),
            out_specs=jax.tree.map(lambda _: vmem, outs),
            compiler_params=pltpu.CompilerParams(vmem_limit_bytes=16 * 2**20),
            cost_estimate=pl.CostEstimate(flops=1000, bytes_accessed=1000, transcendentals=0),
        )(*args, *needs)

    return run


def shaped(shape, dtype=f32):
    return jax.ShapeDtypeStruct(shape, dtype)


def swap(array, axis, apart):
    return lax.ppermute(array, axis, [(i, i ^ apart) for i in range(lax.axis_size(axis))])


def after(array, *others):
    return lax.optimization_barrier((array, *others))[0]


def on_device(
    queries, candidates, positives, hard_blocks, query_hidden, candidate_hidden, adapter_down, adapter_up
):
    q_own, c_own = queries[0], candidates[0, 0]
    hq, hc = query_hidden[0], candidate_hidden[0, 0]
    rows, width = q_own.shape
    block = c_own.shape[0]
    rank, shard_width = adapter_down.shape
    devices, shards = lax.axis_size("dp"), lax.axis_size("fsdp")
    position = lax.axis_index("dp")
    partners = list(range(2, devices, 2))
    even = (position & 1) == 0

    far_q = [swap(q_own, "dp", k) for k in partners]
    c_sib, q_sib, hq_sib, hc_sib = (swap(a, "dp", 1) for a in (c_own, q_own, hq, hc))
    scores, stats = call(scores_kernel, (shaped((2 * block, 2 * rows)), shaped((STATS, rows))), [hq_sib, hc_sib])(
        c_own, c_sib, q_own, q_sib, positives, hard_blocks
    )
    far_stats = [swap(stats, "dp", k) for k in partners]
    sib_stats = swap(stats, "dp", 1)

    mine = jnp.broadcast_to(jnp.where(even, adapter_down, adapter_up), (shards, rank, shard_width))
    maps = lax.all_to_all(mine, "fsdp", 0, 0)

    factors = call(adapter_kernel, shaped((rank, 2 * rows + 2 * block)), [stats])(
        maps, hq, hq_sib, hc, hc_sib, c_own, c_sib, q_own, q_sib
    )
    made, made_sib, answers, sib_answers, far_q_near, far_q_sib, sent, shares = [], [], [], [], [], [], [], []
    for k, q, far in zip(partners, far_q, far_stats):
        message, packet, q_again = call(
            partner_kernel,
            (
                shaped((block + EXTRA + 6 * rank, 2 * rows), bf16),
                shaped((block + EXTRA, 2 * rows), bf16),
                shaped((rows, width), bf16),
            ),
            [sib_stats],
        )(c_own, c_sib, q, far, factors)
        answers.append(swap(message, "dp", k))
        sib_answers.append(swap(packet, "dp", k ^ 1))
        made.append(packet)
        made_sib.append(swap(packet, "dp", 1))
        far_q_near.append(q_again)
        far_q_sib.append(swap(q_again, "dp", 1))
        sent.append(call(share_kernel, shaped((rows, width), bf16), [made_sib[-1]])(packet, c_own, c_sib))
        shares.append(swap(after(sent[-1], answers[-1], sib_answers[-1]), "dp", k))
    w_grad, w_own, terms = call(
        functools.partial(sums_kernel, len(partners)),
        (
            shaped((block, rows * devices), bf16),
            shaped((2 * block, rows), bf16),
            shaped((shards, rank, shard_width), bf16),
        ),
        sent,
    )(
        c_own, c_sib, q_own, q_sib, *far_q_near, *far_q_sib, hq, hq_sib, hc, hc_sib, stats, sib_stats,
        *answers, *sib_answers, *made, *made_sib, factors, scores,
    )
    queries = [q_own, q_sib]
    for pair in zip(far_q_near, far_q_sib):
        queries += pair
    grad = call(candidate_kernel, shaped((block, width), bf16))(w_grad, *queries)
    question = call(question_kernel, shaped((rows, width), bf16))(w_own, c_own, c_sib, *shares)

    terms = lax.all_to_all(terms, "fsdp", 0, 0)
    terms = after(jnp.sum(terms.astype(f32), 0), *shares)
    apart = 2
    while apart < devices:
        terms = terms + after(swap(terms, "dp", apart), question, grad)
        apart *= 2
    terms = terms * adapter_scale
    others = swap(terms, "dp", 1)
    return (
        question[None],
        grad[None, None],
        jnp.where(even, others, terms),
        jnp.where(even, terms, others),
    )


def solution(mesh):
    placed = (
        P("fsdp", "dp", None),
        P("fsdp", "dp", None, None),
        P("fsdp", "dp"),
        P("fsdp", "dp"),
        P("fsdp", "dp", None),
        P("fsdp", "dp", None, None),
        P(None, "fsdp"),
        P(None, "fsdp"),
    )
    return jax.shard_map(
        on_device,
        mesh=mesh,
        in_specs=placed,
        out_specs=(
            P("fsdp", "dp", None),
            P("fsdp", "dp", None, None),
            P(None, "fsdp"),
            P(None, "fsdp"),
        ),
        check_vma=False,
    )
```

```python
import functools

import jax
import jax.numpy as jnp
from jax import lax
from jax.experimental import pallas as pl
from jax.experimental.pallas import tpu as pltpu
from jax.sharding import PartitionSpec as P

sharpness_factor = 50.0
adapter_scale = 2.0
STEP = 512
MAX, SUM, POSITIVE, HARD, STATS = 0, 1, 2, 3, 8
EXTRA = 16

f32 = jnp.float32
bf16 = jnp.bfloat16


def dot(left, right, left_dim, right_dim):
    return lax.dot_general(
        left, right, (((left_dim,), (right_dim,)), ((), ())), preferred_element_type=f32
    )


def dot_wide(left, right, left_dim, right_dim):
    high = left.astype(bf16)
    low = (left - high.astype(f32)).astype(bf16)
    return dot(high, right, left_dim, right_dim) + dot(low, right, left_dim, right_dim)


def layout(position, block, shape):
    row = lax.broadcasted_iota(jnp.int32, shape, 0)
    own = row < block
    return jnp.where(own, position, position ^ 1), jnp.where(own, row, row - block)


def allowed(owner, slot, hard, rows):
    return (slot < rows) | (hard.astype(jnp.int32) == owner)


def hits(owner, slot, positive, rows):
    return (slot < rows) & (positive.astype(jnp.int32) == owner * rows + slot)


def merge(stats):
    top = functools.reduce(jnp.maximum, [m for m, _ in stats])
    return top + jnp.log(sum(s * jnp.exp(m - top) for m, s in stats))


def terms_of(row):
    rows = []
    for _ in range(3):
        rows.append(row.astype(bf16))
        row = row - rows[-1].astype(f32)
    return rows


def whole(rows):
    rows = rows.astype(f32)
    return rows[0:1] + rows[1:2] + rows[2:3]


def packed(weights, top, share, stats):
    block, rows = weights.shape[0] // 2, weights.shape[1]
    lines = terms_of(top) + terms_of(share)
    for at in (MAX, SUM, POSITIVE):
        lines += terms_of(stats[at : at + 1])
    lines.append(stats[HARD : HARD + 1].astype(bf16))
    lines = jnp.concatenate(lines, 0)
    return jnp.concatenate(
        [jnp.concatenate([weights[:block], weights[block:]], 1), jnp.concatenate([lines, lines], 1)], 0
    )


def unpacked(packet, turned=False):
    block, rows = packet.shape[0] - EXTRA, packet.shape[1] // 2
    halves = packet[:block, :rows], packet[:block, rows:]
    return jnp.concatenate(halves[::-1] if turned else halves, 0)


def packet_stats(packet):
    at, rows = packet.shape[0] - EXTRA, packet.shape[1] // 2
    return whole(packet[at : at + 3, :rows]), whole(packet[at + 3 : at + 6, :rows])


def sender_stats(packet):
    at, rows = packet.shape[0] - EXTRA, packet.shape[1] // 2
    three = [whole(packet[at + i : at + i + 3, :rows]) for i in (6, 9, 12)]
    return three + [packet[at + 15 : at + 16, :rows].astype(f32)]


def wide_rows(array):
    high = array.astype(bf16)
    return [high, (array - high.astype(f32)).astype(bf16)]


def factor_rows(factors, rows, block):
    out = wide_rows(factors[:, : 2 * rows])
    for start in (2 * rows, 2 * rows + block):
        part = factors[:, start : start + block]
        out += [jnp.concatenate([p, jnp.zeros((p.shape[0], 2 * rows - block), bf16)], 1) for p in wide_rows(part)]
    return jnp.concatenate(out, 0)


def factors_of(packed_rows, block):
    rank = packed_rows.shape[0] // 6
    high, low = [[packed_rows[(2 * i + j) * rank : (2 * i + j + 1) * rank].astype(f32) for i in range(3)] for j in (0, 1)]
    query, own, sib = [a + b for a, b in zip(high, low)]
    return query, jnp.concatenate([own[:, :block], sib[:, :block]], 1)


def columns(ref, at, width):
    return ref[:, pl.ds(pl.multiple_of(at * width, width), width)]


def scores_kernel(c_own, c_sib, q_own, q_sib, positives, hard, scores, stats):
    block, rows = c_own.shape[0], q_own.shape[0]
    c = jnp.concatenate([c_own[...], c_sib[...]], 0)
    q = jnp.concatenate([q_own[...], q_sib[...]], 0)
    total = dot(c, q, 1, 1) * sharpness_factor
    scores[...] = total
    mine = total[:, :rows]
    owner, slot = layout(lax.axis_index("dp"), block, mine.shape)
    mine = jnp.where(allowed(owner, slot, hard[...], rows), mine, -jnp.inf)
    top = jnp.max(mine, axis=0, keepdims=True)
    stats[...] = jnp.zeros_like(stats)
    stats[MAX : MAX + 1] = top
    stats[SUM : SUM + 1] = jnp.sum(jnp.exp(mine - top), axis=0, keepdims=True)
    stats[POSITIVE : POSITIVE + 1] = positives[...].astype(f32)
    stats[HARD : HARD + 1] = hard[...].astype(f32)


def copies_kernel(own, out):
    for i in range(out.shape[0]):
        out[i] = own[...]


def adapter_kernel(maps, hq, hq_sib, hc, hc_sib, c_own, c_sib, q_own, q_sib, factors):
    shards, _, width = maps.shape

    def product(parts):
        out = []
        for r in parts:
            total = 0.0
            for at in range(shards):
                total = total + dot(r[:, at * width : (at + 1) * width], maps[at], 1, 1)
            out.append(total)
        return jnp.concatenate(out, 0).T

    core = lax.axis_index("dp") & 1

    @pl.when(core == 0)
    def _():
        factors[...] = product([hq, hq_sib, hc, hc_sib]).astype(bf16).astype(f32)

    @pl.when(core == 1)
    def _():
        factors[...] = product([q_own, q_sib, c_own, c_sib])


def partner_kernel(c_own, c_sib, q, stats, own_stats, factors, message, packet, q_again):
    block, rows = c_own.shape[0], q.shape[0]
    c = jnp.concatenate([c_own[...], c_sib[...]], 0)
    q_again[...] = q[...]
    total = dot(c, q[...], 1, 1)
    owner, slot = layout(lax.axis_index("dp"), block, total.shape)
    keep = allowed(owner, slot, stats[HARD : HARD + 1], rows)
    total = jnp.where(keep, total * sharpness_factor, -jnp.inf)
    top = jnp.max(total, axis=0, keepdims=True)
    share = jnp.sum(jnp.exp(total - top), axis=0, keepdims=True)
    log_total = merge([(stats[MAX : MAX + 1], stats[SUM : SUM + 1]), (top, share)])
    hit = hits(owner, slot, stats[POSITIVE : POSITIVE + 1], rows)
    here = packed((jnp.exp(total - log_total) - hit.astype(f32)).astype(bf16), top, share, own_stats)
    packet[...] = here
    message[: here.shape[0]] = here
    message[here.shape[0] :] = factor_rows(factors[...], rows, block)


def share_kernel(packet, c_own, c_sib, share):
    weights = unpacked(packet[...])
    for i in range(share.shape[1] // STEP):
        at = slice(i * STEP, (i + 1) * STEP)
        c = jnp.concatenate([c_own[:, at], c_sib[:, at]], 0)
        share[:, at] = (dot(weights, c, 0, 0) * sharpness_factor).astype(bf16)


def rows_kernel(partners, w_own, w_grad, c_own, c_sib, *refs):
    queries, shares, (question, grad), here, (sems,) = taken(refs, 2 * partners + 2, partners, 2, 2, 1)
    half = question.shape[1] // 2
    out = []
    for i, (target, rows) in enumerate(zip((question, grad), here)):
        for j in range(2):
            part = pl.ds(j * half, half)
            out.append(pltpu.make_async_copy(rows.at[:, part], target.at[:, part], sems.at[2 * i + j]))
    for j in range(2):
        for start in range(j * half, (j + 1) * half, STEP):
            at = slice(start, start + STEP)
            c = jnp.concatenate([c_own[:, at], c_sib[:, at]], 0)
            total = dot(w_own[...], c, 0, 0) * sharpness_factor
            for share in shares:
                total = total + share[:, at].astype(f32)
            here[0][:, at] = total.astype(bf16)
        out[j].start()
    for j in range(2):
        for start in range(j * half, (j + 1) * half, STEP):
            at = slice(start, start + STEP)
            q = jnp.concatenate([r[:, at] for r in queries], 0)
            here[1][:, at] = (dot(w_grad[...], q, 1, 0) * sharpness_factor).astype(bf16)
        out[2 + j].start()
    for copy in out:
        copy.wait()


def taken(refs, *counts):
    out, at = [], 0
    for count in counts:
        out.append(list(refs[at : at + count]))
        at += count
    return out


def sums_kernel(partners, *refs):
    n = partners
    (c, q, far_q, far_q_sib, hq, hc, (stats,), answers, sib_answers, made, made_sib, (factors, scores),
     (w_grad, w_own, terms)) = taken(refs, 2, 2, n, n, 2, 2, 1, n, n, n, n, 2, 3)
    block, rows = c[0].shape[0], q[0].shape[0]
    shards, rank, width = terms.shape
    end = block + EXTRA
    far_factors = [factors_of(a[end:], block) for a in answers]
    answers, sib_answers = [[a[:end] for a in group] for group in (answers, sib_answers)]

    own = [stats[at : at + 1] for at in (MAX, SUM, POSITIVE, HARD)]
    sib = sender_stats(made_sib[0])

    def log_total(chip, packets):
        return merge([(chip[0], chip[1])] + [packet_stats(p) for p in packets])

    owner, slot = layout(lax.axis_index("dp"), block, scores.shape)
    kept = allowed(owner, slot, jnp.concatenate([own[3], sib[3]], 1), rows)
    hit = hits(owner, slot, jnp.concatenate([own[2], sib[2]], 1), rows)
    log_totals = jnp.concatenate([log_total(own, answers), log_total(sib, sib_answers)], 1)
    near = jnp.exp(jnp.where(kept, scores[...] - log_totals, -jnp.inf)) - hit.astype(f32)
    near = near.astype(bf16)
    w_own[...] = near[:, :rows]
    pieces = [near]
    for mine, other in zip(made, made_sib):
        pieces += [unpacked(mine[...]), unpacked(other[...], turned=True)]
    weights = jnp.concatenate(pieces, 1)
    w_grad[...] = weights[:block]
    by_query = jnp.concatenate([r[:, : 2 * rows] for r in [factors] + [f for f, _ in far_factors]], 1)
    by_candidate = factors[:, 2 * rows :]
    queries = list(q)
    for pair in zip(far_q, far_q_sib):
        queries += pair

    def split(terms):
        high = terms.astype(bf16)
        return jnp.concatenate([high, (terms - high.astype(f32)).astype(bf16)], 0)

    core = lax.axis_index("dp") & 1

    @pl.when(core == 0)
    def _():
        over_c = split(dot(by_query.astype(bf16), weights, 1, 1) * sharpness_factor)
        over_q = split(dot(by_candidate.astype(bf16), weights, 1, 0) * sharpness_factor)
        for i in range(shards):
            at = slice(i * width, (i + 1) * width)
            from_c = jnp.concatenate([r[:, at] for r in c], 0)
            from_q = jnp.concatenate([r[:, at] for r in queries], 0)
            total = dot(over_c, from_c, 1, 0) + dot(over_q, from_q, 1, 0)
            terms[i] = (total[:rank] + total[rank:]).astype(bf16)

    @pl.when(core == 1)
    def _():
        back_q = dot_wide(by_candidate, near, 1, 0)
        for far, mine, other in zip(far_factors, answers, sib_answers):
            there = jnp.concatenate([unpacked(mine), unpacked(other, turned=True)], 1)
            back_q = back_q + dot_wide(far[1], there, 1, 0)
        back_q = (back_q * sharpness_factor).astype(bf16)
        back_c = (dot_wide(by_query, weights, 1, 1) * sharpness_factor).astype(bf16)
        for i in range(shards):
            at = slice(i * width, (i + 1) * width)
            from_q = jnp.concatenate([r[:, at] for r in hq], 0)
            from_c = jnp.concatenate([r[:, at] for r in hc], 0)
            terms[i] = (dot(back_q, from_q, 1, 0) + dot(back_c, from_c, 1, 0)).astype(bf16)


def call(kernel, outs, needs=(), cost=0, scratch=(), away=False):
    vmem = pl.BlockSpec(memory_space=pltpu.VMEM)
    anywhere = pl.BlockSpec(memory_space=pl.ANY)

    def run(*args):
        def body(*refs):
            kernel(*refs[: len(args)], *refs[len(args) + len(needs) :])

        return pl.pallas_call(
            body,
            out_shape=outs,
            in_specs=[vmem] * len(args) + [anywhere] * len(needs),
            out_specs=jax.tree.map(lambda _: anywhere if away else vmem, outs),
            scratch_shapes=list(scratch),
            compiler_params=pltpu.CompilerParams(vmem_limit_bytes=16 * 2**20),
            cost_estimate=pl.CostEstimate(flops=1000 + cost, bytes_accessed=1000 + cost // 300, transcendentals=0),
        )(*args, *needs)

    return run


def shaped(shape, dtype=f32):
    return jax.ShapeDtypeStruct(shape, dtype)


def swap(array, axis, apart):
    return lax.ppermute(array, axis, [(i, i ^ apart) for i in range(lax.axis_size(axis))])


def after(array, *others):
    return lax.optimization_barrier((array, *others))[0]


def on_device(
    queries, candidates, positives, hard_blocks, query_hidden, candidate_hidden, adapter_down, adapter_up
):
    q_own, c_own = queries[0], candidates[0, 0]
    hq, hc = query_hidden[0], candidate_hidden[0, 0]
    rows, width = q_own.shape
    block = c_own.shape[0]
    rank, shard_width = adapter_down.shape
    devices, shards = lax.axis_size("dp"), lax.axis_size("fsdp")
    position = lax.axis_index("dp")
    partners = list(range(2, devices, 2))
    even = (position & 1) == 0

    far_q = [swap(q_own, "dp", k) for k in partners]
    c_sib, q_sib, hq_sib, hc_sib = (swap(a, "dp", 1) for a in (c_own, q_own, hq, hc))
    mine = call(copies_kernel, shaped((shards, rank, shard_width), bf16), cost=5_000_000_000)(
        jnp.where(even, adapter_down, adapter_up)
    )
    maps = lax.all_to_all(mine, "fsdp", 0, 0)

    scores, stats = call(scores_kernel, (shaped((2 * block, 2 * rows)), shaped((STATS, rows))), [maps])(
        c_own, c_sib, q_own, q_sib, positives, hard_blocks
    )
    far_stats = [swap(stats, "dp", k) for k in partners]

    factors = call(adapter_kernel, shaped((rank, 2 * rows + 2 * block)), [stats])(
        maps, hq, hq_sib, hc, hc_sib, c_own, c_sib, q_own, q_sib
    )
    made, made_sib, answers, sib_answers, far_q_near, far_q_sib, sent, shares = [], [], [], [], [], [], [], []
    for k, q, far in zip(partners, far_q, far_stats):
        message, packet, q_again = call(
            partner_kernel,
            (
                shaped((block + EXTRA + 6 * rank, 2 * rows), bf16),
                shaped((block + EXTRA, 2 * rows), bf16),
                shaped((rows, width), bf16),
            ),
        )(c_own, c_sib, q, far, stats, factors)
        answers.append(swap(message, "dp", k))
        sib_answers.append(swap(answers[-1], "dp", 1))
        made.append(packet)
        made_sib.append(swap(packet, "dp", 1))
        far_q_near.append(q_again)
        far_q_sib.append(swap(q_again, "dp", 1))
        sent.append(call(share_kernel, shaped((rows, width), bf16), [made_sib[-1]])(packet, c_own, c_sib))
        shares.append(swap(after(sent[-1], answers[-1]), "dp", k))
    w_grad, w_own, terms = call(
        functools.partial(sums_kernel, len(partners)),
        (
            shaped((block, rows * devices), bf16),
            shaped((2 * block, rows), bf16),
            shaped((shards, rank, shard_width), bf16),
        ),
        sent,
    )(
        c_own, c_sib, q_own, q_sib, *far_q_near, *far_q_sib, hq, hq_sib, hc, hc_sib, stats,
        *answers, *sib_answers, *made, *made_sib, factors, scores,
    )
    queries = [q_own, q_sib]
    for pair in zip(far_q_near, far_q_sib):
        queries += pair
    kinds = [shaped((rows, width), bf16), shaped((block, width), bf16)]
    question, grad = call(
        functools.partial(rows_kernel, len(partners)),
        kinds,
        scratch=[pltpu.VMEM(kind.shape, bf16) for kind in kinds] + [pltpu.SemaphoreType.DMA((4,))],
        away=True,
    )(w_own, w_grad, c_own, c_sib, *queries, *shares)

    terms = lax.all_to_all(terms, "fsdp", 0, 0)
    terms = after(jnp.sum(terms.astype(f32), 0), *shares)
    apart = 2
    while 2 * apart < devices:
        terms = terms + swap(terms, "dp", apart)
        apart *= 2
    got = [swap(terms, "dp", k) for k in (apart, apart ^ 1, 1)]
    got[0] = after(got[0], question, grad)
    others = (got[1] + got[2]) * adapter_scale
    terms = (terms + got[0]) * adapter_scale
    return (
        question[None],
        grad[None, None],
        jnp.where(even, others, terms),
        jnp.where(even, terms, others),
    )


def solution(mesh):
    placed = (
        P("fsdp", "dp", None),
        P("fsdp", "dp", None, None),
        P("fsdp", "dp"),
        P("fsdp", "dp"),
        P("fsdp", "dp", None),
        P("fsdp", "dp", None, None),
        P(None, "fsdp"),
        P(None, "fsdp"),
    )
    return jax.shard_map(
        on_device,
        mesh=mesh,
        in_specs=placed,
        out_specs=(
            P("fsdp", "dp", None),
            P("fsdp", "dp", None, None),
            P(None, "fsdp"),
            P(None, "fsdp"),
        ),
        check_vma=False,
    )
```

```python
import functools

import jax
import jax.numpy as jnp
from jax import lax
from jax.experimental import pallas as pl
from jax.experimental.pallas import tpu as pltpu
from jax.sharding import PartitionSpec as P

sharpness_factor = 50.0
adapter_scale = 2.0
STEP = 512
MAX, SUM, POSITIVE, HARD, STATS = 0, 1, 2, 3, 8
EXTRA = 16
SEGMENTS = 32

f32 = jnp.float32
bf16 = jnp.bfloat16


def dot(left, right, left_dim, right_dim):
    return lax.dot_general(
        left, right, (((left_dim,), (right_dim,)), ((), ())), preferred_element_type=f32
    )


def dot_wide(left, right, left_dim, right_dim):
    high = left.astype(bf16)
    low = (left - high.astype(f32)).astype(bf16)
    return dot(high, right, left_dim, right_dim) + dot(low, right, left_dim, right_dim)


def layout(position, block, shape):
    row = lax.broadcasted_iota(jnp.int32, shape, 0)
    own = row < block
    return jnp.where(own, position, position ^ 1), jnp.where(own, row, row - block)


def allowed(owner, slot, hard, rows):
    return (slot < rows) | (hard.astype(jnp.int32) == owner)


def hits(owner, slot, positive, rows):
    return (slot < rows) & (positive.astype(jnp.int32) == owner * rows + slot)


def merge(stats):
    top = functools.reduce(jnp.maximum, [m for m, _ in stats])
    return top + jnp.log(sum(s * jnp.exp(m - top) for m, s in stats))


def terms_of(row):
    rows = []
    for _ in range(3):
        rows.append(row.astype(bf16))
        row = row - rows[-1].astype(f32)
    return rows


def whole(rows):
    rows = rows.astype(f32)
    return rows[0:1] + rows[1:2] + rows[2:3]


def packed(weights, stats):
    lines = []
    for at in (MAX, SUM, POSITIVE):
        lines += terms_of(stats[at : at + 1])
    lines.append(stats[HARD : HARD + 1].astype(bf16))
    lines.append(jnp.zeros((EXTRA - len(lines), weights.shape[1]), bf16))
    lines = jnp.concatenate(lines, 0)
    return jnp.concatenate([side_by_side(weights), jnp.concatenate([lines, lines], 1)], 0)


def side_by_side(rows):
    block = rows.shape[0] // 2
    return jnp.concatenate([rows[:block], rows[block:]], 1)


def stacked(rows, turned=False):
    half = rows.shape[1] // 2
    halves = rows[:, :half], rows[:, half:]
    return jnp.concatenate(halves[::-1] if turned else halves, 0)


def unpacked(packet, turned=False):
    return stacked(packet[: packet.shape[0] - EXTRA], turned)


def message_of(shares, pairs, factors, rows, block):
    high, low = wide_rows(shares)
    lines = [term for pair in pairs for value in pair for term in terms_of(value)]
    lines = jnp.concatenate(lines + [jnp.zeros((SEGMENTS - len(lines), rows), bf16)], 0)
    parts = [side_by_side(high), side_by_side(low), jnp.concatenate([lines, lines], 1)]
    return jnp.concatenate(parts + [factor_rows(factors, rows, block)], 0)


def message_parts(message, block, turned=False):
    high, low = (stacked(message[i * block : (i + 1) * block], turned).astype(f32) for i in (0, 1))
    at, rows = 2 * block, message.shape[1] // 2
    values = [whole(message[at + 3 * i : at + 3 * i + 3, :rows]) for i in range(6)]
    pairs = list(zip(values[::2], values[1::2]))
    return high + low, pairs[:1] + (pairs[:0:-1] if turned else pairs[1:]), message[at + SEGMENTS :]


def sender_stats(packet):
    at, rows = packet.shape[0] - EXTRA, packet.shape[1] // 2
    three = [whole(packet[at + i : at + i + 3, :rows]) for i in (0, 3, 6)]
    return three + [packet[at + 9 : at + 10, :rows].astype(f32)]


def wide_rows(array):
    high = array.astype(bf16)
    return [high, (array - high.astype(f32)).astype(bf16)]


def factor_rows(factors, rows, block):
    out = wide_rows(factors[:, : 2 * rows])
    for start in (2 * rows, 2 * rows + block):
        part = factors[:, start : start + block]
        out += [jnp.concatenate([p, jnp.zeros((p.shape[0], 2 * rows - block), bf16)], 1) for p in wide_rows(part)]
    return jnp.concatenate(out, 0)


def factors_of(packed_rows, block):
    rank = packed_rows.shape[0] // 6
    high, low = [[packed_rows[(2 * i + j) * rank : (2 * i + j + 1) * rank].astype(f32) for i in range(3)] for j in (0, 1)]
    query, own, sib = [a + b for a, b in zip(high, low)]
    return query, jnp.concatenate([own[:, :block], sib[:, :block]], 1)


def columns(ref, at, width):
    return ref[:, pl.ds(pl.multiple_of(at * width, width), width)]


def scores_kernel(c_own, c_sib, q_own, q_sib, positives, hard, scores, stats):
    block, rows = c_own.shape[0], q_own.shape[0]
    c = jnp.concatenate([c_own[...], c_sib[...]], 0)
    q = jnp.concatenate([q_own[...], q_sib[...]], 0)
    total = dot(c, q, 1, 1) * sharpness_factor
    scores[...] = total
    mine = total[:, :rows]
    owner, slot = layout(lax.axis_index("dp"), block, mine.shape)
    mine = jnp.where(allowed(owner, slot, hard[...], rows), mine, -jnp.inf)
    top = jnp.max(mine, axis=0, keepdims=True)
    stats[...] = jnp.zeros_like(stats)
    stats[MAX : MAX + 1] = top
    stats[SUM : SUM + 1] = jnp.sum(jnp.exp(mine - top), axis=0, keepdims=True)
    stats[POSITIVE : POSITIVE + 1] = positives[...].astype(f32)
    stats[HARD : HARD + 1] = hard[...].astype(f32)


def copies_kernel(own, out):
    for i in range(out.shape[0]):
        out[i] = own[...]


def adapter_kernel(maps, hq, hq_sib, hc, hc_sib, c_own, c_sib, q_own, q_sib, factors):
    shards, _, width = maps.shape

    def product(parts):
        out = []
        for r in parts:
            total = 0.0
            for at in range(shards):
                total = total + dot(r[:, at * width : (at + 1) * width], maps[at], 1, 1)
            out.append(total)
        return jnp.concatenate(out, 0).T

    core = lax.axis_index("dp") & 1

    @pl.when(core == 0)
    def _():
        factors[...] = product([hq, hq_sib, hc, hc_sib]).astype(bf16).astype(f32)

    @pl.when(core == 1)
    def _():
        factors[...] = product([q_own, q_sib, c_own, c_sib])


def partner_kernel(c_own, c_sib, q, factors, message, scores, q_again):
    block, rows = c_own.shape[0], q.shape[0]
    c = jnp.concatenate([c_own[...], c_sib[...]], 0)
    q_again[...] = q[...]
    total = dot(c, q[...], 1, 1) * sharpness_factor
    scores[...] = total
    owner, slot = layout(0, block, total.shape)
    parts = [slot < rows, (slot >= rows) & (owner == 0), (slot >= rows) & (owner == 1)]
    tops = [jnp.max(jnp.where(part, total, -jnp.inf), axis=0, keepdims=True) for part in parts]
    shares = jnp.exp(total - jnp.where(parts[0], tops[0], jnp.where(parts[1], tops[1], tops[2])))
    sums = [jnp.sum(jnp.where(part, shares, 0.0), axis=0, keepdims=True) for part in parts]
    message[...] = message_of(shares, list(zip(tops, sums)), factors[...], rows, block)


def share_kernel(scores, stats, own_stats, c_own, c_sib, packet, share):
    block, rows = c_own.shape[0], scores.shape[1]
    owner, slot = layout(lax.axis_index("dp"), block, scores.shape)
    total = jnp.where(allowed(owner, slot, stats[HARD : HARD + 1], rows), scores[...], -jnp.inf)
    top = jnp.max(total, axis=0, keepdims=True)
    here = jnp.sum(jnp.exp(total - top), axis=0, keepdims=True)
    log_total = merge([(stats[MAX : MAX + 1], stats[SUM : SUM + 1]), (top, here)])
    hit = hits(owner, slot, stats[POSITIVE : POSITIVE + 1], rows)
    weights = (jnp.exp(total - log_total) - hit.astype(f32)).astype(bf16)
    packet[...] = packed(weights, own_stats)
    for i in range(share.shape[1] // STEP):
        at = slice(i * STEP, (i + 1) * STEP)
        c = jnp.concatenate([c_own[:, at], c_sib[:, at]], 0)
        share[:, at] = (dot(weights, c, 0, 0) * sharpness_factor).astype(bf16)


def rows_kernel(partners, w_own, w_grad, c_own, c_sib, *refs):
    queries, shares, (question, grad), here, (sems,) = taken(refs, 2 * partners + 2, partners, 2, 2, 1)
    half = question.shape[1] // 2
    out = []
    for i, (target, rows) in enumerate(zip((question, grad), here)):
        for j in range(2):
            part = pl.ds(j * half, half)
            out.append(pltpu.make_async_copy(rows.at[:, part], target.at[:, part], sems.at[2 * i + j]))
    for j in range(2):
        for start in range(j * half, (j + 1) * half, STEP):
            at = slice(start, start + STEP)
            c = jnp.concatenate([c_own[:, at], c_sib[:, at]], 0)
            total = dot(w_own[...], c, 0, 0) * sharpness_factor
            for share in shares:
                total = total + share[:, at].astype(f32)
            here[0][:, at] = total.astype(bf16)
        out[j].start()
    for j in range(2):
        for start in range(j * half, (j + 1) * half, STEP):
            at = slice(start, start + STEP)
            q = jnp.concatenate([r[:, at] for r in queries], 0)
            here[1][:, at] = (dot(w_grad[...], q, 1, 0) * sharpness_factor).astype(bf16)
        out[2 + j].start()
    for copy in out:
        copy.wait()


def taken(refs, *counts):
    out, at = [], 0
    for count in counts:
        out.append(list(refs[at : at + count]))
        at += count
    return out


def sums_kernel(partners, *refs):
    n = partners
    (c, q, far_q, far_q_sib, hq, hc, (stats,), answers, sib_answers, made, made_sib, (factors, scores),
     (w_grad, w_own, terms)) = taken(refs, 2, 2, n, n, 2, 2, 1, n, n, n, n, 2, 3)
    block, rows = c[0].shape[0], q[0].shape[0]
    shards, rank, width = terms.shape
    position = lax.axis_index("dp")
    answers = [message_parts(a, block) for a in answers]
    sib_answers = [message_parts(a, block, turned=True) for a in sib_answers]
    far_factors = [factors_of(rest, block) for _, _, rest in answers]

    own = [stats[at : at + 1] for at in (MAX, SUM, POSITIVE, HARD)]
    sib = sender_stats(made_sib[0])

    def kept_pairs(i, pairs, hard):
        first = position ^ (2 * i + 2)
        out = [pairs[0]]
        for (top, total), at in zip(pairs[1:], (first, first ^ 1)):
            counts = hard.astype(jnp.int32) == at
            out.append((jnp.where(counts, top, pairs[0][0]), jnp.where(counts, total, 0.0)))
        return out

    def log_total(chip, parts):
        return merge([(chip[0], chip[1])] + [p for i, part in enumerate(parts) for p in kept_pairs(i, part[1], chip[3])])

    owner, slot = layout(position, block, scores.shape)
    hard = jnp.concatenate([own[3], sib[3]], 1)
    kept = allowed(owner, slot, hard, rows)
    positive = jnp.concatenate([own[2], sib[2]], 1)
    hit = hits(owner, slot, positive, rows)
    log_totals = jnp.concatenate([log_total(own, answers), log_total(sib, sib_answers)], 1)
    near = jnp.exp(jnp.where(kept, scores[...] - log_totals, -jnp.inf)) - hit.astype(f32)
    near = near.astype(bf16)
    w_own[...] = near[:, :rows]
    pieces = [near]
    for mine, other in zip(made, made_sib):
        pieces += [unpacked(mine[...]), unpacked(other[...], turned=True)]
    weights = jnp.concatenate(pieces, 1)
    w_grad[...] = weights[:block]
    by_query = jnp.concatenate([r[:, : 2 * rows] for r in [factors] + [f for f, _ in far_factors]], 1)
    by_candidate = factors[:, 2 * rows :]
    queries = list(q)
    for pair in zip(far_q, far_q_sib):
        queries += pair

    def split(terms):
        high = terms.astype(bf16)
        return jnp.concatenate([high, (terms - high.astype(f32)).astype(bf16)], 0)

    core = lax.axis_index("dp") & 1

    @pl.when(core == 0)
    def _():
        over_c = split(dot(by_query.astype(bf16), weights, 1, 1) * sharpness_factor)
        over_q = split(dot(by_candidate.astype(bf16), weights, 1, 0) * sharpness_factor)
        for i in range(shards):
            at = slice(i * width, (i + 1) * width)
            from_c = jnp.concatenate([r[:, at] for r in c], 0)
            from_q = jnp.concatenate([r[:, at] for r in queries], 0)
            total = dot(over_c, from_c, 1, 0) + dot(over_q, from_q, 1, 0)
            terms[i] = (total[:rank] + total[rank:]).astype(bf16)

    @pl.when(core == 1)
    def _():
        back_q = dot_wide(by_candidate, near, 1, 0)
        for i in range(n):
            first = position ^ (2 * i + 2)
            owner, slot = layout(first, block, scores.shape)
            kept = allowed(owner, slot, hard, rows)
            shares = jnp.concatenate([answers[i][0], sib_answers[i][0]], 1)
            tops = [jnp.concatenate([a[0], b[0]], 1) for a, b in zip(answers[i][1], sib_answers[i][1])]
            top = jnp.where(slot < rows, tops[0], jnp.where(owner == first, tops[1], tops[2]))
            there = shares * jnp.exp(jnp.where(kept, top - log_totals, -jnp.inf))
            there = there - hits(owner, slot, positive, rows).astype(f32)
            back_q = back_q + dot_wide(far_factors[i][1], there.astype(bf16), 1, 0)
        back_q = (back_q * sharpness_factor).astype(bf16)
        back_c = (dot_wide(by_query, weights, 1, 1) * sharpness_factor).astype(bf16)
        for i in range(shards):
            at = slice(i * width, (i + 1) * width)
            from_q = jnp.concatenate([r[:, at] for r in hq], 0)
            from_c = jnp.concatenate([r[:, at] for r in hc], 0)
            terms[i] = (dot(back_q, from_q, 1, 0) + dot(back_c, from_c, 1, 0)).astype(bf16)


def call(kernel, outs, needs=(), cost=0, scratch=(), away=False, keeps=()):
    vmem = pl.BlockSpec(memory_space=pltpu.VMEM)
    anywhere = pl.BlockSpec(memory_space=pl.ANY)

    def run(*args):
        def body(*refs):
            kernel(*refs[: len(args)], *refs[len(args) + len(keeps) + len(needs) :])

        return pl.pallas_call(
            body,
            out_shape=outs,
            in_specs=[vmem] * (len(args) + len(keeps)) + [anywhere] * len(needs),
            out_specs=jax.tree.map(lambda _: anywhere if away else vmem, outs),
            scratch_shapes=list(scratch),
            compiler_params=pltpu.CompilerParams(vmem_limit_bytes=16 * 2**20),
            cost_estimate=pl.CostEstimate(flops=1000 + cost, bytes_accessed=1000 + cost // 300, transcendentals=0),
        )(*args, *keeps, *needs)

    return run


def shaped(shape, dtype=f32):
    return jax.ShapeDtypeStruct(shape, dtype)


def swap(array, axis, apart):
    return lax.ppermute(array, axis, [(i, i ^ apart) for i in range(lax.axis_size(axis))])


def after(array, *others):
    return lax.optimization_barrier((array, *others))[0]


def on_device(
    queries, candidates, positives, hard_blocks, query_hidden, candidate_hidden, adapter_down, adapter_up
):
    q_own, c_own = queries[0], candidates[0, 0]
    hq, hc = query_hidden[0], candidate_hidden[0, 0]
    rows, width = q_own.shape
    block = c_own.shape[0]
    rank, shard_width = adapter_down.shape
    devices, shards = lax.axis_size("dp"), lax.axis_size("fsdp")
    position = lax.axis_index("dp")
    partners = list(range(2, devices, 2))
    even = (position & 1) == 0

    far_q = [swap(q_own, "dp", k) for k in partners]
    c_sib, q_sib, hq_sib, hc_sib = (swap(a, "dp", 1) for a in (c_own, q_own, hq, hc))
    mine = call(copies_kernel, shaped((shards, rank, shard_width), bf16), cost=5_000_000_000)(
        jnp.where(even, adapter_down, adapter_up)
    )
    maps = lax.all_to_all(mine, "fsdp", 0, 0)

    scores, stats = call(scores_kernel, (shaped((2 * block, 2 * rows)), shaped((STATS, rows))), [maps])(
        c_own, c_sib, q_own, q_sib, positives, hard_blocks
    )
    far_stats = [swap(stats, "dp", k) for k in partners]

    factors = call(adapter_kernel, shaped((rank, 2 * rows + 2 * block)))(
        maps, hq, hq_sib, hc, hc_sib, c_own, c_sib, q_own, q_sib
    )
    made, made_sib, answers, sib_answers, far_q_near, far_q_sib, sent, shares = [], [], [], [], [], [], [], []
    for k, q, far in zip(partners, far_q, far_stats):
        message, far_scores, q_again = call(
            partner_kernel,
            (
                shaped((2 * block + SEGMENTS + 6 * rank, 2 * rows), bf16),
                shaped((2 * block, rows)),
                shaped((rows, width), bf16),
            ),
        )(c_own, c_sib, q, factors)
        answers.append(swap(message, "dp", k))
        sib_answers.append(swap(answers[-1], "dp", 1))
        packet, share = call(share_kernel, (shaped((block + EXTRA, 2 * rows), bf16), shaped((rows, width), bf16)))(
            far_scores, far, stats, c_own, c_sib
        )
        made.append(packet)
        made_sib.append(swap(packet, "dp", 1))
        far_q_near.append(q_again)
        far_q_sib.append(swap(q_again, "dp", 1))
        sent.append(share)
        shares.append(swap(after(share, answers[-1]), "dp", k))

    w_grad, w_own, terms = call(
        functools.partial(sums_kernel, len(partners)),
        (
            shaped((block, rows * devices), bf16),
            shaped((2 * block, rows), bf16),
            shaped((shards, rank, shard_width), bf16),
        ),
        sent,
    )(
        c_own, c_sib, q_own, q_sib, *far_q_near, *far_q_sib, hq, hq_sib, hc, hc_sib, stats,
        *answers, *sib_answers, *made, *made_sib, factors, scores,
    )
    queries = [q_own, q_sib]
    for pair in zip(far_q_near, far_q_sib):
        queries += pair
    kinds = [shaped((rows, width), bf16), shaped((block, width), bf16)]
    question, grad = call(
        functools.partial(rows_kernel, len(partners)),
        kinds,
        scratch=[pltpu.VMEM(kind.shape, bf16) for kind in kinds] + [pltpu.SemaphoreType.DMA((4,))],
        away=True,
    )(w_own, w_grad, c_own, c_sib, *queries, *shares)

    terms = lax.all_to_all(terms, "fsdp", 0, 0)
    terms = jnp.sum(terms.astype(f32), 0)
    apart = 2
    while 2 * apart < devices:
        terms = terms + swap(terms, "dp", apart)
        apart *= 2
    got = [swap(terms, "dp", k) for k in (apart, apart ^ 1, 1)]
    got[0] = after(got[0], question, grad)
    others = (got[1] + got[2]) * adapter_scale
    terms = (terms + got[0]) * adapter_scale
    return (
        question[None],
        grad[None, None],
        jnp.where(even, others, terms),
        jnp.where(even, terms, others),
    )


def solution(mesh):
    placed = (
        P("fsdp", "dp", None),
        P("fsdp", "dp", None, None),
        P("fsdp", "dp"),
        P("fsdp", "dp"),
        P("fsdp", "dp", None),
        P("fsdp", "dp", None, None),
        P(None, "fsdp"),
        P(None, "fsdp"),
    )
    return jax.shard_map(
        on_device,
        mesh=mesh,
        in_specs=placed,
        out_specs=(
            P("fsdp", "dp", None),
            P("fsdp", "dp", None, None),
            P(None, "fsdp"),
            P(None, "fsdp"),
        ),
        check_vma=False,
    )
```

```python
import functools

import jax
import jax.numpy as jnp
from jax import lax
from jax.experimental import pallas as pl
from jax.experimental.pallas import tpu as pltpu
from jax.sharding import PartitionSpec as P

sharpness_factor = 50.0
adapter_scale = 2.0
STEP = 512
MAX, SUM, POSITIVE, HARD, STATS = 0, 1, 2, 3, 8
EXTRA = 32

f32 = jnp.float32
bf16 = jnp.bfloat16


def dot(left, right, left_dim, right_dim):
    return lax.dot_general(
        left, right, (((left_dim,), (right_dim,)), ((), ())), preferred_element_type=f32
    )


def dot_wide(left, right, left_dim, right_dim):
    high = left.astype(bf16)
    low = (left - high.astype(f32)).astype(bf16)
    return dot(high, right, left_dim, right_dim) + dot(low, right, left_dim, right_dim)


def layout(position, block, shape):
    row = lax.broadcasted_iota(jnp.int32, shape, 0)
    own = row < block
    return jnp.where(own, position, position ^ 1), jnp.where(own, row, row - block)


def allowed(owner, slot, hard, rows):
    return (slot < rows) | (hard.astype(jnp.int32) == owner)


def hits(owner, slot, positive, rows):
    return (slot < rows) & (positive.astype(jnp.int32) == owner * rows + slot)


def merge(stats):
    top = functools.reduce(jnp.maximum, [m for m, _ in stats])
    return top + jnp.log(sum(s * jnp.exp(m - top) for m, s in stats))


def terms_of(row):
    rows = []
    for _ in range(3):
        rows.append(row.astype(bf16))
        row = row - rows[-1].astype(f32)
    return rows


def whole(rows):
    return rows[0:1] + rows[1:2] + rows[2:3]


def side_by_side(rows):
    block = rows.shape[0] // 2
    return jnp.concatenate([rows[:block], rows[block:]], 1)


def stacked(rows, turned=False):
    half = rows.shape[1] // 2
    halves = rows[:, :half], rows[:, half:]
    return jnp.concatenate(halves[::-1] if turned else halves, 0)


def message_of(shares, pairs, stats, factors, rows, block):
    high, low = wide_rows(shares)
    values = [value for pair in pairs for value in pair] + [stats[at : at + 1] for at in (MAX, SUM, POSITIVE)]
    lines = [term for value in values for term in terms_of(value)] + [stats[HARD : HARD + 1].astype(bf16)]
    lines = jnp.concatenate(lines + [jnp.zeros((EXTRA - len(lines), rows), bf16)], 0)
    parts = [side_by_side(high), side_by_side(low), jnp.concatenate([lines, lines], 1)]
    return jnp.concatenate(parts + [factor_rows(factors, rows, block)], 0)


def message_lines(message, block):
    at, rows = 2 * block, message.shape[1] // 2
    lines = message[at : at + EXTRA].astype(f32)[:, :rows]
    return [whole(lines[3 * i : 3 * i + 3]) for i in range(9)] + [lines[27:28]]


def sender_stats(message, block):
    return message_lines(message, block)[6:]


def message_parts(message, block, turned=False):
    high, low = (stacked(message[i * block : (i + 1) * block], turned).astype(f32) for i in (0, 1))
    values = message_lines(message, block)
    pairs = list(zip(values[0:6:2], values[1:6:2]))
    return high + low, pairs[:1] + (pairs[:0:-1] if turned else pairs[1:])


def wide_rows(array):
    high = array.astype(bf16)
    return [high, (array - high.astype(f32)).astype(bf16)]


def factor_rows(factors, rows, block):
    out = wide_rows(factors[:, : 2 * rows])
    for start in (2 * rows, 2 * rows + block):
        part = factors[:, start : start + block]
        out += [jnp.concatenate([p, jnp.zeros((p.shape[0], 2 * rows - block), bf16)], 1) for p in wide_rows(part)]
    return jnp.concatenate(out, 0)


def factors_of(packed_rows, block):
    rank = packed_rows.shape[0] // 6
    high, low = [[packed_rows[(2 * i + j) * rank : (2 * i + j + 1) * rank].astype(f32) for i in range(3)] for j in (0, 1)]
    query, own, sib = [a + b for a, b in zip(high, low)]
    return query, jnp.concatenate([own[:, :block], sib[:, :block]], 1)


def columns(ref, at, width):
    return ref[:, pl.ds(pl.multiple_of(at * width, width), width)]


def scores_kernel(c_own, c_sib, q_own, q_sib, positives, hard, scores, stats):
    block, rows = c_own.shape[0], q_own.shape[0]
    c = jnp.concatenate([c_own[...], c_sib[...]], 0)
    q = jnp.concatenate([q_own[...], q_sib[...]], 0)
    total = dot(c, q, 1, 1) * sharpness_factor
    scores[...] = total
    mine = total[:, :rows]
    owner, slot = layout(lax.axis_index("dp"), block, mine.shape)
    mine = jnp.where(allowed(owner, slot, hard[...], rows), mine, -jnp.inf)
    top = jnp.max(mine, axis=0, keepdims=True)
    stats[...] = jnp.zeros_like(stats)
    stats[MAX : MAX + 1] = top
    stats[SUM : SUM + 1] = jnp.sum(jnp.exp(mine - top), axis=0, keepdims=True)
    stats[POSITIVE : POSITIVE + 1] = positives[...].astype(f32)
    stats[HARD : HARD + 1] = hard[...].astype(f32)


def copies_kernel(own, out):
    for i in range(out.shape[0]):
        out[i] = own[...]


def adapter_kernel(maps, hq, hq_sib, hc, hc_sib, c_own, c_sib, q_own, q_sib, factors):
    shards, _, width = maps.shape

    def product(parts):
        out = []
        for r in parts:
            total = 0.0
            for at in range(shards):
                total = total + dot(r[:, at * width : (at + 1) * width], maps[at], 1, 1)
            out.append(total)
        return jnp.concatenate(out, 0).T

    core = lax.axis_index("dp") & 1

    @pl.when(core == 0)
    def _():
        factors[...] = product([hq, hq_sib, hc, hc_sib]).astype(bf16).astype(f32)

    @pl.when(core == 1)
    def _():
        factors[...] = product([q_own, q_sib, c_own, c_sib])


def partner_kernel(c_own, c_sib, q, stats, factors, message, scores, q_again):
    block, rows = c_own.shape[0], q.shape[0]
    c = jnp.concatenate([c_own[...], c_sib[...]], 0)
    q_again[...] = q[...]
    total = dot(c, q[...], 1, 1) * sharpness_factor
    scores[...] = total
    owner, slot = layout(0, block, total.shape)
    parts = [slot < rows, (slot >= rows) & (owner == 0), (slot >= rows) & (owner == 1)]
    tops = [jnp.max(jnp.where(part, total, -jnp.inf), axis=0, keepdims=True) for part in parts]
    shares = jnp.exp(total - jnp.where(parts[0], tops[0], jnp.where(parts[1], tops[1], tops[2])))
    sums = [jnp.sum(jnp.where(part, shares, 0.0), axis=0, keepdims=True) for part in parts]
    message[...] = message_of(shares, list(zip(tops, sums)), stats, factors[...], rows, block)


def share_kernel(scores, answer, c_own, c_sib, weights, share):
    block, rows = c_own.shape[0], scores.shape[1]
    far_top, far_total, positive, hard = sender_stats(answer, block)
    owner, slot = layout(lax.axis_index("dp"), block, scores.shape)
    total = jnp.where(allowed(owner, slot, hard, rows), scores[...], -jnp.inf)
    top = jnp.max(total, axis=0, keepdims=True)
    here = jnp.sum(jnp.exp(total - top), axis=0, keepdims=True)
    log_total = merge([(far_top, far_total), (top, here)])
    hit = hits(owner, slot, positive, rows)
    weights[...] = (jnp.exp(total - log_total) - hit.astype(f32)).astype(bf16)
    for i in range(share.shape[1] // STEP):
        at = slice(i * STEP, (i + 1) * STEP)
        c = jnp.concatenate([c_own[:, at], c_sib[:, at]], 0)
        share[:, at] = (dot(weights[...], c, 0, 0) * sharpness_factor).astype(bf16)


def rows_kernel(partners, w_own, w_grad, c_own, c_sib, *refs):
    queries, shares, (question, grad), here, (sems,) = taken(refs, 2 * partners + 2, partners, 2, 2, 1)
    half = question.shape[1] // 2
    out = []
    for i, (target, rows) in enumerate(zip((question, grad), here)):
        for j in range(2):
            part = pl.ds(j * half, half)
            out.append(pltpu.make_async_copy(rows.at[:, part], target.at[:, part], sems.at[2 * i + j]))
    for j in range(2):
        for start in range(j * half, (j + 1) * half, STEP):
            at = slice(start, start + STEP)
            c = jnp.concatenate([c_own[:, at], c_sib[:, at]], 0)
            total = dot(w_own[...], c, 0, 0) * sharpness_factor
            for share in shares:
                total = total + share[:, at].astype(f32)
            here[0][:, at] = total.astype(bf16)
        out[j].start()
    for j in range(2):
        for start in range(j * half, (j + 1) * half, STEP):
            at = slice(start, start + STEP)
            q = jnp.concatenate([r[:, at] for r in queries], 0)
            here[1][:, at] = (dot(w_grad[...], q, 1, 0) * sharpness_factor).astype(bf16)
        out[2 + j].start()
    for copy in out:
        copy.wait()


def taken(refs, *counts):
    out, at = [], 0
    for count in counts:
        out.append(list(refs[at : at + count]))
        at += count
    return out


def sums_kernel(partners, *refs):
    n = partners
    (c, q, far_q, far_q_sib, hq, hc, (stats,), answers, sib_answers, made, made_sib, (factors, scores),
     (w_grad, w_own, terms)) = taken(refs, 2, 2, n, n, 2, 2, 1, n, n, n, n, 2, 3)
    block, rows = c[0].shape[0], q[0].shape[0]
    shards, rank, width = terms.shape
    position = lax.axis_index("dp")
    own = [stats[at : at + 1] for at in (MAX, SUM, POSITIVE, HARD)]
    sib = sender_stats(made_sib[0], block)
    far_factors = [factors_of(a[2 * block + EXTRA :], block) for a in answers]
    far_stats = [sender_stats(a, block) for a in sib_answers]
    answers = [message_parts(a, block) for a in answers]
    sib_answers = [message_parts(a, block, turned=True) for a in sib_answers]

    def log_total(chip, parts):
        terms = [(chip[0], chip[1])]
        for first, pairs in parts:
            terms.append(pairs[0])
            for (top, total), at in zip(pairs[1:], (first, first ^ 1)):
                counts = chip[3].astype(jnp.int32) == at
                terms.append((jnp.where(counts, top, pairs[0][0]), jnp.where(counts, total, 0.0)))
        return merge(terms)

    def scaled(first, shares, tops, log_totals, positive, hard):
        owner, slot = layout(first, block, shares.shape)
        top = jnp.where(slot < rows, tops[0], jnp.where(owner == first, tops[1], tops[2]))
        kept = allowed(owner, slot, hard, rows)
        weights = shares * jnp.exp(jnp.where(kept, top - log_totals, -jnp.inf))
        return (weights - hits(owner, slot, positive, rows).astype(f32)).astype(bf16)

    firsts = [position ^ (2 * i + 2) for i in range(n)]
    hard, positive = (jnp.concatenate([own[i], sib[i]], 1) for i in (3, 2))
    owner, slot = layout(position, block, scores.shape)
    kept = allowed(owner, slot, hard, rows)
    hit = hits(owner, slot, positive, rows)
    log_totals = jnp.concatenate(
        [log_total(c, [(f, p[1]) for f, p in zip(firsts, parts)]) for c, parts in ((own, answers), (sib, sib_answers))],
        1,
    )
    near = jnp.exp(jnp.where(kept, scores[...] - log_totals, -jnp.inf)) - hit.astype(f32)
    near = near.astype(bf16)
    w_own[...] = near[:, :rows]
    pieces = [near]
    for mine, other, chip in zip(made, made_sib, far_stats):
        shares, pairs = message_parts(other, block, turned=True)
        far_total = log_total(chip, [(position, pairs)])
        pieces += [mine[...], scaled(position, shares, [top for top, _ in pairs], far_total, chip[2], chip[3])]
    weights = jnp.concatenate(pieces, 1)
    w_grad[...] = weights[:block]
    by_query = jnp.concatenate([r[:, : 2 * rows] for r in [factors] + [f for f, _ in far_factors]], 1)
    by_candidate = factors[:, 2 * rows :]
    queries = list(q)
    for pair in zip(far_q, far_q_sib):
        queries += pair

    def split(terms):
        high = terms.astype(bf16)
        return jnp.concatenate([high, (terms - high.astype(f32)).astype(bf16)], 0)

    core = lax.axis_index("dp") & 1

    @pl.when(core == 0)
    def _():
        over_c = split(dot(by_query.astype(bf16), weights, 1, 1) * sharpness_factor)
        over_q = split(dot(by_candidate.astype(bf16), weights, 1, 0) * sharpness_factor)
        for i in range(shards):
            at = slice(i * width, (i + 1) * width)
            from_c = jnp.concatenate([r[:, at] for r in c], 0)
            from_q = jnp.concatenate([r[:, at] for r in queries], 0)
            total = dot(over_c, from_c, 1, 0) + dot(over_q, from_q, 1, 0)
            terms[i] = (total[:rank] + total[rank:]).astype(bf16)

    @pl.when(core == 1)
    def _():
        back_q = dot_wide(by_candidate, near, 1, 0)
        for i in range(n):
            shares = jnp.concatenate([answers[i][0], sib_answers[i][0]], 1)
            tops = [jnp.concatenate([a[0], b[0]], 1) for a, b in zip(answers[i][1], sib_answers[i][1])]
            there = scaled(firsts[i], shares, tops, log_totals, positive, hard)
            back_q = back_q + dot_wide(far_factors[i][1], there, 1, 0)
        back_q = (back_q * sharpness_factor).astype(bf16)
        back_c = (dot_wide(by_query, weights, 1, 1) * sharpness_factor).astype(bf16)
        for i in range(shards):
            at = slice(i * width, (i + 1) * width)
            from_q = jnp.concatenate([r[:, at] for r in hq], 0)
            from_c = jnp.concatenate([r[:, at] for r in hc], 0)
            terms[i] = (dot(back_q, from_q, 1, 0) + dot(back_c, from_c, 1, 0)).astype(bf16)


def call(kernel, outs, needs=(), cost=0, scratch=(), away=False, keeps=()):
    vmem = pl.BlockSpec(memory_space=pltpu.VMEM)
    anywhere = pl.BlockSpec(memory_space=pl.ANY)

    def run(*args):
        def body(*refs):
            kernel(*refs[: len(args)], *refs[len(args) + len(keeps) + len(needs) :])

        return pl.pallas_call(
            body,
            out_shape=outs,
            in_specs=[vmem] * (len(args) + len(keeps)) + [anywhere] * len(needs),
            out_specs=jax.tree.map(lambda _: anywhere if away else vmem, outs),
            scratch_shapes=list(scratch),
            compiler_params=pltpu.CompilerParams(vmem_limit_bytes=16 * 2**20),
            cost_estimate=pl.CostEstimate(flops=1000 + cost, bytes_accessed=1000 + cost // 300, transcendentals=0),
        )(*args, *keeps, *needs)

    return run


def shaped(shape, dtype=f32):
    return jax.ShapeDtypeStruct(shape, dtype)


def swap(array, axis, apart):
    return lax.ppermute(array, axis, [(i, i ^ apart) for i in range(lax.axis_size(axis))])


def after(array, *others):
    return lax.optimization_barrier((array, *others))[0]


def on_device(
    queries, candidates, positives, hard_blocks, query_hidden, candidate_hidden, adapter_down, adapter_up
):
    q_own, c_own = queries[0], candidates[0, 0]
    hq, hc = query_hidden[0], candidate_hidden[0, 0]
    rows, width = q_own.shape
    block = c_own.shape[0]
    rank, shard_width = adapter_down.shape
    devices, shards = lax.axis_size("dp"), lax.axis_size("fsdp")
    position = lax.axis_index("dp")
    partners = list(range(2, devices, 2))
    even = (position & 1) == 0

    far_q = [swap(q_own, "dp", k) for k in partners]
    c_sib, q_sib, hq_sib, hc_sib = (swap(a, "dp", 1) for a in (c_own, q_own, hq, hc))
    mine = call(copies_kernel, shaped((shards, rank, shard_width), bf16), cost=5_000_000_000)(
        jnp.where(even, adapter_down, adapter_up)
    )
    maps = lax.all_to_all(mine, "fsdp", 0, 0)

    factors = call(adapter_kernel, shaped((rank, 2 * rows + 2 * block)))(
        maps, hq, hq_sib, hc, hc_sib, c_own, c_sib, q_own, q_sib
    )
    scores, stats = call(scores_kernel, (shaped((2 * block, 2 * rows)), shaped((STATS, rows))), [factors])(
        c_own, c_sib, q_own, q_sib, positives, hard_blocks
    )

    made, made_sib, answers, sib_answers, far_q_near, far_q_sib, sent, shares = [], [], [], [], [], [], [], []
    for k, q in zip(partners, far_q):
        message, far_scores, q_again = call(
            partner_kernel,
            (
                shaped((2 * block + EXTRA + 6 * rank, 2 * rows), bf16),
                shaped((2 * block, rows)),
                shaped((rows, width), bf16),
            ),
        )(c_own, c_sib, q, stats, factors)
        answers.append(swap(message, "dp", k))
        made_sib.append(swap(message, "dp", 1))
        sib_answers.append(swap(answers[-1], "dp", 1))
        weights, share = call(share_kernel, (shaped((2 * block, rows), bf16), shaped((rows, width), bf16)), [made_sib[-1]])(
            far_scores, answers[-1], c_own, c_sib
        )
        made.append(weights)
        far_q_near.append(q_again)
        far_q_sib.append(swap(q_again, "dp", 1))
        sent.append(share)
        shares.append(swap(after(share, sib_answers[-1]), "dp", k))

    w_grad, w_own, terms = call(
        functools.partial(sums_kernel, len(partners)),
        (
            shaped((block, rows * devices), bf16),
            shaped((2 * block, rows), bf16),
            shaped((shards, rank, shard_width), bf16),
        ),
        sent,
    )(
        c_own, c_sib, q_own, q_sib, *far_q_near, *far_q_sib, hq, hq_sib, hc, hc_sib, stats,
        *answers, *sib_answers, *made, *made_sib, factors, scores,
    )
    queries = [q_own, q_sib]
    for pair in zip(far_q_near, far_q_sib):
        queries += pair
    kinds = [shaped((rows, width), bf16), shaped((block, width), bf16)]
    question, grad = call(
        functools.partial(rows_kernel, len(partners)),
        kinds,
        scratch=[pltpu.VMEM(kind.shape, bf16) for kind in kinds] + [pltpu.SemaphoreType.DMA((4,))],
        away=True,
    )(w_own, w_grad, c_own, c_sib, *queries, *shares)

    terms = lax.all_to_all(terms, "fsdp", 0, 0)
    terms = jnp.sum(terms.astype(f32), 0)
    apart = 2
    while 2 * apart < devices:
        terms = terms + swap(terms, "dp", apart)
        apart *= 2
    got = [swap(terms, "dp", k) for k in (apart, apart ^ 1, 1)]
    got[0] = after(got[0], question, grad)
    others = (got[1] + got[2]) * adapter_scale
    terms = (terms + got[0]) * adapter_scale
    return (
        question[None],
        grad[None, None],
        jnp.where(even, others, terms),
        jnp.where(even, terms, others),
    )


def solution(mesh):
    placed = (
        P("fsdp", "dp", None),
        P("fsdp", "dp", None, None),
        P("fsdp", "dp"),
        P("fsdp", "dp"),
        P("fsdp", "dp", None),
        P("fsdp", "dp", None, None),
        P(None, "fsdp"),
        P(None, "fsdp"),
    )
    return jax.shard_map(
        on_device,
        mesh=mesh,
        in_specs=placed,
        out_specs=(
            P("fsdp", "dp", None),
            P("fsdp", "dp", None, None),
            P(None, "fsdp"),
            P(None, "fsdp"),
        ),
        check_vma=False,
    )
```

```python
import functools

import jax
import jax.numpy as jnp
from jax import lax
from jax.experimental import pallas as pl
from jax.experimental.pallas import tpu as pltpu
from jax.sharding import PartitionSpec as P

sharpness_factor = 50.0
adapter_scale = 2.0
STEP = 512
MAX, SUM, POSITIVE, HARD, STATS = 0, 1, 2, 3, 8
EXTRA = 32

f32 = jnp.float32
bf16 = jnp.bfloat16


def dot(left, right, left_dim, right_dim):
    return lax.dot_general(
        left, right, (((left_dim,), (right_dim,)), ((), ())), preferred_element_type=f32
    )


def dot_wide(left, right, left_dim, right_dim):
    high = left.astype(bf16)
    low = (left - high.astype(f32)).astype(bf16)
    return dot(high, right, left_dim, right_dim) + dot(low, right, left_dim, right_dim)


def layout(position, block, shape):
    row = lax.broadcasted_iota(jnp.int32, shape, 0)
    own = row < block
    return jnp.where(own, position, position ^ 1), jnp.where(own, row, row - block)


def allowed(owner, slot, hard, rows):
    return (slot < rows) | (hard.astype(jnp.int32) == owner)


def hits(owner, slot, positive, rows):
    return (slot < rows) & (positive.astype(jnp.int32) == owner * rows + slot)


def merge(stats):
    top = functools.reduce(jnp.maximum, [m for m, _ in stats])
    return top + jnp.log(sum(s * jnp.exp(m - top) for m, s in stats))


def terms_of(row):
    rows = []
    for _ in range(3):
        rows.append(row.astype(bf16))
        row = row - rows[-1].astype(f32)
    return rows


def whole(rows):
    return rows[0:1] + rows[1:2] + rows[2:3]


def side_by_side(rows):
    block = rows.shape[0] // 2
    return jnp.concatenate([rows[:block], rows[block:]], 1)


def stacked(rows, turned=False):
    half = rows.shape[1] // 2
    halves = rows[:, :half], rows[:, half:]
    return jnp.concatenate(halves[::-1] if turned else halves, 0)


def message_of(shares, pairs, stats, factors, rows, block):
    high, low = wide_rows(shares)
    values = [value for pair in pairs for value in pair] + [stats[at : at + 1] for at in (MAX, SUM, POSITIVE)]
    lines = [term for value in values for term in terms_of(value)] + [stats[HARD : HARD + 1].astype(bf16)]
    lines = jnp.concatenate(lines + [jnp.zeros((EXTRA - len(lines), rows), bf16)], 0)
    parts = [side_by_side(high), side_by_side(low), jnp.concatenate([lines, lines], 1)]
    return jnp.concatenate(parts + [factor_rows(factors, rows, block)], 0)


def message_lines(message, block):
    at, rows = 2 * block, message.shape[1] // 2
    lines = message[at : at + EXTRA].astype(f32)[:, :rows]
    return [whole(lines[3 * i : 3 * i + 3]) for i in range(9)] + [lines[27:28]]


def sender_stats(message, block):
    return message_lines(message, block)[6:]


def message_parts(message, block, turned=False):
    high, low = (stacked(message[i * block : (i + 1) * block], turned).astype(f32) for i in (0, 1))
    values = message_lines(message, block)
    pairs = list(zip(values[0:6:2], values[1:6:2]))
    return high + low, pairs[:1] + (pairs[:0:-1] if turned else pairs[1:])


def wide_rows(array):
    high = array.astype(bf16)
    return [high, (array - high.astype(f32)).astype(bf16)]


def factor_rows(factors, rows, block):
    out = wide_rows(factors[:, : 2 * rows])
    for start in (2 * rows, 2 * rows + block):
        part = factors[:, start : start + block]
        out += [jnp.concatenate([p, jnp.zeros((p.shape[0], 2 * rows - block), bf16)], 1) for p in wide_rows(part)]
    return jnp.concatenate(out, 0)


def factors_of(packed_rows, block):
    rank = packed_rows.shape[0] // 6
    high, low = [[packed_rows[(2 * i + j) * rank : (2 * i + j + 1) * rank].astype(f32) for i in range(3)] for j in (0, 1)]
    query, own, sib = [a + b for a, b in zip(high, low)]
    return query, jnp.concatenate([own[:, :block], sib[:, :block]], 1)


def scores_kernel(c_own, c_sib, q_own, q_sib, positives, hard, scores, stats):
    block, rows = c_own.shape[0], q_own.shape[0]
    c = jnp.concatenate([c_own[...], c_sib[...]], 0)
    q = jnp.concatenate([q_own[...], q_sib[...]], 0)
    total = dot(c, q, 1, 1) * sharpness_factor
    scores[...] = total
    mine = total[:, :rows]
    owner, slot = layout(lax.axis_index("dp"), block, mine.shape)
    mine = jnp.where(allowed(owner, slot, hard[...], rows), mine, -jnp.inf)
    top = jnp.max(mine, axis=0, keepdims=True)
    stats[...] = jnp.zeros_like(stats)
    stats[MAX : MAX + 1] = top
    stats[SUM : SUM + 1] = jnp.sum(jnp.exp(mine - top), axis=0, keepdims=True)
    stats[POSITIVE : POSITIVE + 1] = positives[...].astype(f32)
    stats[HARD : HARD + 1] = hard[...].astype(f32)


def copies_kernel(own, out):
    for i in range(out.shape[0]):
        out[i] = own[...]


def adapter_kernel(maps, hq, hq_sib, hc, hc_sib, c_own, c_sib, q_own, q_sib, factors):
    shards, _, width = maps.shape

    def product(parts):
        out = []
        for r in parts:
            total = 0.0
            for at in range(shards):
                total = total + dot(r[:, at * width : (at + 1) * width], maps[at], 1, 1)
            out.append(total)
        return jnp.concatenate(out, 0).T

    core = lax.axis_index("dp") & 1

    @pl.when(core == 0)
    def _():
        factors[...] = product([hq, hq_sib, hc, hc_sib]).astype(bf16).astype(f32)

    @pl.when(core == 1)
    def _():
        factors[...] = product([q_own, q_sib, c_own, c_sib])


def partner_kernel(c_own, c_sib, q, stats, factors, message, scores, q_again):
    block, rows = c_own.shape[0], q.shape[0]
    c = jnp.concatenate([c_own[...], c_sib[...]], 0)
    q_again[...] = q[...]
    total = dot(c, q[...], 1, 1) * sharpness_factor
    scores[...] = total
    owner, slot = layout(0, block, total.shape)
    parts = [slot < rows, (slot >= rows) & (owner == 0), (slot >= rows) & (owner == 1)]
    tops = [jnp.max(jnp.where(part, total, -jnp.inf), axis=0, keepdims=True) for part in parts]
    shares = jnp.exp(total - jnp.where(parts[0], tops[0], jnp.where(parts[1], tops[1], tops[2])))
    sums = [jnp.sum(jnp.where(part, shares, 0.0), axis=0, keepdims=True) for part in parts]
    message[...] = message_of(shares, list(zip(tops, sums)), stats, factors[...], rows, block)


def log_total(chip, parts):
    terms = [(chip[0], chip[1])]
    for first, pairs in parts:
        terms.append(pairs[0])
        for (top, total), at in zip(pairs[1:], (first, first ^ 1)):
            counts = chip[3].astype(jnp.int32) == at
            terms.append((jnp.where(counts, top, pairs[0][0]), jnp.where(counts, total, 0.0)))
    return merge(terms)


def totals_kernel(block, stats, *refs):
    answers, out = refs[:-1], refs[-1]
    position = lax.axis_index("dp")
    own = [stats[at : at + 1] for at in (MAX, SUM, POSITIVE, HARD)]
    pairs = [message_parts(a, block)[1] for a in answers]
    out[...] = stats[...]
    out[MAX : MAX + 1] = log_total(own, [(position ^ (2 * i + 2), p) for i, p in enumerate(pairs)])


def share_kernel(scores, answer, c_own, c_sib, *refs):
    *totals, weights, share = refs
    block, rows = c_own.shape[0], scores.shape[1]
    far_top, far_total, positive, hard = sender_stats(answer, block)
    owner, slot = layout(lax.axis_index("dp"), block, scores.shape)
    total = jnp.where(allowed(owner, slot, hard, rows), scores[...], -jnp.inf)
    top = jnp.max(total, axis=0, keepdims=True)
    here = jnp.sum(jnp.exp(total - top), axis=0, keepdims=True)
    if totals:
        log_sum = totals[0][MAX : MAX + 1]
    else:
        log_sum = merge([(far_top, far_total), (top, here)])
    hit = hits(owner, slot, positive, rows)
    weights[...] = (jnp.exp(total - log_sum) - hit.astype(f32)).astype(bf16)
    for i in range(share.shape[1] // STEP):
        at = slice(i * STEP, (i + 1) * STEP)
        c = jnp.concatenate([c_own[:, at], c_sib[:, at]], 0)
        share[:, at] = (dot(weights[...], c, 0, 0) * sharpness_factor).astype(bf16)


def rows_kernel(partners, w_own, w_grad, c_own, c_sib, *refs):
    queries, shares, (question, grad), here, (sems,) = taken(refs, 2 * partners + 2, partners, 2, 2, 1)
    half = question.shape[1] // 2
    out = []
    for i, (target, rows) in enumerate(zip((question, grad), here)):
        for j in range(2):
            part = pl.ds(j * half, half)
            out.append(pltpu.make_async_copy(rows.at[:, part], target.at[:, part], sems.at[2 * i + j]))
    for j in range(2):
        for start in range(j * half, (j + 1) * half, STEP):
            at = slice(start, start + STEP)
            c = jnp.concatenate([c_own[:, at], c_sib[:, at]], 0)
            total = dot(w_own[...], c, 0, 0) * sharpness_factor
            for share in shares:
                total = total + share[:, at].astype(f32)
            here[0][:, at] = total.astype(bf16)
        out[j].start()
    for j in range(2):
        for start in range(j * half, (j + 1) * half, STEP):
            at = slice(start, start + STEP)
            q = jnp.concatenate([r[:, at] for r in queries], 0)
            here[1][:, at] = (dot(w_grad[...], q, 1, 0) * sharpness_factor).astype(bf16)
        out[2 + j].start()
    for copy in out:
        copy.wait()


def taken(refs, *counts):
    out, at = [], 0
    for count in counts:
        out.append(list(refs[at : at + count]))
        at += count
    return out


def sums_kernel(partners, *refs):
    n = partners
    (c, q, far_q, far_q_sib, hq, hc, (stats,), answers, sib_answers, made, made_sib, (factors, scores), totals,
     (w_grad, w_own, terms)) = taken(refs, 2, 2, n, n, 2, 2, 1, n, n, n, n, 2, n if n > 1 else 0, 3)
    block, rows = c[0].shape[0], q[0].shape[0]
    shards, rank, width = terms.shape
    position = lax.axis_index("dp")
    own = [stats[at : at + 1] for at in (MAX, SUM, POSITIVE, HARD)]
    sib = sender_stats(made_sib[0], block)
    far_factors = [factors_of(a[2 * block + EXTRA :], block) for a in answers]
    far_stats = [sender_stats(a, block) for a in sib_answers]
    answers = [message_parts(a, block) for a in answers]
    sib_answers = [message_parts(a, block, turned=True) for a in sib_answers]

    def scaled(first, shares, tops, log_totals, positive, hard):
        owner, slot = layout(first, block, shares.shape)
        top = jnp.where(slot < rows, tops[0], jnp.where(owner == first, tops[1], tops[2]))
        kept = allowed(owner, slot, hard, rows)
        weights = shares * jnp.exp(jnp.where(kept, top - log_totals, -jnp.inf))
        return (weights - hits(owner, slot, positive, rows).astype(f32)).astype(bf16)

    firsts = [position ^ (2 * i + 2) for i in range(n)]
    hard, positive = (jnp.concatenate([own[i], sib[i]], 1) for i in (3, 2))
    owner, slot = layout(position, block, scores.shape)
    kept = allowed(owner, slot, hard, rows)
    hit = hits(owner, slot, positive, rows)
    log_totals = jnp.concatenate(
        [log_total(c, [(f, p[1]) for f, p in zip(firsts, parts)]) for c, parts in ((own, answers), (sib, sib_answers))],
        1,
    )
    near = jnp.exp(jnp.where(kept, scores[...] - log_totals, -jnp.inf)) - hit.astype(f32)
    near = near.astype(bf16)
    w_own[...] = near[:, :rows]
    pieces = [near]
    for i, (mine, other, chip) in enumerate(zip(made, made_sib, far_stats)):
        shares, pairs = message_parts(other, block, turned=True)
        far_total = totals[i][MAX : MAX + 1] if totals else log_total(chip, [(position, pairs)])
        pieces += [mine[...], scaled(position, shares, [top for top, _ in pairs], far_total, chip[2], chip[3])]
    weights = jnp.concatenate(pieces, 1)
    w_grad[...] = weights[:block]
    by_query = jnp.concatenate([r[:, : 2 * rows] for r in [factors] + [f for f, _ in far_factors]], 1)
    by_candidate = factors[:, 2 * rows :]
    queries = list(q)
    for pair in zip(far_q, far_q_sib):
        queries += pair

    def split(terms):
        high = terms.astype(bf16)
        return jnp.concatenate([high, (terms - high.astype(f32)).astype(bf16)], 0)

    core = lax.axis_index("dp") & 1

    @pl.when(core == 0)
    def _():
        over_c = split(dot(by_query.astype(bf16), weights, 1, 1) * sharpness_factor)
        over_q = split(dot(by_candidate.astype(bf16), weights, 1, 0) * sharpness_factor)
        for i in range(shards):
            at = slice(i * width, (i + 1) * width)
            from_c = jnp.concatenate([r[:, at] for r in c], 0)
            from_q = jnp.concatenate([r[:, at] for r in queries], 0)
            total = dot(over_c, from_c, 1, 0) + dot(over_q, from_q, 1, 0)
            terms[i] = (total[:rank] + total[rank:]).astype(bf16)

    @pl.when(core == 1)
    def _():
        back_q = dot_wide(by_candidate, near, 1, 0)
        for i in range(n):
            shares = jnp.concatenate([answers[i][0], sib_answers[i][0]], 1)
            tops = [jnp.concatenate([a[0], b[0]], 1) for a, b in zip(answers[i][1], sib_answers[i][1])]
            there = scaled(firsts[i], shares, tops, log_totals, positive, hard)
            back_q = back_q + dot_wide(far_factors[i][1], there, 1, 0)
        back_q = (back_q * sharpness_factor).astype(bf16)
        back_c = (dot_wide(by_query, weights, 1, 1) * sharpness_factor).astype(bf16)
        for i in range(shards):
            at = slice(i * width, (i + 1) * width)
            from_q = jnp.concatenate([r[:, at] for r in hq], 0)
            from_c = jnp.concatenate([r[:, at] for r in hc], 0)
            terms[i] = (dot(back_q, from_q, 1, 0) + dot(back_c, from_c, 1, 0)).astype(bf16)


def call(kernel, outs, needs=(), cost=0, scratch=(), away=False):
    vmem = pl.BlockSpec(memory_space=pltpu.VMEM)
    anywhere = pl.BlockSpec(memory_space=pl.ANY)

    def run(*args):
        def body(*refs):
            kernel(*refs[: len(args)], *refs[len(args) + len(needs) :])

        return pl.pallas_call(
            body,
            out_shape=outs,
            in_specs=[vmem] * len(args) + [anywhere] * len(needs),
            out_specs=jax.tree.map(lambda _: anywhere if away else vmem, outs),
            scratch_shapes=list(scratch),
            compiler_params=pltpu.CompilerParams(vmem_limit_bytes=16 * 2**20),
            cost_estimate=pl.CostEstimate(flops=1000 + cost, bytes_accessed=1000 + cost // 300, transcendentals=0),
        )(*args, *needs)

    return run


def shaped(shape, dtype=f32):
    return jax.ShapeDtypeStruct(shape, dtype)


def swap(array, axis, apart):
    return lax.ppermute(array, axis, [(i, i ^ apart) for i in range(lax.axis_size(axis))])


def after(array, *others):
    return lax.optimization_barrier((array, *others))[0]


def on_device(
    queries, candidates, positives, hard_blocks, query_hidden, candidate_hidden, adapter_down, adapter_up
):
    q_own, c_own = queries[0], candidates[0, 0]
    hq, hc = query_hidden[0], candidate_hidden[0, 0]
    rows, width = q_own.shape
    block = c_own.shape[0]
    rank, shard_width = adapter_down.shape
    devices, shards = lax.axis_size("dp"), lax.axis_size("fsdp")
    position = lax.axis_index("dp")
    partners = list(range(2, devices, 2))
    even = (position & 1) == 0

    far_q = [swap(q_own, "dp", k) for k in partners]
    c_sib, q_sib, hq_sib, hc_sib = (swap(a, "dp", 1) for a in (c_own, q_own, hq, hc))
    mine = call(copies_kernel, shaped((shards, rank, shard_width), bf16), cost=5_000_000_000)(
        jnp.where(even, adapter_down, adapter_up)
    )
    maps = lax.all_to_all(mine, "fsdp", 0, 0)

    factors = call(adapter_kernel, shaped((rank, 2 * rows + 2 * block)))(
        maps, hq, hq_sib, hc, hc_sib, c_own, c_sib, q_own, q_sib
    )
    scores, stats = call(scores_kernel, (shaped((2 * block, 2 * rows)), shaped((STATS, rows))), [factors])(
        c_own, c_sib, q_own, q_sib, positives, hard_blocks
    )

    made, made_sib, answers, sib_answers, far_q_near, far_q_sib, sent, shares = [], [], [], [], [], [], [], []
    far_scores = []
    for k, q in zip(partners, far_q):
        message, far, q_again = call(
            partner_kernel,
            (
                shaped((2 * block + EXTRA + 6 * rank, 2 * rows), bf16),
                shaped((2 * block, rows)),
                shaped((rows, width), bf16),
            ),
        )(c_own, c_sib, q, stats, factors)
        answers.append(swap(message, "dp", k))
        made_sib.append(swap(message, "dp", 1))
        sib_answers.append(swap(answers[-1], "dp", 1))
        far_scores.append(far)
        far_q_near.append(q_again)
        far_q_sib.append(swap(q_again, "dp", 1))
    far_totals, sib_totals = [], []
    if len(partners) > 1:
        totals = call(functools.partial(totals_kernel, block), shaped((STATS, rows)))(stats, *answers)
        far_totals = [swap(totals, "dp", k) for k in partners]
        sib_totals = [swap(total, "dp", 1) for total in far_totals]
    for i, k in enumerate(partners):
        weights, share = call(
            share_kernel, (shaped((2 * block, rows), bf16), shaped((rows, width), bf16)), [made_sib[i]]
        )(far_scores[i], answers[i], c_own, c_sib, *far_totals[i : i + 1])
        made.append(weights)
        sent.append(share)
        shares.append(swap(after(share, sib_answers[i]), "dp", k))

    w_grad, w_own, terms = call(
        functools.partial(sums_kernel, len(partners)),
        (
            shaped((block, rows * devices), bf16),
            shaped((2 * block, rows), bf16),
            shaped((shards, rank, shard_width), bf16),
        ),
        sent,
    )(
        c_own, c_sib, q_own, q_sib, *far_q_near, *far_q_sib, hq, hq_sib, hc, hc_sib, stats,
        *answers, *sib_answers, *made, *made_sib, factors, scores, *sib_totals,
    )
    queries = [q_own, q_sib]
    for pair in zip(far_q_near, far_q_sib):
        queries += pair
    kinds = [shaped((rows, width), bf16), shaped((block, width), bf16)]
    question, grad = call(
        functools.partial(rows_kernel, len(partners)),
        kinds,
        scratch=[pltpu.VMEM(kind.shape, bf16) for kind in kinds] + [pltpu.SemaphoreType.DMA((4,))],
        away=True,
    )(w_own, w_grad, c_own, c_sib, *queries, *shares)

    terms = lax.all_to_all(terms, "fsdp", 0, 0)
    terms = jnp.sum(terms.astype(f32), 0)
    apart = 2
    while 2 * apart < devices:
        terms = terms + swap(terms, "dp", apart)
        apart *= 2
    got = [swap(terms, "dp", k) for k in (apart, apart ^ 1, 1)]
    got[0] = after(got[0], question, grad)
    others = (got[1] + got[2]) * adapter_scale
    terms = (terms + got[0]) * adapter_scale
    return (
        question[None],
        grad[None, None],
        jnp.where(even, others, terms),
        jnp.where(even, terms, others),
    )


def solution(mesh):
    placed = (
        P("fsdp", "dp", None),
        P("fsdp", "dp", None, None),
        P("fsdp", "dp"),
        P("fsdp", "dp"),
        P("fsdp", "dp", None),
        P("fsdp", "dp", None, None),
        P(None, "fsdp"),
        P(None, "fsdp"),
    )
    return jax.shard_map(
        on_device,
        mesh=mesh,
        in_specs=placed,
        out_specs=(
            P("fsdp", "dp", None),
            P("fsdp", "dp", None, None),
            P(None, "fsdp"),
            P(None, "fsdp"),
        ),
        check_vma=False,
    )
```

```python
import functools

import jax
import jax.numpy as jnp
from jax import lax
from jax.experimental import pallas as pl
from jax.experimental.pallas import tpu as pltpu
from jax.sharding import PartitionSpec as P

sharpness_factor = 50.0
adapter_scale = 2.0
STEP = 512
MAX, SUM, POSITIVE, HARD, STATS = 0, 1, 2, 3, 8
EXTRA = 32

f32 = jnp.float32
bf16 = jnp.bfloat16


def dot(left, right, left_dim, right_dim):
    return lax.dot_general(
        left, right, (((left_dim,), (right_dim,)), ((), ())), preferred_element_type=f32
    )


def dot_wide(left, right, left_dim, right_dim):
    high = left.astype(bf16)
    low = (left - high.astype(f32)).astype(bf16)
    return dot(high, right, left_dim, right_dim) + dot(low, right, left_dim, right_dim)


def layout(position, block, shape):
    row = lax.broadcasted_iota(jnp.int32, shape, 0)
    own = row < block
    return jnp.where(own, position, position ^ 1), jnp.where(own, row, row - block)


def allowed(owner, slot, hard, rows):
    return (slot < rows) | (hard.astype(jnp.int32) == owner)


def hits(owner, slot, positive, rows):
    return (slot < rows) & (positive.astype(jnp.int32) == owner * rows + slot)


def merge(stats):
    top = functools.reduce(jnp.maximum, [m for m, _ in stats])
    return top + jnp.log(sum(s * jnp.exp(m - top) for m, s in stats))


def terms_of(row):
    rows = []
    for _ in range(3):
        rows.append(row.astype(bf16))
        row = row - rows[-1].astype(f32)
    return rows


def whole(rows):
    return rows[0:1] + rows[1:2] + rows[2:3]


def side_by_side(rows):
    block = rows.shape[0] // 2
    return jnp.concatenate([rows[:block], rows[block:]], 1)


def stacked(rows, turned=False):
    half = rows.shape[1] // 2
    halves = rows[:, :half], rows[:, half:]
    return jnp.concatenate(halves[::-1] if turned else halves, 0)


def message_of(shares, pairs, stats, factors, rows, block):
    high, low = wide_rows(shares)
    values = [value for pair in pairs for value in pair] + [stats[at : at + 1] for at in (MAX, SUM, POSITIVE)]
    lines = [term for value in values for term in terms_of(value)] + [stats[HARD : HARD + 1].astype(bf16)]
    lines = jnp.concatenate(lines + [jnp.zeros((EXTRA - len(lines), rows), bf16)], 0)
    parts = [side_by_side(high), side_by_side(low), jnp.concatenate([lines, lines], 1)]
    return jnp.concatenate(parts + [factor_rows(factors, rows, block)], 0)


def message_lines(message, block):
    at, rows = 2 * block, message.shape[1] // 2
    lines = message[at : at + EXTRA].astype(f32)[:, :rows]
    return [whole(lines[3 * i : 3 * i + 3]) for i in range(9)] + [lines[27:28]]


def sender_stats(message, block):
    return message_lines(message, block)[6:]


def message_parts(message, block, turned=False):
    high, low = (stacked(message[i * block : (i + 1) * block], turned).astype(f32) for i in (0, 1))
    values = message_lines(message, block)
    pairs = list(zip(values[0:6:2], values[1:6:2]))
    return high + low, pairs[:1] + (pairs[:0:-1] if turned else pairs[1:])


def wide_rows(array):
    high = array.astype(bf16)
    return [high, (array - high.astype(f32)).astype(bf16)]


def factor_rows(factors, rows, block):
    out = wide_rows(factors[:, : 2 * rows])
    for start in (2 * rows, 2 * rows + block):
        part = factors[:, start : start + block]
        out += [jnp.concatenate([p, jnp.zeros((p.shape[0], 2 * rows - block), bf16)], 1) for p in wide_rows(part)]
    return jnp.concatenate(out, 0)


def factors_of(packed_rows, block):
    rank = packed_rows.shape[0] // 6
    high, low = [[packed_rows[(2 * i + j) * rank : (2 * i + j + 1) * rank].astype(f32) for i in range(3)] for j in (0, 1)]
    query, own, sib = [a + b for a, b in zip(high, low)]
    return query, jnp.concatenate([own[:, :block], sib[:, :block]], 1)


def scores_kernel(c_own, c_sib, q_own, q_sib, positives, hard, scores, stats):
    block, rows = c_own.shape[0], q_own.shape[0]
    c = jnp.concatenate([c_own[...], c_sib[...]], 0)
    q = jnp.concatenate([q_own[...], q_sib[...]], 0)
    total = dot(c, q, 1, 1) * sharpness_factor
    scores[...] = total
    mine = total[:, :rows]
    owner, slot = layout(lax.axis_index("dp"), block, mine.shape)
    mine = jnp.where(allowed(owner, slot, hard[...], rows), mine, -jnp.inf)
    top = jnp.max(mine, axis=0, keepdims=True)
    stats[...] = jnp.zeros_like(stats)
    stats[MAX : MAX + 1] = top
    stats[SUM : SUM + 1] = jnp.sum(jnp.exp(mine - top), axis=0, keepdims=True)
    stats[POSITIVE : POSITIVE + 1] = positives[...].astype(f32)
    stats[HARD : HARD + 1] = hard[...].astype(f32)


def copies_kernel(own, out):
    for i in range(out.shape[0]):
        out[i] = own[...]


def chip_kernel(maps, hq, hq_sib, hc, hc_sib, c_own, c_sib, q_own, q_sib, positives, hard, factors, scores, stats):
    scores_kernel(c_own, c_sib, q_own, q_sib, positives, hard, scores, stats)
    shards, _, width = maps.shape

    def product(parts):
        out = []
        for r in parts:
            total = 0.0
            for at in range(shards):
                total = total + dot(r[:, at * width : (at + 1) * width], maps[at], 1, 1)
            out.append(total)
        return jnp.concatenate(out, 0).T

    core = lax.axis_index("dp") & 1

    @pl.when(core == 0)
    def _():
        factors[...] = product([hq, hq_sib, hc, hc_sib]).astype(bf16).astype(f32)

    @pl.when(core == 1)
    def _():
        factors[...] = product([q_own, q_sib, c_own, c_sib])


def partner_kernel(c_own, c_sib, q, stats, factors, message, scores, q_again):
    block, rows = c_own.shape[0], q.shape[0]
    c = jnp.concatenate([c_own[...], c_sib[...]], 0)
    q_again[...] = q[...]
    total = dot(c, q[...], 1, 1) * sharpness_factor
    scores[...] = total
    owner, slot = layout(0, block, total.shape)
    parts = [slot < rows, (slot >= rows) & (owner == 0), (slot >= rows) & (owner == 1)]
    tops = [jnp.max(jnp.where(part, total, -jnp.inf), axis=0, keepdims=True) for part in parts]
    shares = jnp.exp(total - jnp.where(parts[0], tops[0], jnp.where(parts[1], tops[1], tops[2])))
    sums = [jnp.sum(jnp.where(part, shares, 0.0), axis=0, keepdims=True) for part in parts]
    message[...] = message_of(shares, list(zip(tops, sums)), stats, factors[...], rows, block)


def log_total(chip, parts):
    terms = [(chip[0], chip[1])]
    for first, pairs in parts:
        terms.append(pairs[0])
        for (top, total), at in zip(pairs[1:], (first, first ^ 1)):
            counts = chip[3].astype(jnp.int32) == at
            terms.append((jnp.where(counts, top, pairs[0][0]), jnp.where(counts, total, 0.0)))
    return merge(terms)


def totals_kernel(block, stats, *refs):
    answers, out = refs[:-1], refs[-1]
    position = lax.axis_index("dp")
    own = [stats[at : at + 1] for at in (MAX, SUM, POSITIVE, HARD)]
    pairs = [message_parts(a, block)[1] for a in answers]
    out[...] = stats[...]
    out[MAX : MAX + 1] = log_total(own, [(position ^ (2 * i + 2), p) for i, p in enumerate(pairs)])


def share_kernel(scores, answer, c_own, c_sib, *refs):
    *totals, weights, share = refs
    block, rows = c_own.shape[0], scores.shape[1]
    far_top, far_total, positive, hard = sender_stats(answer, block)
    owner, slot = layout(lax.axis_index("dp"), block, scores.shape)
    total = jnp.where(allowed(owner, slot, hard, rows), scores[...], -jnp.inf)
    top = jnp.max(total, axis=0, keepdims=True)
    here = jnp.sum(jnp.exp(total - top), axis=0, keepdims=True)
    if totals:
        log_sum = totals[0][MAX : MAX + 1]
    else:
        log_sum = merge([(far_top, far_total), (top, here)])
    hit = hits(owner, slot, positive, rows)
    weights[...] = (jnp.exp(total - log_sum) - hit.astype(f32)).astype(bf16)
    for i in range(share.shape[1] // STEP):
        at = slice(i * STEP, (i + 1) * STEP)
        c = jnp.concatenate([c_own[:, at], c_sib[:, at]], 0)
        share[:, at] = (dot(weights[...], c, 0, 0) * sharpness_factor).astype(bf16)


def rows_kernel(partners, w_own, w_grad, c_own, c_sib, *refs):
    queries, shares, (question, grad), here, (sems,) = taken(refs, 2 * partners + 2, partners, 2, 2, 1)
    half = question.shape[1] // 2
    out = []
    for i, (target, rows) in enumerate(zip((question, grad), here)):
        for j in range(2):
            part = pl.ds(j * half, half)
            out.append(pltpu.make_async_copy(rows.at[:, part], target.at[:, part], sems.at[2 * i + j]))
    for j in range(2):
        for start in range(j * half, (j + 1) * half, STEP):
            at = slice(start, start + STEP)
            c = jnp.concatenate([c_own[:, at], c_sib[:, at]], 0)
            total = dot(w_own[...], c, 0, 0) * sharpness_factor
            for share in shares:
                total = total + share[:, at].astype(f32)
            here[0][:, at] = total.astype(bf16)
        out[j].start()
    for j in range(2):
        for start in range(j * half, (j + 1) * half, STEP):
            at = slice(start, start + STEP)
            q = jnp.concatenate([r[:, at] for r in queries], 0)
            here[1][:, at] = (dot(w_grad[...], q, 1, 0) * sharpness_factor).astype(bf16)
        out[2 + j].start()
    for copy in out:
        copy.wait()


def taken(refs, *counts):
    out, at = [], 0
    for count in counts:
        out.append(list(refs[at : at + count]))
        at += count
    return out


def sums_kernel(partners, *refs):
    n = partners
    (c, q, far_q, far_q_sib, hq, hc, (stats,), answers, sib_answers, made, made_sib, (factors, scores), totals,
     (w_grad, w_own, terms)) = taken(refs, 2, 2, n, n, 2, 2, 1, n, n, n, n, 2, n if n > 1 else 0, 3)
    block, rows = c[0].shape[0], q[0].shape[0]
    shards, rank, width = terms.shape
    position = lax.axis_index("dp")
    own = [stats[at : at + 1] for at in (MAX, SUM, POSITIVE, HARD)]
    sib = sender_stats(made_sib[0], block)
    far_factors = [factors_of(a[2 * block + EXTRA :], block) for a in answers]
    far_stats = [sender_stats(a, block) for a in sib_answers]
    answers = [message_parts(a, block) for a in answers]
    sib_answers = [message_parts(a, block, turned=True) for a in sib_answers]

    def scaled(first, shares, tops, log_totals, positive, hard):
        owner, slot = layout(first, block, shares.shape)
        top = jnp.where(slot < rows, tops[0], jnp.where(owner == first, tops[1], tops[2]))
        kept = allowed(owner, slot, hard, rows)
        weights = shares * jnp.exp(jnp.where(kept, top - log_totals, -jnp.inf))
        return (weights - hits(owner, slot, positive, rows).astype(f32)).astype(bf16)

    firsts = [position ^ (2 * i + 2) for i in range(n)]
    hard, positive = (jnp.concatenate([own[i], sib[i]], 1) for i in (3, 2))
    owner, slot = layout(position, block, scores.shape)
    kept = allowed(owner, slot, hard, rows)
    hit = hits(owner, slot, positive, rows)
    log_totals = jnp.concatenate(
        [log_total(c, [(f, p[1]) for f, p in zip(firsts, parts)]) for c, parts in ((own, answers), (sib, sib_answers))],
        1,
    )
    near = jnp.exp(jnp.where(kept, scores[...] - log_totals, -jnp.inf)) - hit.astype(f32)
    near = near.astype(bf16)
    w_own[...] = near[:, :rows]
    pieces = [near]
    for i, (mine, other, chip) in enumerate(zip(made, made_sib, far_stats)):
        shares, pairs = message_parts(other, block, turned=True)
        far_total = totals[i][MAX : MAX + 1] if totals else log_total(chip, [(position, pairs)])
        pieces += [mine[...], scaled(position, shares, [top for top, _ in pairs], far_total, chip[2], chip[3])]
    weights = jnp.concatenate(pieces, 1)
    w_grad[...] = weights[:block]
    by_query = jnp.concatenate([r[:, : 2 * rows] for r in [factors] + [f for f, _ in far_factors]], 1)
    by_candidate = factors[:, 2 * rows :]
    queries = list(q)
    for pair in zip(far_q, far_q_sib):
        queries += pair

    def split(terms):
        high = terms.astype(bf16)
        return jnp.concatenate([high, (terms - high.astype(f32)).astype(bf16)], 0)

    core = lax.axis_index("dp") & 1

    @pl.when(core == 0)
    def _():
        over_c = split(dot(by_query.astype(bf16), weights, 1, 1) * sharpness_factor)
        over_q = split(dot(by_candidate.astype(bf16), weights, 1, 0) * sharpness_factor)
        for i in range(shards):
            at = slice(i * width, (i + 1) * width)
            from_c = jnp.concatenate([r[:, at] for r in c], 0)
            from_q = jnp.concatenate([r[:, at] for r in queries], 0)
            total = dot(over_c, from_c, 1, 0) + dot(over_q, from_q, 1, 0)
            terms[i] = (total[:rank] + total[rank:]).astype(bf16)

    @pl.when(core == 1)
    def _():
        back_q = dot_wide(by_candidate, near, 1, 0)
        for i in range(n):
            shares = jnp.concatenate([answers[i][0], sib_answers[i][0]], 1)
            tops = [jnp.concatenate([a[0], b[0]], 1) for a, b in zip(answers[i][1], sib_answers[i][1])]
            there = scaled(firsts[i], shares, tops, log_totals, positive, hard)
            back_q = back_q + dot_wide(far_factors[i][1], there, 1, 0)
        back_q = (back_q * sharpness_factor).astype(bf16)
        back_c = (dot_wide(by_query, weights, 1, 1) * sharpness_factor).astype(bf16)
        for i in range(shards):
            at = slice(i * width, (i + 1) * width)
            from_q = jnp.concatenate([r[:, at] for r in hq], 0)
            from_c = jnp.concatenate([r[:, at] for r in hc], 0)
            terms[i] = (dot(back_q, from_q, 1, 0) + dot(back_c, from_c, 1, 0)).astype(bf16)


def call(kernel, outs, needs=(), cost=0, scratch=(), away=False):
    vmem = pl.BlockSpec(memory_space=pltpu.VMEM)
    anywhere = pl.BlockSpec(memory_space=pl.ANY)

    def run(*args):
        def body(*refs):
            kernel(*refs[: len(args)], *refs[len(args) + len(needs) :])

        return pl.pallas_call(
            body,
            out_shape=outs,
            in_specs=[vmem] * len(args) + [anywhere] * len(needs),
            out_specs=jax.tree.map(lambda _: anywhere if away else vmem, outs),
            scratch_shapes=list(scratch),
            compiler_params=pltpu.CompilerParams(vmem_limit_bytes=16 * 2**20),
            cost_estimate=pl.CostEstimate(flops=1000 + cost, bytes_accessed=1000 + cost // 300, transcendentals=0),
        )(*args, *needs)

    return run


def shaped(shape, dtype=f32):
    return jax.ShapeDtypeStruct(shape, dtype)


def swap(array, axis, apart):
    return lax.ppermute(array, axis, [(i, i ^ apart) for i in range(lax.axis_size(axis))])


def after(array, *others):
    return lax.optimization_barrier((array, *others))[0]


def on_device(
    queries, candidates, positives, hard_blocks, query_hidden, candidate_hidden, adapter_down, adapter_up
):
    q_own, c_own = queries[0], candidates[0, 0]
    hq, hc = query_hidden[0], candidate_hidden[0, 0]
    rows, width = q_own.shape
    block = c_own.shape[0]
    rank, shard_width = adapter_down.shape
    devices, shards = lax.axis_size("dp"), lax.axis_size("fsdp")
    position = lax.axis_index("dp")
    partners = list(range(2, devices, 2))
    even = (position & 1) == 0

    far_q = [swap(q_own, "dp", k) for k in partners]
    c_sib, q_sib, hq_sib, hc_sib = (swap(a, "dp", 1) for a in (c_own, q_own, hq, hc))
    mine = call(copies_kernel, shaped((shards, rank, shard_width), bf16), cost=5_000_000_000)(
        jnp.where(even, adapter_down, adapter_up)
    )
    maps = lax.all_to_all(mine, "fsdp", 0, 0)

    factors, scores, stats = call(
        chip_kernel,
        (shaped((rank, 2 * rows + 2 * block)), shaped((2 * block, 2 * rows)), shaped((STATS, rows))),
    )(maps, hq, hq_sib, hc, hc_sib, c_own, c_sib, q_own, q_sib, positives, hard_blocks)

    made, made_sib, answers, sib_answers, far_q_near, far_q_sib, sent, shares = [], [], [], [], [], [], [], []
    far_scores = []
    for k, q in zip(partners, far_q):
        message, far, q_again = call(
            partner_kernel,
            (
                shaped((2 * block + EXTRA + 6 * rank, 2 * rows), bf16),
                shaped((2 * block, rows)),
                shaped((rows, width), bf16),
            ),
        )(c_own, c_sib, q, stats, factors)
        answers.append(swap(message, "dp", k))
        made_sib.append(swap(message, "dp", 1))
        sib_answers.append(swap(answers[-1], "dp", 1))
        far_scores.append(far)
        far_q_near.append(q_again)
        far_q_sib.append(swap(q_again, "dp", 1))
    far_totals, sib_totals = [], []
    if len(partners) > 1:
        totals = call(functools.partial(totals_kernel, block), shaped((STATS, rows)))(stats, *answers)
        far_totals = [swap(totals, "dp", k) for k in partners]
        sib_totals = [swap(total, "dp", 1) for total in far_totals]
    for i, k in enumerate(partners):
        weights, share = call(
            share_kernel, (shaped((2 * block, rows), bf16), shaped((rows, width), bf16)), [made_sib[i]]
        )(far_scores[i], answers[i], c_own, c_sib, *far_totals[i : i + 1])
        made.append(weights)
        sent.append(share)
        shares.append(swap(after(share, sib_answers[i]), "dp", k))

    w_grad, w_own, terms = call(
        functools.partial(sums_kernel, len(partners)),
        (
            shaped((block, rows * devices), bf16),
            shaped((2 * block, rows), bf16),
            shaped((shards, rank, shard_width), bf16),
        ),
        sent,
    )(
        c_own, c_sib, q_own, q_sib, *far_q_near, *far_q_sib, hq, hq_sib, hc, hc_sib, stats,
        *answers, *sib_answers, *made, *made_sib, factors, scores, *sib_totals,
    )
    queries = [q_own, q_sib]
    for pair in zip(far_q_near, far_q_sib):
        queries += pair
    kinds = [shaped((rows, width), bf16), shaped((block, width), bf16)]
    question, grad = call(
        functools.partial(rows_kernel, len(partners)),
        kinds,
        scratch=[pltpu.VMEM(kind.shape, bf16) for kind in kinds] + [pltpu.SemaphoreType.DMA((4,))],
        away=True,
    )(w_own, w_grad, c_own, c_sib, *queries, *shares)

    terms = lax.all_to_all(terms, "fsdp", 0, 0)
    terms = jnp.sum(terms.astype(f32), 0)
    apart = 2
    while 2 * apart < devices:
        terms = terms + swap(terms, "dp", apart)
        apart *= 2
    got = [swap(terms, "dp", k) for k in (apart, apart ^ 1, 1)]
    got[0] = after(got[0], question, grad)
    others = (got[1] + got[2]) * adapter_scale
    terms = (terms + got[0]) * adapter_scale
    return (
        question[None],
        grad[None, None],
        jnp.where(even, others, terms),
        jnp.where(even, terms, others),
    )


def solution(mesh):
    placed = (
        P("fsdp", "dp", None),
        P("fsdp", "dp", None, None),
        P("fsdp", "dp"),
        P("fsdp", "dp"),
        P("fsdp", "dp", None),
        P("fsdp", "dp", None, None),
        P(None, "fsdp"),
        P(None, "fsdp"),
    )
    return jax.shard_map(
        on_device,
        mesh=mesh,
        in_specs=placed,
        out_specs=(
            P("fsdp", "dp", None),
            P("fsdp", "dp", None, None),
            P(None, "fsdp"),
            P(None, "fsdp"),
        ),
        check_vma=False,
    )
```

```python
import functools

import jax
import jax.numpy as jnp
from jax import lax
from jax.experimental import pallas as pl
from jax.experimental.pallas import tpu as pltpu
from jax.sharding import PartitionSpec as P

sharpness_factor = 50.0
adapter_scale = 2.0
STEP = 512
MAX, SUM, POSITIVE, HARD, STATS = 0, 1, 2, 3, 8
EXTRA = 32

f32 = jnp.float32
bf16 = jnp.bfloat16


def dot(left, right, left_dim, right_dim):
    return lax.dot_general(
        left, right, (((left_dim,), (right_dim,)), ((), ())), preferred_element_type=f32
    )


def dot_wide(left, right, left_dim, right_dim):
    high = left.astype(bf16)
    low = (left - high.astype(f32)).astype(bf16)
    return dot(high, right, left_dim, right_dim) + dot(low, right, left_dim, right_dim)


def layout(position, block, shape):
    row = lax.broadcasted_iota(jnp.int32, shape, 0)
    own = row < block
    return jnp.where(own, position, position ^ 1), jnp.where(own, row, row - block)


def allowed(owner, slot, hard, rows):
    return (slot < rows) | (hard.astype(jnp.int32) == owner)


def hits(owner, slot, positive, rows):
    return (slot < rows) & (positive.astype(jnp.int32) == owner * rows + slot)


def merge(stats):
    top = functools.reduce(jnp.maximum, [m for m, _ in stats])
    return top + jnp.log(sum(s * jnp.exp(m - top) for m, s in stats))


def terms_of(row):
    rows = []
    for _ in range(3):
        rows.append(row.astype(bf16))
        row = row - rows[-1].astype(f32)
    return rows


def whole(rows):
    return rows[0:1] + rows[1:2] + rows[2:3]


def side_by_side(rows):
    block = rows.shape[0] // 2
    return jnp.concatenate([rows[:block], rows[block:]], 1)


def stacked(rows, turned=False):
    half = rows.shape[1] // 2
    halves = rows[:, :half], rows[:, half:]
    return jnp.concatenate(halves[::-1] if turned else halves, 0)


def message_of(shares, pairs, stats, factors, rows, block):
    high, low = wide_rows(shares)
    values = [value for pair in pairs for value in pair] + [stats[at : at + 1] for at in (MAX, SUM, POSITIVE)]
    lines = [term for value in values for term in terms_of(value)] + [stats[HARD : HARD + 1].astype(bf16)]
    lines = jnp.concatenate(lines + [jnp.zeros((EXTRA - len(lines), rows), bf16)], 0)
    parts = [side_by_side(high), side_by_side(low), jnp.concatenate([lines, lines], 1)]
    return jnp.concatenate(parts + [factor_rows(factors, rows, block)], 0)


def message_lines(message, block):
    at, rows = 2 * block, message.shape[1] // 2
    lines = message[at : at + EXTRA].astype(f32)[:, :rows]
    return [whole(lines[3 * i : 3 * i + 3]) for i in range(9)] + [lines[27:28]]


def sender_stats(message, block):
    return message_lines(message, block)[6:]


def message_parts(message, block, turned=False):
    high, low = (stacked(message[i * block : (i + 1) * block], turned).astype(f32) for i in (0, 1))
    values = message_lines(message, block)
    pairs = list(zip(values[0:6:2], values[1:6:2]))
    return high + low, pairs[:1] + (pairs[:0:-1] if turned else pairs[1:])


def wide_rows(array):
    high = array.astype(bf16)
    return [high, (array - high.astype(f32)).astype(bf16)]


def factor_rows(factors, rows, block):
    out = wide_rows(factors[:, : 2 * rows])
    for start in (2 * rows, 2 * rows + block):
        part = factors[:, start : start + block]
        out += [jnp.concatenate([p, jnp.zeros((p.shape[0], 2 * rows - block), bf16)], 1) for p in wide_rows(part)]
    return jnp.concatenate(out, 0)


def factors_of(packed_rows, block):
    rank = packed_rows.shape[0] // 6
    high, low = [[packed_rows[(2 * i + j) * rank : (2 * i + j + 1) * rank].astype(f32) for i in range(3)] for j in (0, 1)]
    query, own, sib = [a + b for a, b in zip(high, low)]
    return query, jnp.concatenate([own[:, :block], sib[:, :block]], 1)


def scores_kernel(c_own, c_sib, q_own, q_sib, positives, hard, scores, stats):
    block, rows = c_own.shape[0], q_own.shape[0]
    c = jnp.concatenate([c_own[...], c_sib[...]], 0)
    q = jnp.concatenate([q_own[...], q_sib[...]], 0)
    total = dot(c, q, 1, 1) * sharpness_factor
    scores[...] = total
    mine = total[:, :rows]
    owner, slot = layout(lax.axis_index("dp"), block, mine.shape)
    mine = jnp.where(allowed(owner, slot, hard[...], rows), mine, -jnp.inf)
    top = jnp.max(mine, axis=0, keepdims=True)
    stats[...] = jnp.zeros_like(stats)
    stats[MAX : MAX + 1] = top
    stats[SUM : SUM + 1] = jnp.sum(jnp.exp(mine - top), axis=0, keepdims=True)
    stats[POSITIVE : POSITIVE + 1] = positives[...].astype(f32)
    stats[HARD : HARD + 1] = hard[...].astype(f32)


def copies_kernel(own, out):
    for i in range(out.shape[0]):
        out[i] = own[...]


def adapter_kernel(maps, hq, hq_sib, hc, hc_sib, c_own, c_sib, q_own, q_sib, factors):
    shards, _, width = maps.shape

    def product(parts):
        out = []
        for r in parts:
            total = 0.0
            for at in range(shards):
                total = total + dot(r[:, at * width : (at + 1) * width], maps[at], 1, 1)
            out.append(total)
        return jnp.concatenate(out, 0).T

    core = lax.axis_index("dp") & 1

    @pl.when(core == 0)
    def _():
        factors[...] = product([hq, hq_sib, hc, hc_sib]).astype(bf16).astype(f32)

    @pl.when(core == 1)
    def _():
        factors[...] = product([q_own, q_sib, c_own, c_sib])


def partner_kernel(c_own, c_sib, q, stats, factors, message, scores, q_again):
    block, rows = c_own.shape[0], q.shape[0]
    c = jnp.concatenate([c_own[...], c_sib[...]], 0)
    q_again[...] = q[...]
    total = dot(c, q[...], 1, 1) * sharpness_factor
    scores[...] = total
    owner, slot = layout(0, block, total.shape)
    parts = [slot < rows, (slot >= rows) & (owner == 0), (slot >= rows) & (owner == 1)]
    tops = [jnp.max(jnp.where(part, total, -jnp.inf), axis=0, keepdims=True) for part in parts]
    shares = jnp.exp(total - jnp.where(parts[0], tops[0], jnp.where(parts[1], tops[1], tops[2])))
    sums = [jnp.sum(jnp.where(part, shares, 0.0), axis=0, keepdims=True) for part in parts]
    message[...] = message_of(shares, list(zip(tops, sums)), stats, factors[...], rows, block)


def log_total(chip, parts):
    terms = [(chip[0], chip[1])]
    for first, pairs in parts:
        terms.append(pairs[0])
        for (top, total), at in zip(pairs[1:], (first, first ^ 1)):
            counts = chip[3].astype(jnp.int32) == at
            terms.append((jnp.where(counts, top, pairs[0][0]), jnp.where(counts, total, 0.0)))
    return merge(terms)


def totals_kernel(block, stats, *refs):
    answers, out = refs[:-1], refs[-1]
    position = lax.axis_index("dp")
    own = [stats[at : at + 1] for at in (MAX, SUM, POSITIVE, HARD)]
    pairs = [message_parts(a, block)[1] for a in answers]
    out[...] = stats[...]
    out[MAX : MAX + 1] = log_total(own, [(position ^ (2 * i + 2), p) for i, p in enumerate(pairs)])


def share_kernel(scores, answer, c_own, c_sib, *refs):
    *totals, weights, share = refs
    block, rows = c_own.shape[0], scores.shape[1]
    far_top, far_total, positive, hard = sender_stats(answer, block)
    owner, slot = layout(lax.axis_index("dp"), block, scores.shape)
    total = jnp.where(allowed(owner, slot, hard, rows), scores[...], -jnp.inf)
    top = jnp.max(total, axis=0, keepdims=True)
    here = jnp.sum(jnp.exp(total - top), axis=0, keepdims=True)
    if totals:
        log_sum = totals[0][MAX : MAX + 1]
    else:
        log_sum = merge([(far_top, far_total), (top, here)])
    hit = hits(owner, slot, positive, rows)
    weights[...] = (jnp.exp(total - log_sum) - hit.astype(f32)).astype(bf16)
    for i in range(share.shape[1] // STEP):
        at = slice(i * STEP, (i + 1) * STEP)
        c = jnp.concatenate([c_own[:, at], c_sib[:, at]], 0)
        share[:, at] = (dot(weights[...], c, 0, 0) * sharpness_factor).astype(bf16)


def rows_kernel(partners, w_own, w_grad, c_own, c_sib, *refs):
    queries, shares, (question, grad), here, (sems,) = taken(refs, 2 * partners + 2, partners, 2, 2, 1)
    half = question.shape[1] // 2
    out = []
    for i, (target, rows) in enumerate(zip((question, grad), here)):
        for j in range(2):
            part = pl.ds(j * half, half)
            out.append(pltpu.make_async_copy(rows.at[:, part], target.at[:, part], sems.at[2 * i + j]))
    for j in range(2):
        for start in range(j * half, (j + 1) * half, STEP):
            at = slice(start, start + STEP)
            c = jnp.concatenate([c_own[:, at], c_sib[:, at]], 0)
            total = dot(w_own[...], c, 0, 0) * sharpness_factor
            for share in shares:
                total = total + share[:, at].astype(f32)
            here[0][:, at] = total.astype(bf16)
        out[j].start()
    for j in range(2):
        for start in range(j * half, (j + 1) * half, STEP):
            at = slice(start, start + STEP)
            q = jnp.concatenate([r[:, at] for r in queries], 0)
            here[1][:, at] = (dot(w_grad[...], q, 1, 0) * sharpness_factor).astype(bf16)
        out[2 + j].start()
    for copy in out:
        copy.wait()


def taken(refs, *counts):
    out, at = [], 0
    for count in counts:
        out.append(list(refs[at : at + count]))
        at += count
    return out


def sums_kernel(partners, *refs):
    n = partners
    (c, q, far_q, far_q_sib, hq, hc, (stats,), answers, sib_answers, made, made_sib, (factors, scores), totals,
     (w_grad, w_own, terms)) = taken(refs, 2, 2, n, n, 2, 2, 1, n, n, n, n, 2, n if n > 1 else 0, 3)
    block, rows = c[0].shape[0], q[0].shape[0]
    shards, rank, width = terms.shape
    position = lax.axis_index("dp")
    own = [stats[at : at + 1] for at in (MAX, SUM, POSITIVE, HARD)]
    sib = sender_stats(made_sib[0], block)
    far_factors = [factors_of(a[2 * block + EXTRA :], block) for a in answers]
    far_stats = [sender_stats(a, block) for a in sib_answers]
    answers = [message_parts(a, block) for a in answers]
    sib_answers = [message_parts(a, block, turned=True) for a in sib_answers]

    def scaled(first, shares, tops, log_totals, positive, hard):
        owner, slot = layout(first, block, shares.shape)
        top = jnp.where(slot < rows, tops[0], jnp.where(owner == first, tops[1], tops[2]))
        kept = allowed(owner, slot, hard, rows)
        weights = shares * jnp.exp(jnp.where(kept, top - log_totals, -jnp.inf))
        return (weights - hits(owner, slot, positive, rows).astype(f32)).astype(bf16)

    firsts = [position ^ (2 * i + 2) for i in range(n)]
    hard, positive = (jnp.concatenate([own[i], sib[i]], 1) for i in (3, 2))
    owner, slot = layout(position, block, scores.shape)
    kept = allowed(owner, slot, hard, rows)
    hit = hits(owner, slot, positive, rows)
    log_totals = jnp.concatenate(
        [log_total(c, [(f, p[1]) for f, p in zip(firsts, parts)]) for c, parts in ((own, answers), (sib, sib_answers))],
        1,
    )
    near = jnp.exp(jnp.where(kept, scores[...] - log_totals, -jnp.inf)) - hit.astype(f32)
    near = near.astype(bf16)
    w_own[...] = near[:, :rows]
    pieces = [near]
    for i, (mine, other, chip) in enumerate(zip(made, made_sib, far_stats)):
        shares, pairs = message_parts(other, block, turned=True)
        far_total = totals[i][MAX : MAX + 1] if totals else log_total(chip, [(position, pairs)])
        pieces += [mine[...], scaled(position, shares, [top for top, _ in pairs], far_total, chip[2], chip[3])]
    weights = jnp.concatenate(pieces, 1)
    w_grad[...] = weights[:block]
    by_query = jnp.concatenate([r[:, : 2 * rows] for r in [factors] + [f for f, _ in far_factors]], 1)
    by_candidate = factors[:, 2 * rows :]
    queries = list(q)
    for pair in zip(far_q, far_q_sib):
        queries += pair

    def split(terms):
        high = terms.astype(bf16)
        return jnp.concatenate([high, (terms - high.astype(f32)).astype(bf16)], 0)

    core = lax.axis_index("dp") & 1

    @pl.when(core == 0)
    def _():
        over_c = split(dot(by_query.astype(bf16), weights, 1, 1) * sharpness_factor)
        over_q = split(dot(by_candidate.astype(bf16), weights, 1, 0) * sharpness_factor)
        for i in range(shards):
            at = slice(i * width, (i + 1) * width)
            from_c = jnp.concatenate([r[:, at] for r in c], 0)
            from_q = jnp.concatenate([r[:, at] for r in queries], 0)
            total = dot(over_c, from_c, 1, 0) + dot(over_q, from_q, 1, 0)
            terms[i] = (total[:rank] + total[rank:]).astype(bf16)

    @pl.when(core == 1)
    def _():
        back_q = dot_wide(by_candidate, near, 1, 0)
        for i in range(n):
            shares = jnp.concatenate([answers[i][0], sib_answers[i][0]], 1)
            tops = [jnp.concatenate([a[0], b[0]], 1) for a, b in zip(answers[i][1], sib_answers[i][1])]
            there = scaled(firsts[i], shares, tops, log_totals, positive, hard)
            back_q = back_q + dot_wide(far_factors[i][1], there, 1, 0)
        back_q = (back_q * sharpness_factor).astype(bf16)
        back_c = (dot_wide(by_query, weights, 1, 1) * sharpness_factor).astype(bf16)
        for i in range(shards):
            at = slice(i * width, (i + 1) * width)
            from_q = jnp.concatenate([r[:, at] for r in hq], 0)
            from_c = jnp.concatenate([r[:, at] for r in hc], 0)
            terms[i] = (dot(back_q, from_q, 1, 0) + dot(back_c, from_c, 1, 0)).astype(bf16)


def call(kernel, outs, needs=(), cost=0, scratch=(), away=False):
    vmem = pl.BlockSpec(memory_space=pltpu.VMEM)
    anywhere = pl.BlockSpec(memory_space=pl.ANY)

    def run(*args):
        def body(*refs):
            kernel(*refs[: len(args)], *refs[len(args) + len(needs) :])

        return pl.pallas_call(
            body,
            out_shape=outs,
            in_specs=[vmem] * len(args) + [anywhere] * len(needs),
            out_specs=jax.tree.map(lambda _: anywhere if away else vmem, outs),
            scratch_shapes=list(scratch),
            compiler_params=pltpu.CompilerParams(vmem_limit_bytes=16 * 2**20),
            cost_estimate=pl.CostEstimate(flops=1000 + cost, bytes_accessed=1000 + cost // 300, transcendentals=0),
        )(*args, *needs)

    return run


def shaped(shape, dtype=f32):
    return jax.ShapeDtypeStruct(shape, dtype)


def swap(array, axis, apart):
    return lax.ppermute(array, axis, [(i, i ^ apart) for i in range(lax.axis_size(axis))])


def after(array, *others):
    return lax.optimization_barrier((array, *others))[0]


def on_device(
    queries, candidates, positives, hard_blocks, query_hidden, candidate_hidden, adapter_down, adapter_up
):
    q_own, c_own = queries[0], candidates[0, 0]
    hq, hc = query_hidden[0], candidate_hidden[0, 0]
    rows, width = q_own.shape
    block = c_own.shape[0]
    rank, shard_width = adapter_down.shape
    devices, shards = lax.axis_size("dp"), lax.axis_size("fsdp")
    position = lax.axis_index("dp")
    partners = list(range(2, devices, 2))
    even = (position & 1) == 0

    far_q = [swap(q_own, "dp", k) for k in partners]
    c_sib, q_sib, hq_sib, hc_sib = (swap(a, "dp", 1) for a in (c_own, q_own, hq, hc))
    mine = call(copies_kernel, shaped((shards, rank, shard_width), bf16), cost=5_000_000_000)(
        jnp.where(even, adapter_down, adapter_up)
    )
    maps = lax.all_to_all(mine, "fsdp", 0, 0)

    factors = call(adapter_kernel, shaped((rank, 2 * rows + 2 * block)))(
        maps, hq, hq_sib, hc, hc_sib, c_own, c_sib, q_own, q_sib
    )
    scores, stats = call(scores_kernel, (shaped((2 * block, 2 * rows)), shaped((STATS, rows))), [factors])(
        c_own, c_sib, q_own, q_sib, positives, hard_blocks
    )

    made, made_sib, answers, sib_answers, far_q_near, far_q_sib, sent, shares = [], [], [], [], [], [], [], []
    far_scores = []
    for k, q in zip(partners, far_q):
        message, far, q_again = call(
            partner_kernel,
            (
                shaped((2 * block + EXTRA + 6 * rank, 2 * rows), bf16),
                shaped((2 * block, rows)),
                shaped((rows, width), bf16),
            ),
        )(c_own, c_sib, q, stats, factors)
        answers.append(swap(message, "dp", k))
        made_sib.append(swap(message, "dp", 1))
        sib_answers.append(swap(answers[-1], "dp", 1))
        far_scores.append(far)
        far_q_near.append(q_again)
        far_q_sib.append(swap(q_again, "dp", 1))
    far_totals, sib_totals = [], []
    if len(partners) > 1:
        totals = call(functools.partial(totals_kernel, block), shaped((STATS, rows)))(stats, *answers)
        far_totals = [swap(totals, "dp", k) for k in partners]
        sib_totals = [swap(total, "dp", 1) for total in far_totals]
    for i, k in enumerate(partners):
        weights, share = call(
            share_kernel, (shaped((2 * block, rows), bf16), shaped((rows, width), bf16)), [made_sib[i]]
        )(far_scores[i], answers[i], c_own, c_sib, *far_totals[i : i + 1])
        made.append(weights)
        sent.append(share)
        shares.append(swap(after(share, sib_answers[i]), "dp", k))

    w_grad, w_own, terms = call(
        functools.partial(sums_kernel, len(partners)),
        (
            shaped((block, rows * devices), bf16),
            shaped((2 * block, rows), bf16),
            shaped((shards, rank, shard_width), bf16),
        ),
        sent,
    )(
        c_own, c_sib, q_own, q_sib, *far_q_near, *far_q_sib, hq, hq_sib, hc, hc_sib, stats,
        *answers, *sib_answers, *made, *made_sib, factors, scores, *sib_totals,
    )
    queries = [q_own, q_sib]
    for pair in zip(far_q_near, far_q_sib):
        queries += pair
    kinds = [shaped((rows, width), bf16), shaped((block, width), bf16)]
    question, grad = call(
        functools.partial(rows_kernel, len(partners)),
        kinds,
        scratch=[pltpu.VMEM(kind.shape, bf16) for kind in kinds] + [pltpu.SemaphoreType.DMA((4,))],
        away=True,
    )(w_own, w_grad, c_own, c_sib, *queries, *shares)

    terms = lax.all_to_all(terms, "fsdp", 0, 0)
    terms = jnp.sum(terms.astype(f32), 0)
    apart = 2
    while 2 * apart < devices:
        terms = terms + swap(terms, "dp", apart)
        apart *= 2
    terms = terms.astype(bf16)
    got = [swap(terms, "dp", k).astype(f32) for k in (apart, apart ^ 1, 1)]
    terms = terms.astype(f32)
    got[0] = after(got[0], question, grad)
    others = (got[1] + got[2]) * adapter_scale
    terms = (terms + got[0]) * adapter_scale
    return (
        question[None],
        grad[None, None],
        jnp.where(even, others, terms),
        jnp.where(even, terms, others),
    )


def solution(mesh):
    placed = (
        P("fsdp", "dp", None),
        P("fsdp", "dp", None, None),
        P("fsdp", "dp"),
        P("fsdp", "dp"),
        P("fsdp", "dp", None),
        P("fsdp", "dp", None, None),
        P(None, "fsdp"),
        P(None, "fsdp"),
    )
    return jax.shard_map(
        on_device,
        mesh=mesh,
        in_specs=placed,
        out_specs=(
            P("fsdp", "dp", None),
            P("fsdp", "dp", None, None),
            P(None, "fsdp"),
            P(None, "fsdp"),
        ),
        check_vma=False,
    )
```
